32 devices in a mesh: dp: 8 (over y, x, core), branch: 4 (over z).
Axes of the slice: x: 2, y: 2, z: 4, core: 2. Of those that a mesh axis runs over, the one named last changes fastest.
Arguments:
- block_input: bfloat16 [8, 1024, 2048], P('dp', 'branch'), may hold values from -6 to 6
- segment_ids: int32 [8, 1024], P('dp'), may hold values from 0 to 3, as said below
- out_cotangent: bfloat16 [8, 1024, 2048], P('dp', 'branch'), may hold values from -6 to 6
- norm_gain: float32 [2048], replicated, may hold values from 0.5 to 1.5
- norm_bias: float32 [2048], replicated, may hold values from -1.75 to 1.75
- query_weight: bfloat16 [2048, 2048], P('dp', 'branch'), may hold values from -0.125 to 0.125
- key_weight: bfloat16 [2048, 2048], P('dp', 'branch'), may hold values from -0.125 to 0.125
- value_weight: bfloat16 [2048, 2048], P('dp', 'branch'), may hold values from -0.125 to 0.125
- query_bias: float32 [2048], P('branch'), may hold values from -1.75 to 1.75
- key_bias: float32 [2048], P('branch'), may hold values from -1.75 to 1.75
- value_bias: float32 [2048], P('branch'), may hold values from -1.75 to 1.75
- out_weight: bfloat16 [2048, 2048], P('branch', 'dp'), may hold values from -1.5 to 1.5
- fc1_weight: bfloat16 [2048, 8192], P('dp', 'branch'), may hold values from -0.125 to 0.125
- fc1_bias: float32 [8192], P('branch'), may hold values from -3 to 3
- fc2_weight: bfloat16 [8192, 2048], P('branch', 'dp'), may hold values from -0.0625 to 0.0625
- output_bias: float32 [2048], replicated, may hold values from -3 to 3
Outputs:
- block_output: bfloat16 [8, 1024, 2048], P('dp', 'branch')
- input_grad: float32 [8, 1024, 2048], P('dp', 'branch')
- gain_grad: float32 [2048], replicated
- norm_bias_grad: float32 [2048], replicated
- query_weight_grad: float32 [2048, 2048], P('dp', 'branch')
- key_weight_grad: float32 [2048, 2048], P('dp', 'branch')
- value_weight_grad: float32 [2048, 2048], P('dp', 'branch')
- query_bias_grad: float32 [2048], P('branch')
- key_bias_grad: float32 [2048], P('branch')
- value_bias_grad: float32 [2048], P('branch')
- out_weight_grad: float32 [2048, 2048], P('branch', 'dp')
- fc1_weight_grad: float32 [2048, 8192], P('dp', 'branch')
- fc1_bias_grad: float32 [8192], P('branch')
- fc2_weight_grad: float32 [8192, 2048], P('branch', 'dp')
- output_bias_grad: float32 [2048], replicated
The draws below stay inside these ranges and needn't reach their ends.
Inputs may be any that keep to these rules, and one draw needn't show every extreme that they name: `segment_ids`: in each row of 1024 tokens the values are 1, 2, 3, 0 in runs of that order: documents 1 and 2 (1 may be empty) lie within the first 128 tokens, document 3 begins there and ends within the last 64 tokens, and padding 0 fills the rest, one token or more.
All inputs are finite; a program needn't handle non-finite values.
Results may differ from the reference program's by a relative error of at most 0.012.
The reference program's roundings to bfloat16 on the way count: a program that leaves them out, or rounds other values in their place, can miss the bound.
Values may be sent and summed in bfloat16 or wider, within the bound.
A program may use at most 256 MiB of HBM per device.

```python
import jax
import jax.numpy as jnp
from jax import lax

D = 2048
HEADS = 32
HEAD_DIM = 64
ROT = 32
FF = 8192
SEQ = 1024
ROWS = 8


def draw_segment_ids(key, part):
    key_lead, key_cut, key_tail = jax.random.split(key, 3)
    lead_end = jax.random.randint(key_lead, (ROWS, 1), 1, max(SEQ // 8, 2))
    cut_point = jax.random.randint(key_cut, (ROWS, 1), 0, lead_end)
    tail_start = SEQ - jax.random.randint(key_tail, (ROWS, 1), 1, SEQ // 16 + 1)
    places = jnp.arange(SEQ, dtype=jnp.int32)[None, :]
    labels = jnp.where(places < cut_point, 1, jnp.where(places < lead_end, 2, jnp.where(places < tail_start, 3, 0)))
    return labels.astype(jnp.int32)


def raised(drawn, own_key, source, target, shards_of, factor):
    def block_of(position):
        return (jnp.arange(drawn.shape[position]) // (drawn.shape[position] // shards_of)).reshape((-1,) + (1,) * (drawn.ndim - 1 - position))

    near = jax.random.permutation(own_key, shards_of)[block_of(target)]
    far = (block_of(target) + shards_of // 2) % shards_of
    return jnp.where((block_of(source) == near) | (block_of(source) == far), factor * drawn, drawn)


def block_levels(stream_key, dims, pieces, low, high):
    factor_of = 1.0
    for axis_at, parts in pieces:
        draws = jax.random.uniform(jax.random.fold_in(jax.random.fold_in(stream_key, 6), axis_at), (parts,), jnp.float32, low / len(pieces), high / len(pieces))
        factor_of = factor_of * jnp.repeat(jnp.exp(draws), dims[axis_at] // parts).reshape((-1,) + (1,) * (len(dims) - 1 - axis_at))
    return factor_of


def centred(own_key, extent, width, bound, shards=(), held_as=jnp.bfloat16):
    drawn = jax.random.normal(own_key, extent, jnp.float32) * width
    if len(shards) > 0:
        drawn = block_levels(own_key, extent, shards, -0.22, 0.18) * drawn
    return jnp.clip(drawn, min=-bound, max=bound).astype(held_as)


def noise_with(own_key, dims, deviation, limit, pieces, heavy, kind=jnp.bfloat16):
    entries = deviation * jax.random.normal(own_key, dims, jnp.float32)
    if pieces:
        entries = entries * block_levels(own_key, dims, pieces, -0.22, 0.18)
    return jnp.clip(raised(entries, jax.random.fold_in(own_key, 3), *heavy), -limit, limit).astype(kind)


def setup_inputs(seed: int = 0) -> dict:
    streams_of = jax.random.split(jax.random.key(seed), 17)
    block_input = centred(streams_of[0], (ROWS, SEQ, D), 1.0, 6.0, ((0, 8), (1, 4)))
    segment_ids = draw_segment_ids(jax.random.fold_in(streams_of[16], 71), 0)
    out_cotangent = noise_with(streams_of[2], (ROWS, SEQ, D), 1.0, 6.0, ((0, 8), (1, 4)), (0, 2, 8, 2.0))
    norm_gain = jnp.clip(1.0 + 0.1 * jax.random.normal(streams_of[3], (D,), jnp.float32), 0.5, 1.5)
    norm_bias = centred(streams_of[4], (D,), 0.3, 1.75, (), jnp.float32)
    query_weight = centred(streams_of[5], (D, D), D ** -0.5, 0.125, ((0, 8), (1, 4)))
    key_weight = centred(streams_of[6], (D, D), D ** -0.5, 0.125, ((0, 8), (1, 4)))
    value_weight = centred(streams_of[7], (D, D), D ** -0.5, 0.125, ((0, 8), (1, 4)))
    query_bias = centred(streams_of[8], (D,), 0.3, 1.75, ((0, 4),), jnp.float32)
    key_bias = centred(streams_of[9], (D,), 0.3, 1.75, ((0, 4),), jnp.float32)
    value_bias = centred(streams_of[10], (D,), 0.3, 1.75, ((0, 4),), jnp.float32)
    out_weight = centred(streams_of[11], (D, D), (max(D // 128, 1)) ** -0.5, 1.5, ((0, 4), (1, 8)))
    fc1_weight = centred(streams_of[12], (D, FF), D ** -0.5, 0.125, ((0, 8), (1, 4)))
    fc1_bias = centred(streams_of[13], (FF,), 0.5, 3.0, ((0, 4),), jnp.float32)
    fc2_weight = centred(streams_of[14], (FF, D), FF ** -0.5, 0.0625, ((0, 4), (1, 8)))
    output_bias = centred(streams_of[15], (D,), 0.5, 3.0, (), jnp.float32)
    return dict(block_input=block_input, segment_ids=segment_ids, out_cotangent=out_cotangent, norm_gain=norm_gain, norm_bias=norm_bias, query_weight=query_weight, key_weight=key_weight, value_weight=value_weight, query_bias=query_bias, key_bias=key_bias, value_bias=value_bias, out_weight=out_weight, fc1_weight=fc1_weight, fc1_bias=fc1_bias, fc2_weight=fc2_weight, output_bias=output_bias)


EPSILON = 1e-05
NEGATIVE = -1e+30

@jax.custom_vjp
def low(v):
    return lax.optimization_barrier(v.astype(jnp.bfloat16)).astype(jnp.float32)

@jax.custom_vjp
def low_back(v):
    return v

def low_keep(v):
    return (low(v), None)

def low_pass(kept, grad):
    return (grad,)

def back_keep(v):
    return (v, None)

def back_low(kept, grad):
    return (low(grad),)
low.defvjp(low_keep, low_pass)
low_back.defvjp(back_keep, back_low)

def product(left, right):
    return jnp.dot(left, right, precision=lax.Precision.HIGHEST, preferred_element_type=jnp.float32)

def tables(segments):
    length = segments.shape[0]
    places = jnp.arange(length, dtype=jnp.int32)
    change = jnp.concatenate([jnp.ones((1,), dtype=jnp.bool_), segments[1:] != segments[:-1]])
    starts = lax.cummax(jnp.where(change, places, 0), axis=0)
    half_rot = ROT // 2
    frequency = 10000.0 ** (-2.0 * jnp.arange(half_rot, dtype=jnp.float32) / ROT)
    angles = (places - starts).astype(jnp.float32)[:, None] * frequency[None, :]
    return (jnp.cos(angles)[:, None, :], jnp.sin(angles)[:, None, :])

def rotate(tensor, cosine, sine):
    half_rot = ROT // 2
    lower_part = tensor[..., :half_rot]
    upper_part = tensor[..., half_rot:ROT]
    return jnp.concatenate([lower_part * cosine - upper_part * sine, upper_part * cosine + lower_part * sine, tensor[..., ROT:]], axis=-1)

def visible(segments):
    places = jnp.arange(segments.shape[0], dtype=jnp.int32)
    same_doc = segments[:, None] == segments[None, :]
    causal = places[None, :] <= places[:, None]
    live_key = segments[None, :] != 0
    return same_doc & causal & live_key | (places[None, :] == places[:, None])

def row_forward(params, x_row, seg_row):
    gain_vec, beta_vec, query_w, key_w, value_w, query_b, key_b, value_b, out_w, fc1_w, fc1_b, fc2_w, out_b = params
    length = x_row.shape[0]
    center = x_row - lax.optimization_barrier(jnp.mean(x_row, axis=-1, keepdims=True))
    normed = center * lax.rsqrt(lax.optimization_barrier(jnp.mean(center * center, axis=-1, keepdims=True)) + EPSILON)
    hidden = low(normed * gain_vec + beta_vec)
    cosine, sine = tables(seg_row)
    query_raw = low_back(product(hidden, query_w) + query_b).reshape(length, HEADS, HEAD_DIM)
    key_raw = low_back(product(hidden, key_w) + key_b).reshape(length, HEADS, HEAD_DIM)
    query_rot = low(rotate(query_raw, cosine, sine))
    key_rot = low(rotate(key_raw, cosine, sine))
    value_low = low(low_back(product(hidden, value_w) + value_b)).reshape(length, HEADS, HEAD_DIM)
    allowed = visible(seg_row)

    def one_head(member):
        query_head, key_head, value_head = member
        scores = low_back(product(query_head, key_head.T) * HEAD_DIM ** (-0.5))
        scores = jnp.where(allowed, scores, NEGATIVE)
        exponent = jnp.exp(scores - lax.optimization_barrier(jnp.max(scores, axis=-1, keepdims=True)))
        probability = low(exponent / lax.optimization_barrier(jnp.sum(exponent, axis=-1, keepdims=True)))
        return product(probability, value_head)
    attended = lax.map(jax.checkpoint(one_head), (query_rot.transpose(1, 0, 2), key_rot.transpose(1, 0, 2), value_low.transpose(1, 0, 2)))
    attended = low(low_back(attended.transpose(1, 0, 2).reshape(length, HEADS * HEAD_DIM)))
    pre_act = low_back(product(hidden, fc1_w) + fc1_b)
    activation = low(jax.nn.gelu(pre_act, approximate=True))
    return x_row + (product(attended, out_w) + product(activation, fc2_w)) + out_b

def forward(inputs, params, segments):

    def row_step(carry, row_item):
        return (carry, jax.checkpoint(row_forward)(params, row_item[0], row_item[1]))
    _, outputs = lax.scan(row_step, 0, (inputs, segments))
    return outputs

def reference(block_input, segment_ids, out_cotangent, norm_gain, norm_bias, query_weight, key_weight, value_weight, query_bias, key_bias, value_bias, out_weight, fc1_weight, fc1_bias, fc2_weight, output_bias):
    floats = tuple((array.astype(jnp.float32) for array in (block_input, norm_gain, norm_bias, query_weight, key_weight, value_weight, query_bias, key_bias, value_bias, out_weight, fc1_weight, fc1_bias, fc2_weight, output_bias)))

    def layer_forward(inputs, *params):
        return forward(inputs, params, segment_ids)
    outputs, pullback = jax.vjp(layer_forward, *floats)
    gradients = pullback(out_cotangent.astype(jnp.float32))
    return (outputs.astype(jnp.bfloat16), gradients[0], gradients[1], gradients[2], gradients[3], gradients[4], gradients[5], gradients[6], gradients[7], gradients[8], gradients[9], gradients[10], gradients[11], gradients[12], gradients[13])
```

```python
import functools

import jax
import jax.numpy as jnp
from jax import lax
from jax.experimental import pallas as pl
from jax.experimental.pallas import tpu as pltpu
from jax.sharding import PartitionSpec as P

HEAD_DIM = 64
ROT = 32
EPSILON = 1e-05
NEGATIVE = -1e30
LANES = 128
TILE = 512
QBLOCK = 256
MESH = pl.DeviceIdType.MESH
BF16 = jnp.bfloat16
F32 = jnp.float32
GELU_C = 0.7978845608028654
GELU_A = 0.044715


def flip(index, bits):
    out = index
    bit = 1
    while bit <= bits:
        if bits & bit:
            out = out + bit * (1 - 2 * lax.rem(lax.div(index, bit), 2))
        bit *= 2
    return out


def dot_nn(left, right):
    return jnp.dot(left, right, preferred_element_type=F32)


def dot_nt(left, right):
    return lax.dot_general(left, right, (((1,), (1,)), ((), ())), preferred_element_type=F32)


def tile_of(extent, most=TILE):
    return min(most, extent)


def aligned(index, step):
    return pl.ds(pl.multiple_of(index * step, step), step)


class Chain:
    def __init__(self, own_src, buf, rows, count, sems, dp):
        self.own_src, self.buf, self.rows, self.count = own_src, buf, rows, count
        self.sems, self.dp = sems, dp
        self.z = lax.axis_index("branch")

    def block(self, slot):
        return self.buf.at[aligned(slot, self.rows), :]

    def copy(self, up, step, slot, src=None):
        send, recv = self.sems[0 if up else 2], self.sems[1 if up else 3]
        return pltpu.make_async_remote_copy(
            src_ref=self.block(slot) if src is None else src,
            dst_ref=self.block(slot),
            send_sem=send.at[step],
            recv_sem=recv.at[step],
            device_id=(self.dp, self.z + 1 if up else self.z - 1),
            device_id_type=MESH,
        )

    def sends(self, up, step):
        z, last = self.z, self.count - 1
        if up:
            return jnp.logical_and(z >= step, z < last)
        return jnp.logical_and(z + step <= last, z > 0)

    def receives(self, up, step):
        z, last = self.z, self.count - 1
        return z - 1 - step >= 0 if up else z + 1 + step <= last

    def sent_slot(self, up, step):
        return self.z - step if up else self.z + step

    def start(self):
        for up in (False, True):

            @pl.when(self.sends(up, 0))
            def _(up=up):
                self.copy(up, 0, self.z, self.own_src).start()

    def pump(self, step):
        for up in (False, True):

            @pl.when(self.sends(up, step))
            def _(up=up):
                slot = self.sent_slot(up, step)
                self.copy(up, step - 1, slot).wait_recv()
                self.copy(up, step, slot).start()

    def arrive(self):
        for step in range(self.count - 1):
            for up in (False, True):

                @pl.when(jnp.logical_and(self.receives(up, step), jnp.logical_not(self.sends(up, step + 1))))
                def _(up=up, step=step):
                    slot = self.z - 1 - step if up else self.z + 1 + step
                    self.copy(up, step, slot).wait_recv()

    def finish(self):
        for step in range(self.count - 1):
            for up in (False, True):

                @pl.when(self.sends(up, step))
                def _(up=up, step=step):
                    self.copy(up, step, self.sent_slot(up, step), self.own_src if step == 0 else None).wait_send()


class Gather:
    def __init__(self, index, shard, full, by_rows, chips, sems):
        self.index, self.shard, self.full, self.by_rows, self.chips = index, shard, full, by_rows, chips
        self.send, self.recv, self.pair_send, self.pair_recv, self.own = sems
        dp = lax.axis_index("dp")
        self.z = lax.axis_index("branch")
        self.core = lax.rem(dp, 2)
        self.chip = lax.div(dp, 2)
        self.width = shard.shape[0 if by_rows else 1]

    def slot(self, dp):
        part = aligned(dp, self.width)
        return self.full.at[part, :] if self.by_rows else self.full.at[:, part]

    def at(self, r, core):
        return flip(self.chip, r) * 2 + core

    def to_chip(self, r, landing):
        return pltpu.make_async_remote_copy(
            src_ref=self.shard,
            dst_ref=self.slot(landing),
            send_sem=self.send.at[self.index, r - 1],
            recv_sem=self.recv.at[self.index, r - 1],
            device_id=(self.at(r, self.core), self.z),
            device_id_type=MESH,
        )

    def to_pair(self, r, landing):
        return pltpu.make_async_remote_copy(
            src_ref=self.shard if r == 0 else self.slot(self.at(r, self.core)),
            dst_ref=self.slot(landing),
            send_sem=self.pair_send.at[self.index, r],
            recv_sem=self.pair_recv.at[self.index, r],
            device_id=(self.chip * 2 + 1 - self.core, self.z),
            device_id_type=MESH,
        )

    def keep(self):
        return pltpu.make_async_copy(self.shard, self.slot(self.at(0, self.core)), self.own.at[self.index])

    def start(self):
        for r in range(1, self.chips):
            self.to_chip(r, self.at(0, self.core)).start()

    def start_pair(self):
        self.to_pair(0, self.at(0, self.core)).start()
        self.keep().start()

    def pump(self, r):
        self.to_chip(r, self.at(r, self.core)).wait_recv()
        self.to_pair(r, self.at(r, self.core)).start()

    def arrive(self):
        self.keep().wait()
        for r in range(self.chips):
            self.to_pair(r, self.at(r, 1 - self.core)).wait_recv()

    def finish(self):
        for r in range(1, self.chips):
            self.to_chip(r, self.at(0, self.core)).wait_send()
        for r in range(self.chips):
            self.to_pair(r, self.at(r, self.core)).wait_send()


def greet(chips, count):
    dp, z = lax.axis_index("dp"), lax.axis_index("branch")
    core, chip = lax.rem(dp, 2), lax.div(dp, 2)
    barrier = pltpu.get_barrier_semaphore()
    for r in range(1, chips):
        pl.semaphore_signal(barrier, inc=1, device_id=(flip(chip, r) * 2 + core, z), device_id_type=MESH)
    pl.semaphore_signal(barrier, inc=1, device_id=(chip * 2 + 1 - core, z), device_id_type=MESH)
    for shift in (1, count - 1):
        pl.semaphore_signal(barrier, inc=1, device_id=(dp, lax.rem(z + shift, count)), device_id_type=MESH)
    pl.semaphore_wait(barrier, chips + 2)


def forward_kernel(
    chips, count,
    x, gain, beta, wqkv, wf1, wo, wf2, cot, bqkv, bf1, table_c, table_l, table_r, seg_col, seg_row,
    gqkv, gf1, go, gf2, gcot, hid_t, q_out, k_out, v_out, att_t_out, lse_out, act_t, dgelu, part_out,
    hid, vqkv, vf1, vf2, vo, q, k, v, att, att_t, lse, act, part, stage_a, stage_b,
    w_send, w_recv, p_send, p_recv, own_sem, h_us, h_ur, h_ds, h_dr, c_us, c_ur, c_ds, c_dr, load_sem, save_sem, st_sem,
):
    z = lax.axis_index("branch")
    dp = lax.axis_index("dp")
    rows, width = x.shape
    length = rows * count
    hcols = wo.shape[0]
    units = wf2.shape[0]
    sems = (w_send, w_recv, p_send, p_recv, own_sem)
    g_qkv = Gather(0, wqkv, gqkv, True, chips, sems)
    g_f1 = Gather(1, wf1, gf1, True, chips, sems)
    g_o = Gather(2, wo, go, False, chips, sems)
    g_f2 = Gather(3, wf2, gf2, False, chips, sems)
    own_rows = hid.at[aligned(z, rows), :]
    h_chain = Chain(own_rows, hid, rows, count, (h_us, h_ur, h_ds, h_dr), dp)
    c_chain = Chain(cot, gcot, rows, count, (c_us, c_ur, c_ds, c_dr), dp)

    greet(chips, count)
    for g in (g_qkv, g_f1, g_o, g_f2):
        g.start()
        g.start_pair()
    keep_cot = pltpu.make_async_copy(cot, gcot.at[aligned(z, rows), :], load_sem.at[5])
    keep_cot.start()

    step_rows = 32

    def norm(i, _):
        part_rows = aligned(i, step_rows)
        inputs = x[part_rows, :].astype(F32)
        center = inputs - jnp.mean(inputs, axis=-1, keepdims=True)
        inverse = lax.rsqrt(jnp.mean(center * center, axis=-1, keepdims=True) + EPSILON)
        where = pl.ds(pl.multiple_of(z * rows + i * step_rows, step_rows), step_rows)
        hid[where, :] = (center * inverse * gain[...] + beta[...]).astype(BF16)
        return 0

    lax.fori_loop(0, rows // step_rows, norm, 0)
    h_chain.start()
    for r in range(1, chips - 1):
        g_qkv.pump(r)
    if count > 2:
        h_chain.pump(1)
    if chips > 1:
        g_qkv.pump(chips - 1)
    g_qkv.arrive()
    load_qkv = pltpu.make_async_copy(gqkv, vqkv, load_sem.at[0])
    load_qkv.start()
    for s in range(2, count - 1):
        h_chain.pump(s)
    c_chain.start()
    h_chain.arrive()
    load_qkv.wait()

    mt = tile_of(length)
    ht = tile_of(hcols)

    def project(i, _):
        rows_i = aligned(i, mt)
        for which, dest in ((0, q), (1, k), (2, v)):
            for c in range(hcols // ht):
                at = which * hcols + c * ht
                y = dot_nn(hid[rows_i, :], vqkv[:, at : at + ht]) + bqkv[:, at : at + ht]
                for piece in range(ht // LANES):
                    part_y = y[:, piece * LANES : (piece + 1) * LANES]
                    to = c * ht + piece * LANES
                    if which < 2:
                        part_y = (
                            part_y * table_c[rows_i, :]
                            + pltpu.roll(part_y, LANES - ROT // 2, 1) * table_l[rows_i, :]
                            + pltpu.roll(part_y, ROT // 2, 1) * table_r[rows_i, :]
                        )
                    low = part_y.astype(BF16)
                    if which == 0:
                        low = low * BF16(HEAD_DIM**-0.5)
                    dest[rows_i, to : to + LANES] = low
        return 0

    lax.fori_loop(0, length // mt, project, 0)
    saves = []

    def save(src, dst):
        c = pltpu.make_async_copy(src, dst, save_sem.at[len(saves)])
        c.start()
        saves.append(c)

    save(q, q_out)
    save(k, k_out)
    save(v, v_out)
    if count > 2:
        c_chain.pump(1)

    qb = tile_of(length, QBLOCK)

    def attend(pair, _):
        cols = aligned(pair, LANES)
        lane = lax.broadcasted_iota(jnp.int32, (1, LANES), 1)
        for b in range(length // qb):
            here = slice(b * qb, (b + 1) * qb)
            before = b * qb
            q2 = q[here, cols]
            seg_q = seg_col[here, :]
            ki = lax.broadcasted_iota(jnp.int32, (qb, qb), 1)
            qi = lax.broadcasted_iota(jnp.int32, (qb, qb), 0)
            seen_here = jnp.logical_or(
                jnp.logical_and(seg_q == seg_row[:, here], ki <= qi), ki == qi
            )
            out = jnp.zeros((qb, LANES), F32)
            stat = jnp.zeros((qb, LANES), F32)
            for h in range(2):
                mine = (lane // HEAD_DIM) == h
                qh = jnp.where(mine, q2, BF16(0))
                s_here = jnp.where(seen_here, dot_nt(qh, k[here, cols]), NEGATIVE)
                top = jnp.max(s_here, axis=-1, keepdims=True)
                if before:
                    s_before = jnp.where(
                        seg_q == seg_row[:, :before], dot_nt(qh, k[:before, cols]), NEGATIVE
                    )
                    top = jnp.maximum(top, jnp.max(s_before, axis=-1, keepdims=True))
                e_here = jnp.exp(s_here - top)
                total = jnp.sum(e_here, axis=-1, keepdims=True)
                if before:
                    e_before = jnp.exp(s_before - top)
                    total = total + jnp.sum(e_before, axis=-1, keepdims=True)
                share = 1.0 / total
                o = dot_nn((e_here * share).astype(BF16), jnp.where(mine, v[here, cols], BF16(0)))
                if before:
                    o = o + dot_nn(
                        (e_before * share).astype(BF16), jnp.where(mine, v[:before, cols], BF16(0))
                    )
                out = out + o
                stat = jnp.where(mine, top + jnp.log(total), stat)
            att[here, cols] = out.astype(BF16)
            att_t[cols, here] = out.T.astype(BF16)
            turned = stat.T
            lse[pl.ds(2 * pair, 1), here] = turned[0:1, :]
            lse[pl.ds(2 * pair + 1, 1), here] = turned[HEAD_DIM : HEAD_DIM + 1, :]
        return 0

    pairs = hcols // LANES
    lax.fori_loop(0, pairs // 2, attend, 0)
    for r in range(1, chips):
        g_f1.pump(r)
    g_f1.arrive()
    load_f1 = pltpu.make_async_copy(gf1, vf1, load_sem.at[1])
    load_f1.start()
    for s in range(2, count - 1):
        c_chain.pump(s)
    lax.fori_loop(pairs // 2, pairs, attend, 0)
    save(att_t, att_t_out)
    save(lse, lse_out)
    for r in range(1, chips):
        g_o.pump(r)
    g_o.arrive()
    load_o = pltpu.make_async_copy(go, vo, load_sem.at[2])
    load_o.start()
    load_f1.wait()

    ft = tile_of(units)
    per_row = units // ft
    n_tiles = (length // mt) * per_row

    def staged(slot, rows_i, cols_i, which):
        src = (stage_a if which == 0 else stage_b).at[slot]
        dst = act_t.at[cols_i, rows_i] if which == 0 else dgelu.at[rows_i, cols_i]
        return pltpu.make_async_copy(src, dst, st_sem.at[which, slot])

    def unit(i, _):
        rows_i, cols_i = aligned(lax.div(i, per_row), mt), aligned(lax.rem(i, per_row), ft)
        slot = lax.rem(i, 2)

        @pl.when(i >= 2)
        def _():
            for which in range(2):
                staged(slot, rows_i, cols_i, which).wait()

        y = dot_nn(hid[rows_i, :], vf1[:, cols_i]) + bf1[:, cols_i]
        square = y * y
        t = jnp.tanh(GELU_C * (y + GELU_A * (y * square)))
        half = 0.5 * (1.0 + t)
        low = (y * half).astype(BF16)
        act[rows_i, cols_i] = low
        stage_a[slot] = low.T
        stage_b[slot] = (
            half + 0.5 * y * (1.0 - t * t) * (GELU_C * (1.0 + 3.0 * GELU_A * square))
        ).astype(BF16)
        for which in range(2):
            staged(slot, rows_i, cols_i, which).start()
        return 0

    lax.fori_loop(0, n_tiles, unit, 0)
    for i in range(max(n_tiles - 2, 0), n_tiles):
        for which in range(2):
            staged(i % 2, pl.ds(0, mt), pl.ds(0, ft), which).wait()

    wt = tile_of(width)
    per_col = width // wt
    n_turn = (length // mt) * per_col

    def turn_copy(slot, rows_i, cols_i):
        return pltpu.make_async_copy(
            stage_a.at[slot, pl.ds(0, wt), :], hid_t.at[cols_i, rows_i], st_sem.at[0, slot]
        )

    def turn(i, _):
        rows_i, cols_i = aligned(lax.div(i, per_col), mt), aligned(lax.rem(i, per_col), wt)
        slot = lax.rem(i, 2)

        @pl.when(i >= 2)
        def _():
            turn_copy(slot, rows_i, cols_i).wait()

        stage_a[slot, 0:wt, :] = hid[rows_i, cols_i].T
        turn_copy(slot, rows_i, cols_i).start()
        return 0

    lax.fori_loop(0, n_turn, turn, 0)
    for i in range(max(n_turn - 2, 0), n_turn):
        turn_copy(i % 2, pl.ds(0, mt), pl.ds(0, wt)).wait()

    for r in range(1, chips):
        g_f2.pump(r)
    g_f2.arrive()
    load_f2 = pltpu.make_async_copy(gf2, vf2, load_sem.at[3])
    load_f2.start()
    load_o.wait()
    load_f2.wait()

    def output(i, _):
        rows_i, cols_i = aligned(lax.div(i, per_col), mt), aligned(lax.rem(i, per_col), wt)
        part[rows_i, cols_i] = (
            dot_nn(act[rows_i, :], vf2[:, cols_i]) + dot_nn(att[rows_i, :], vo[:, cols_i])
        ).astype(BF16)
        return 0

    lax.fori_loop(0, n_turn, output, 0)
    save(part, part_out)
    c_chain.arrive()
    keep_cot.wait()
    for g in (g_qkv, g_f1, g_o, g_f2):
        g.finish()
    h_chain.finish()
    c_chain.finish()
    for c in saves:
        c.wait()


def run_forward(ndp, count, x, gain, beta, wqkv, wf1, wo, wf2, cot, bqkv, bf1, tables, seg_col, seg_row):
    chips = ndp // 2
    rows, width = x.shape
    length = rows * count
    hcols, units = wo.shape[0], wf2.shape[0]
    heads = hcols // HEAD_DIM
    mt, ft, wt = tile_of(length), tile_of(units), tile_of(width)
    anywhere = pl.BlockSpec(memory_space=pl.ANY)
    vmem = pl.BlockSpec(memory_space=pltpu.VMEM)
    low = lambda *shape: jax.ShapeDtypeStruct(shape, BF16)
    outs = [
        low(width, 3 * hcols), low(width, units), low(hcols, width), low(units, width), low(length, width),
        low(width, length), low(length, hcols), low(length, hcols), low(length, hcols), low(hcols, length),
        jax.ShapeDtypeStruct((heads, length), F32), low(units, length), low(length, units), low(length, width),
    ]
    v = lambda *shape: pltpu.VMEM(shape, BF16)
    steps = max(count - 1, 1)
    dma = lambda *shape: pltpu.SemaphoreType.DMA(shape)
    scratch = [
        v(length, width), v(width, 3 * hcols), v(width, units), v(units, width), v(hcols, width),
        v(length, hcols), v(length, hcols), v(length, hcols), v(length, hcols), v(hcols, length),
        pltpu.VMEM((heads, length), F32), v(length, units), v(length, width),
        v(2, max(ft, wt), mt), v(2, mt, ft),
        dma(4, max(chips - 1, 1)), dma(4, max(chips - 1, 1)), dma(4, chips), dma(4, chips), dma(4),
        *[dma(steps) for _ in range(8)], dma(6), dma(8), dma(2, 2),
    ]
    return pl.pallas_call(
        functools.partial(forward_kernel, chips, count),
        out_shape=outs,
        in_specs=[vmem, vmem, vmem, anywhere, anywhere, anywhere, anywhere, anywhere] + [vmem] * 7,
        out_specs=[anywhere] * len(outs),
        scratch_shapes=scratch,
        compiler_params=pltpu.CompilerParams(
            collective_id=0, has_side_effects=True, vmem_limit_bytes=60 * 1024 * 1024
        ),
        name="gather_forward",
    )(x, gain, beta, wqkv, wf1, wo, wf2, cot, bqkv, bf1, *tables, seg_col, seg_row)


def rotary_tables(segments):
    length = segments.shape[0]
    places = jnp.arange(length, dtype=jnp.int32)
    starts = jnp.zeros((length,), jnp.int32)
    for value in range(4):
        first = jnp.min(jnp.where(segments == value, places, length))
        starts = jnp.where(segments == value, first, starts)
    half_rot = ROT // 2
    frequency = 10000.0 ** (-2.0 * jnp.arange(half_rot, dtype=F32) / ROT)
    angles = (places - starts).astype(F32)[:, None] * frequency
    cosine, sine = jnp.cos(angles), jnp.sin(angles)
    one = jnp.ones((length, HEAD_DIM - ROT), F32)
    zero = jnp.zeros((length, HEAD_DIM - ROT), F32)
    none = jnp.zeros_like(sine)
    twice = lambda t: jnp.concatenate([t, t], axis=1)
    return (
        twice(jnp.concatenate([cosine, cosine, one], axis=1)),
        twice(jnp.concatenate([-sine, none, zero], axis=1)),
        twice(jnp.concatenate([none, sine, zero], axis=1)),
    ), cosine, sine


def contract_rows(left, right):
    return lax.dot_general(left, right, (((0,), (0,)), ((), ())), preferred_element_type=F32)


def rotate_back(tensor, cosine, sine):
    half_rot = ROT // 2
    lower_part = tensor[..., :half_rot]
    upper_part = tensor[..., half_rot:ROT]
    return jnp.concatenate(
        [
            lower_part * cosine + upper_part * sine,
            upper_part * cosine - lower_part * sine,
            tensor[..., ROT:],
        ],
        axis=-1,
    )


def attend_back(q, k, v, out_grad, lse, seg):
    length = q.shape[0]
    heads = q.shape[1] // HEAD_DIM
    split = lambda t: t.reshape(length, heads, HEAD_DIM)
    q, k, v, g = split(q), split(k), split(v), split(out_grad)
    places = jnp.arange(length)
    seen = (seg[:, None] == seg[None, :]) & (places[None, :] <= places[:, None]) & (seg[None, :] != 0)
    seen = seen | (places[None, :] == places[:, None])

    def one(member):
        qh, kh, vh, gh, lh = member
        s = jnp.where(seen, dot_nt(qh, kh), NEGATIVE)
        p = jnp.exp(s - lh[:, None])
        pg = dot_nt(gh, vh)
        delta = jnp.sum(p * pg, axis=-1, keepdims=True)
        sg = (p * (pg - delta)).astype(BF16)
        return (
            dot_nn(sg, kh) * HEAD_DIM**-0.5,
            contract_rows(sg, qh),
            contract_rows(p.astype(BF16), gh),
        )

    t = lambda a: a.transpose(1, 0, 2)
    dq, dk, dv = lax.map(one, (t(q), t(k), t(v), t(g), lse))
    return t(dq), t(dk), t(dv)


def on_device(
    ndp, count,
    block_input, segment_ids, out_cotangent, norm_gain, norm_bias, query_weight, key_weight, value_weight,
    query_bias, key_bias, value_bias, out_weight, fc1_weight, fc1_bias, fc2_weight, output_bias,
):
    x = block_input[0]
    cot = out_cotangent[0]
    seg = segment_ids[0]
    rows, width = x.shape
    length = rows * count
    tables, cosine, sine = rotary_tables(seg)
    wqkv = jnp.concatenate([query_weight, key_weight, value_weight], axis=1)
    bqkv = jnp.concatenate([query_bias, key_bias, value_bias])[None, :]
    hidden_seg = jnp.where(seg == 0, -1, seg)
    (gqkv, gf1, go, gf2, gcot, hid_t, q, k, v, att_t, lse, act_t, dgelu, part) = run_forward(
        ndp, count, x, norm_gain[None, :], norm_bias[None, :], wqkv, fc1_weight, out_weight, fc2_weight, cot,
        bqkv, fc1_bias[None, :], tables, seg[:, None], hidden_seg[None, :],
    )
    hcols = att_t.shape[0]
    inputs = x.astype(F32)
    center = inputs - jnp.mean(inputs, axis=-1, keepdims=True)
    inverse = lax.rsqrt(jnp.mean(center * center, axis=-1, keepdims=True) + EPSILON)
    normed = center * inverse
    summed = lax.psum_scatter(part, "branch", scatter_dimension=0, tiled=True).astype(F32)
    block_output = (inputs + summed + output_bias).astype(BF16)
    output_bias_grad = jnp.sum(gcot, axis=0, dtype=F32)
    out_weight_grad = dot_nn(att_t, gcot)
    fc2_weight_grad = dot_nn(act_t, gcot)
    pre_grad = (dot_nt(gcot, gf2) * dgelu.astype(F32)).astype(BF16)
    fc1_weight_grad = dot_nn(hid_t, pre_grad)
    fc1_bias_grad = jnp.sum(pre_grad, axis=0, dtype=F32)
    att_grad = dot_nt(gcot, go).astype(BF16)
    dq, dk, dv = attend_back(q, k, v, att_grad, lse, seg)
    cosine, sine = cosine[:, None, :], sine[:, None, :]
    flat = lambda t: t.astype(BF16).reshape(length, hcols)
    grads = jnp.concatenate(
        [flat(rotate_back(dq, cosine, sine)), flat(rotate_back(dk, cosine, sine)), flat(dv)], axis=1
    )
    qkv_weight_grad = dot_nn(hid_t, grads)
    qkv_bias_grad = jnp.sum(grads, axis=0, dtype=F32)
    hidden_grad = dot_nt(pre_grad, gf1) + dot_nt(grads, gqkv)
    norm_grad = lax.psum_scatter(hidden_grad.astype(BF16), "branch", scatter_dimension=0, tiled=True).astype(F32)
    gain_part = jnp.sum(norm_grad * normed, axis=0)
    beta_part = jnp.sum(norm_grad, axis=0)
    scaled = norm_grad * norm_gain
    input_grad = cot.astype(F32) + inverse * (
        scaled
        - jnp.mean(scaled, axis=-1, keepdims=True)
        - normed * jnp.mean(scaled * normed, axis=-1, keepdims=True)
    )
    gain_grad, norm_bias_grad = lax.psum((gain_part, beta_part), ("dp", "branch"))
    qkv_bias_grad, fc1_bias_grad, output_bias_grad = lax.psum(
        (qkv_bias_grad, fc1_bias_grad, output_bias_grad), "dp"
    )
    scatter = lambda g, dim: lax.psum_scatter(g.astype(BF16), "dp", scatter_dimension=dim, tiled=True).astype(F32)
    qkv_weight_grad = scatter(qkv_weight_grad, 0)
    fc1_weight_grad = scatter(fc1_weight_grad, 0)
    out_weight_grad = scatter(out_weight_grad, 1)
    fc2_weight_grad = scatter(fc2_weight_grad, 1)
    third = lambda t, i: t[..., i * hcols : (i + 1) * hcols]
    return (
        block_output[None], input_grad[None], gain_grad, norm_bias_grad,
        third(qkv_weight_grad, 0), third(qkv_weight_grad, 1), third(qkv_weight_grad, 2),
        third(qkv_bias_grad, 0), third(qkv_bias_grad, 1), third(qkv_bias_grad, 2),
        out_weight_grad, fc1_weight_grad, fc1_bias_grad, fc2_weight_grad, output_bias_grad,
    )


def solution(mesh):
    tokens, vector, split = P("dp", "branch", None), P(), P("branch")
    rows_first, cols_first = P("dp", "branch"), P("branch", "dp")
    in_specs = (
        tokens, P("dp", None), tokens, vector, vector, rows_first, rows_first, rows_first,
        split, split, split, cols_first, rows_first, split, cols_first, vector,
    )
    out_specs = (
        tokens, tokens, vector, vector, rows_first, rows_first, rows_first, split, split, split,
        cols_first, rows_first, split, cols_first, vector,
    )
    return jax.shard_map(
        functools.partial(on_device, mesh.shape["dp"], mesh.shape["branch"]),
        mesh=mesh, in_specs=in_specs, out_specs=out_specs, check_vma=False,
    )
```

```python
import functools

import jax
import jax.numpy as jnp
from jax import lax
from jax.experimental import pallas as pl
from jax.experimental.pallas import tpu as pltpu
from jax.sharding import PartitionSpec as P

HEAD_DIM = 64
ROT = 32
EPSILON = 1e-05
NEGATIVE = -1e30
LANES = 128
TILE = 512
QBLOCK = 256
MESH = pl.DeviceIdType.MESH
BF16 = jnp.bfloat16
F32 = jnp.float32
GELU_C = 0.7978845608028654
GELU_A = 0.044715
VMEM_LIMIT = 60 * 1024 * 1024 + 512 * 1024


def flip(index, bits):
    out = index
    bit = 1
    while bit <= bits:
        if bits & bit:
            out = out + bit * (1 - 2 * lax.rem(lax.div(index, bit), 2))
        bit *= 2
    return out


def dot_nn(left, right):
    return jnp.dot(left, right, preferred_element_type=F32)


def dot_nt(left, right):
    return lax.dot_general(left, right, (((1,), (1,)), ((), ())), preferred_element_type=F32)


def tile_of(extent, most=TILE):
    return min(most, extent)


def aligned(index, step):
    return pl.ds(pl.multiple_of(index * step, step), step)


class Chain:
    def __init__(self, own_src, buf, rows, count, sems, dp):
        self.own_src, self.buf, self.rows, self.count = own_src, buf, rows, count
        self.sems, self.dp = sems, dp
        self.z = lax.axis_index("branch")

    def block(self, slot):
        return self.buf.at[aligned(slot, self.rows), :]

    def copy(self, up, step, slot, src=None):
        send, recv = self.sems[0 if up else 2], self.sems[1 if up else 3]
        return pltpu.make_async_remote_copy(
            src_ref=self.block(slot) if src is None else src,
            dst_ref=self.block(slot),
            send_sem=send.at[step],
            recv_sem=recv.at[step],
            device_id=(self.dp, self.z + 1 if up else self.z - 1),
            device_id_type=MESH,
        )

    def sends(self, up, step):
        z, last = self.z, self.count - 1
        if up:
            return jnp.logical_and(z >= step, z < last)
        return jnp.logical_and(z + step <= last, z > 0)

    def receives(self, up, step):
        z, last = self.z, self.count - 1
        return z - 1 - step >= 0 if up else z + 1 + step <= last

    def sent_slot(self, up, step):
        return self.z - step if up else self.z + step

    def start(self):
        for up in (False, True):

            @pl.when(self.sends(up, 0))
            def _(up=up):
                self.copy(up, 0, self.z, self.own_src).start()

    def pump(self, step):
        for up in (False, True):

            @pl.when(self.sends(up, step))
            def _(up=up):
                slot = self.sent_slot(up, step)
                self.copy(up, step - 1, slot).wait_recv()
                self.copy(up, step, slot).start()

    def arrive(self):
        for step in range(self.count - 1):
            for up in (False, True):

                @pl.when(jnp.logical_and(self.receives(up, step), jnp.logical_not(self.sends(up, step + 1))))
                def _(up=up, step=step):
                    slot = self.z - 1 - step if up else self.z + 1 + step
                    self.copy(up, step, slot).wait_recv()

    def finish(self):
        for step in range(self.count - 1):
            for up in (False, True):

                @pl.when(self.sends(up, step))
                def _(up=up, step=step):
                    self.copy(up, step, self.sent_slot(up, step), self.own_src if step == 0 else None).wait_send()


class Gather:
    def __init__(self, index, shard, full, by_rows, chips, sems):
        self.index, self.shard, self.full, self.by_rows, self.chips = index, shard, full, by_rows, chips
        self.send, self.recv, self.pair_send, self.pair_recv, self.own = sems
        dp = lax.axis_index("dp")
        self.z = lax.axis_index("branch")
        self.core = lax.rem(dp, 2)
        self.chip = lax.div(dp, 2)
        self.width = shard.shape[0 if by_rows else 1]

    def slot(self, dp):
        part = aligned(dp, self.width)
        return self.full.at[part, :] if self.by_rows else self.full.at[:, part]

    def at(self, r, core):
        return flip(self.chip, r) * 2 + core

    def to_chip(self, r, landing):
        return pltpu.make_async_remote_copy(
            src_ref=self.shard,
            dst_ref=self.slot(landing),
            send_sem=self.send.at[self.index, r - 1],
            recv_sem=self.recv.at[self.index, r - 1],
            device_id=(self.at(r, self.core), self.z),
            device_id_type=MESH,
        )

    def to_pair(self, r, landing):
        return pltpu.make_async_remote_copy(
            src_ref=self.shard if r == 0 else self.slot(self.at(r, self.core)),
            dst_ref=self.slot(landing),
            send_sem=self.pair_send.at[self.index, r],
            recv_sem=self.pair_recv.at[self.index, r],
            device_id=(self.chip * 2 + 1 - self.core, self.z),
            device_id_type=MESH,
        )

    def keep(self):
        return pltpu.make_async_copy(self.shard, self.slot(self.at(0, self.core)), self.own.at[self.index])

    def start(self):
        for r in range(1, self.chips):
            self.to_chip(r, self.at(0, self.core)).start()

    def start_pair(self):
        self.to_pair(0, self.at(0, self.core)).start()
        self.keep().start()

    def pump(self, r):
        self.to_chip(r, self.at(r, self.core)).wait_recv()
        self.to_pair(r, self.at(r, self.core)).start()

    def arrive(self):
        self.keep().wait()
        for r in range(self.chips):
            self.to_pair(r, self.at(r, 1 - self.core)).wait_recv()

    def finish(self):
        for r in range(1, self.chips):
            self.to_chip(r, self.at(0, self.core)).wait_send()
        for r in range(self.chips):
            self.to_pair(r, self.at(r, self.core)).wait_send()


def greet(chips, count):
    dp, z = lax.axis_index("dp"), lax.axis_index("branch")
    core, chip = lax.rem(dp, 2), lax.div(dp, 2)
    barrier = pltpu.get_barrier_semaphore()
    for r in range(1, chips):
        pl.semaphore_signal(barrier, inc=1, device_id=(flip(chip, r) * 2 + core, z), device_id_type=MESH)
    pl.semaphore_signal(barrier, inc=1, device_id=(chip * 2 + 1 - core, z), device_id_type=MESH)
    for shift in (1, count - 1):
        pl.semaphore_signal(barrier, inc=1, device_id=(dp, lax.rem(z + shift, count)), device_id_type=MESH)
    pl.semaphore_wait(barrier, chips + 2)


def forward_kernel(
    chips, count,
    x, gain, beta, wqkv, wf1, wo, wf2, cot, bqkv, bf1, table_c, table_s, seg_col, seg_row,
    gqkv, gf1, go, gf2, gcot, hid_t, q_out, k_out, v_out, att_t_out, lse_out, act_t, dgelu, part_out,
    hid, vqkv, vf1, vf2, vo, q, k, v, att, att_t, lse, act, part, stage_a, stage_b,
    w_send, w_recv, p_send, p_recv, own_sem, h_us, h_ur, h_ds, h_dr, c_us, c_ur, c_ds, c_dr, load_sem, save_sem, st_sem,
):
    z = lax.axis_index("branch")
    dp = lax.axis_index("dp")
    rows, width = x.shape
    length = rows * count
    hcols = wo.shape[0]
    units = wf2.shape[0]
    sems = (w_send, w_recv, p_send, p_recv, own_sem)
    g_qkv = Gather(0, wqkv, gqkv, True, chips, sems)
    g_f1 = Gather(1, wf1, gf1, True, chips, sems)
    g_o = Gather(2, wo, go, False, chips, sems)
    g_f2 = Gather(3, wf2, gf2, False, chips, sems)
    own_rows = hid.at[aligned(z, rows), :]
    h_chain = Chain(own_rows, hid, rows, count, (h_us, h_ur, h_ds, h_dr), dp)
    c_chain = Chain(cot, gcot, rows, count, (c_us, c_ur, c_ds, c_dr), dp)

    greet(chips, count)
    for g in (g_qkv, g_f1, g_o, g_f2):
        g.start()
        g.start_pair()
    keep_cot = pltpu.make_async_copy(cot, gcot.at[aligned(z, rows), :], load_sem.at[5])
    keep_cot.start()

    step_rows = 32

    def norm(i, _):
        part_rows = aligned(i, step_rows)
        inputs = x[part_rows, :].astype(F32)
        center = inputs - jnp.mean(inputs, axis=-1, keepdims=True)
        inverse = lax.rsqrt(jnp.mean(center * center, axis=-1, keepdims=True) + EPSILON)
        where = pl.ds(pl.multiple_of(z * rows + i * step_rows, step_rows), step_rows)
        hid[where, :] = (center * inverse * gain[...] + beta[...]).astype(BF16)
        return 0

    lax.fori_loop(0, rows // step_rows, norm, 0)
    h_chain.start()
    for r in range(1, chips - 1):
        g_qkv.pump(r)
    if count > 2:
        h_chain.pump(1)
    if chips > 1:
        g_qkv.pump(chips - 1)
    g_qkv.arrive()
    load_qkv = pltpu.make_async_copy(gqkv, vqkv, load_sem.at[0])
    load_qkv.start()
    for s in range(2, count - 1):
        h_chain.pump(s)
    c_chain.start()
    h_chain.arrive()
    load_qkv.wait()

    mt = tile_of(length)
    ht = tile_of(hcols)

    def project(i, _):
        rows_i = aligned(i, mt)
        for which, dest in ((0, q), (1, k), (2, v)):
            for c in range(hcols // ht):
                at = which * hcols + c * ht
                y = dot_nn(hid[rows_i, :], vqkv[:, at : at + ht]) + bqkv[:, at : at + ht]
                for piece in range(ht // LANES):
                    part_y = y[:, piece * LANES : (piece + 1) * LANES]
                    to = c * ht + piece * LANES
                    if which < 2:
                        lane = lax.rem(lax.broadcasted_iota(jnp.int32, part_y.shape, 1), HEAD_DIM)
                        other = jnp.where(
                            lane < ROT // 2,
                            pltpu.roll(part_y, LANES - ROT // 2, 1),
                            pltpu.roll(part_y, ROT // 2, 1),
                        )
                        part_y = part_y * table_c[rows_i, :] + other * table_s[rows_i, :]
                    low = part_y.astype(BF16)
                    if which == 0:
                        low = low * BF16(HEAD_DIM**-0.5)
                    dest[rows_i, to : to + LANES] = low
        return 0

    lax.fori_loop(0, length // mt, project, 0)
    saves = []

    def save(src, dst):
        c = pltpu.make_async_copy(src, dst, save_sem.at[len(saves)])
        c.start()
        saves.append(c)

    save(q, q_out)
    save(k, k_out)
    save(v, v_out)
    if count > 2:
        c_chain.pump(1)

    qb = tile_of(length, QBLOCK)

    def attend(pair, _):
        cols = aligned(pair, LANES)
        lane = lax.broadcasted_iota(jnp.int32, (1, LANES), 1)
        for b in range(length // qb):
            here = slice(b * qb, (b + 1) * qb)
            before = b * qb
            q2 = q[here, cols]
            seg_q = seg_col[here, :]
            ki = lax.broadcasted_iota(jnp.int32, (qb, qb), 1)
            qi = lax.broadcasted_iota(jnp.int32, (qb, qb), 0)
            seen_here = jnp.logical_or(
                jnp.logical_and(seg_q == seg_row[:, here], ki <= qi), ki == qi
            )
            out = jnp.zeros((qb, LANES), F32)
            stat = jnp.zeros((qb, LANES), F32)
            for h in range(2):
                mine = (lane // HEAD_DIM) == h
                qh = jnp.where(mine, q2, BF16(0))
                s_here = jnp.where(seen_here, dot_nt(qh, k[here, cols]), NEGATIVE)
                top = jnp.max(s_here, axis=-1, keepdims=True)
                if before:
                    s_before = jnp.where(
                        seg_q == seg_row[:, :before], dot_nt(qh, k[:before, cols]), NEGATIVE
                    )
                    top = jnp.maximum(top, jnp.max(s_before, axis=-1, keepdims=True))
                e_here = jnp.exp(s_here - top)
                total = jnp.sum(e_here, axis=-1, keepdims=True)
                if before:
                    e_before = jnp.exp(s_before - top)
                    total = total + jnp.sum(e_before, axis=-1, keepdims=True)
                share = 1.0 / total
                o = dot_nn((e_here * share).astype(BF16), jnp.where(mine, v[here, cols], BF16(0)))
                if before:
                    o = o + dot_nn(
                        (e_before * share).astype(BF16), jnp.where(mine, v[:before, cols], BF16(0))
                    )
                out = out + o
                stat = jnp.where(mine, top + jnp.log(total), stat)
            att[here, cols] = out.astype(BF16)
            att_t[cols, here] = out.T.astype(BF16)
            turned = stat.T
            lse[pl.ds(2 * pair, 1), here] = turned[0:1, :]
            lse[pl.ds(2 * pair + 1, 1), here] = turned[HEAD_DIM : HEAD_DIM + 1, :]
        return 0

    pairs = hcols // LANES
    lax.fori_loop(0, pairs // 2, attend, 0)
    for r in range(1, chips):
        g_f1.pump(r)
    g_f1.arrive()
    load_f1 = pltpu.make_async_copy(gf1, vf1, load_sem.at[1])
    load_f1.start()
    for s in range(2, count - 1):
        c_chain.pump(s)
    lax.fori_loop(pairs // 2, pairs, attend, 0)
    save(att_t, att_t_out)
    save(lse, lse_out)
    for r in range(1, chips):
        g_o.pump(r)
    g_o.arrive()
    load_o = pltpu.make_async_copy(go, vo, load_sem.at[2])
    load_o.start()
    load_f1.wait()

    ft = tile_of(units)
    per_row = units // ft
    n_tiles = (length // mt) * per_row

    def staged(slot, rows_i, cols_i, which):
        src = (stage_a if which == 0 else stage_b).at[slot]
        dst = act_t.at[cols_i, rows_i] if which == 0 else dgelu.at[rows_i, cols_i]
        return pltpu.make_async_copy(src, dst, st_sem.at[which, slot])

    def unit(i, _):
        rows_i, cols_i = aligned(lax.div(i, per_row), mt), aligned(lax.rem(i, per_row), ft)
        slot = lax.rem(i, 2)

        @pl.when(i >= 2)
        def _():
            for which in range(2):
                staged(slot, rows_i, cols_i, which).wait()

        y = dot_nn(hid[rows_i, :], vf1[:, cols_i]) + bf1[:, cols_i]
        square = y * y
        t = jnp.tanh(GELU_C * (y + GELU_A * (y * square)))
        half = 0.5 * (1.0 + t)
        low = (y * half).astype(BF16)
        act[rows_i, cols_i] = low
        stage_a[slot] = low.T
        stage_b[slot] = (
            half + 0.5 * y * (1.0 - t * t) * (GELU_C * (1.0 + 3.0 * GELU_A * square))
        ).astype(BF16)
        for which in range(2):
            staged(slot, rows_i, cols_i, which).start()
        return 0

    lax.fori_loop(0, n_tiles, unit, 0)
    for i in range(max(n_tiles - 2, 0), n_tiles):
        for which in range(2):
            staged(i % 2, pl.ds(0, mt), pl.ds(0, ft), which).wait()

    wt = tile_of(width)
    per_col = width // wt
    n_turn = (length // mt) * per_col

    def turn_copy(slot, rows_i, cols_i):
        return pltpu.make_async_copy(
            stage_a.at[slot, pl.ds(0, wt), :], hid_t.at[cols_i, rows_i], st_sem.at[0, slot]
        )

    def turn(i, _):
        rows_i, cols_i = aligned(lax.div(i, per_col), mt), aligned(lax.rem(i, per_col), wt)
        slot = lax.rem(i, 2)

        @pl.when(i >= 2)
        def _():
            turn_copy(slot, rows_i, cols_i).wait()

        stage_a[slot, 0:wt, :] = hid[rows_i, cols_i].T
        turn_copy(slot, rows_i, cols_i).start()
        return 0

    lax.fori_loop(0, n_turn, turn, 0)
    for i in range(max(n_turn - 2, 0), n_turn):
        turn_copy(i % 2, pl.ds(0, mt), pl.ds(0, wt)).wait()

    for r in range(1, chips):
        g_f2.pump(r)
    g_f2.arrive()
    load_f2 = pltpu.make_async_copy(gf2, vf2, load_sem.at[3])
    load_f2.start()
    load_o.wait()
    load_f2.wait()

    def output(i, _):
        rows_i, cols_i = aligned(lax.div(i, per_col), mt), aligned(lax.rem(i, per_col), wt)
        part[rows_i, cols_i] = (
            dot_nn(act[rows_i, :], vf2[:, cols_i]) + dot_nn(att[rows_i, :], vo[:, cols_i])
        ).astype(BF16)
        return 0

    lax.fori_loop(0, n_turn, output, 0)
    save(part, part_out)
    c_chain.arrive()
    keep_cot.wait()
    for g in (g_qkv, g_f1, g_o, g_f2):
        g.finish()
    h_chain.finish()
    c_chain.finish()
    for c in saves:
        c.wait()


def run_forward(ndp, count, x, gain, beta, wqkv, wf1, wo, wf2, cot, bqkv, bf1, tables, seg_col, seg_row):
    chips = ndp // 2
    rows, width = x.shape
    length = rows * count
    hcols, units = wo.shape[0], wf2.shape[0]
    heads = hcols // HEAD_DIM
    mt, ft, wt = tile_of(length), tile_of(units), tile_of(width)
    anywhere = pl.BlockSpec(memory_space=pl.ANY)
    vmem = pl.BlockSpec(memory_space=pltpu.VMEM)
    low = lambda *shape: jax.ShapeDtypeStruct(shape, BF16)
    outs = [
        low(width, 3 * hcols), low(width, units), low(hcols, width), low(units, width), low(length, width),
        low(width, length), low(length, hcols), low(length, hcols), low(length, hcols), low(hcols, length),
        jax.ShapeDtypeStruct((heads, length), F32), low(units, length), low(length, units), low(length, width),
    ]
    v = lambda *shape: pltpu.VMEM(shape, BF16)
    steps = max(count - 1, 1)
    dma = lambda *shape: pltpu.SemaphoreType.DMA(shape)
    scratch = [
        v(length, width), v(width, 3 * hcols), v(width, units), v(units, width), v(hcols, width),
        v(length, hcols), v(length, hcols), v(length, hcols), v(length, hcols), v(hcols, length),
        pltpu.VMEM((heads, length), F32), v(length, units), v(length, width),
        v(2, max(ft, wt), mt), v(2, mt, ft),
        dma(4, max(chips - 1, 1)), dma(4, max(chips - 1, 1)), dma(4, chips), dma(4, chips), dma(4),
        *[dma(steps) for _ in range(8)], dma(6), dma(8), dma(2, 2),
    ]
    return pl.pallas_call(
        functools.partial(forward_kernel, chips, count),
        out_shape=outs,
        in_specs=[vmem, vmem, vmem, anywhere, anywhere, anywhere, anywhere, anywhere] + [vmem] * 6,
        out_specs=[anywhere] * len(outs),
        scratch_shapes=scratch,
        compiler_params=pltpu.CompilerParams(
            collective_id=0, has_side_effects=True, vmem_limit_bytes=VMEM_LIMIT
        ),
        name="gather_forward",
    )(x, gain, beta, wqkv, wf1, wo, wf2, cot, bqkv, bf1, *tables, seg_col, seg_row)


class Fold:
    def __init__(self, bufs, sems, count, dp):
        self.bufs, self.sems, self.count, self.dp = bufs, sems, count, dp
        self.z = lax.axis_index("branch")

    def place(self, up):
        return self.z if up else self.count - 1 - self.z

    def dest(self, up, step):
        return self.count - 1 - step if up else step

    def hop(self, up, step, src=None):
        buf = self.bufs[0 if up else 1]
        send, recv = self.sems[0 if up else 2], self.sems[1 if up else 3]
        return pltpu.make_async_remote_copy(
            src_ref=buf.at[step] if src is None else src,
            dst_ref=buf.at[step],
            send_sem=send.at[step],
            recv_sem=recv.at[step],
            device_id=(self.dp, self.z + 1 if up else self.z - 1),
            device_id_type=MESH,
        )

    def first(self, up, step, src):
        @pl.when(self.place(up) == 0)
        def _():
            self.hop(up, step, src).start()

    def pump(self, k, own_block, rows):
        for up in (False, True):
            place = self.place(up)

            @pl.when(jnp.logical_and(place >= 1, place <= k))
            def _(up=up, place=place):
                step = k - place
                own = own_block(up, self.dest(up, step))
                self.hop(up, step).wait_recv()
                buf = self.bufs[0 if up else 1]

                def add(i, _):
                    part = aligned(i, 32)
                    buf[step, part, :] = (buf[step, part, :].astype(F32) + own[part, :].astype(F32)).astype(BF16)
                    return 0

                lax.fori_loop(0, rows // 32, add, 0)
                self.hop(up, step).start()

    def last_step(self, up):
        return jnp.clip(self.count - 1 - self.place(up), 0, self.count - 2)

    def arrive(self):
        for up in (False, True):

            @pl.when(self.place(up) >= 1)
            def _(up=up):
                self.hop(up, self.last_step(up)).wait_recv()

    def total(self, own, part):
        out = own
        for up in (False, True):
            got = self.bufs[0 if up else 1][self.last_step(up), part, :].astype(F32)
            out = out + jnp.where(self.place(up) >= 1, got, 0.0)
        return out

    def finish(self):
        for step in range(self.count - 1):
            for up in (False, True):

                @pl.when(self.place(up) + step <= self.count - 2)
                def _(up=up, step=step):
                    self.hop(up, step).wait_send()


class Scatter:
    def __init__(self, index, block, tile, rows_first, slots, landing, own_out, stage, wide, chips, sems):
        self.index, self.block, self.tile, self.rows_first = index, block, tile, rows_first
        self.slots, self.landing, self.own_out, self.stage, self.wide = slots, landing, own_out, stage, wide
        self.chips = chips
        self.st_sem, self.pair_recv, self.send, self.recv, self.wide_sem = sems
        dp = lax.axis_index("dp")
        self.z = lax.axis_index("branch")
        self.core, self.chip = lax.rem(dp, 2), lax.div(dp, 2)
        self.tiles = slots.shape[2 if rows_first else 1] // tile
        self.height = slots.shape[1] if rows_first else tile
        self.breadth = tile if rows_first else slots.shape[2]
        self.order = [*range(1, chips), 0]

    def part(self, ref, i):
        at = aligned(i, self.tile)
        return ref.at[:, at] if self.rows_first else ref.at[at, :]

    def view(self, ref, slot):
        return ref.at[slot, pl.ds(0, self.height), pl.ds(0, self.breadth)]

    def to_pair(self, r, i, slot):
        return pltpu.make_async_remote_copy(
            src_ref=self.view(self.stage, slot),
            dst_ref=self.part(self.slots.at[r], i),
            send_sem=self.st_sem.at[slot],
            recv_sem=self.pair_recv.at[self.index, r],
            device_id=(self.chip * 2 + 1 - self.core, self.z),
            device_id_type=MESH,
        )

    def from_pair(self, r):
        return pltpu.make_async_remote_copy(
            src_ref=self.slots.at[r],
            dst_ref=self.slots.at[r],
            send_sem=self.st_sem.at[0],
            recv_sem=self.pair_recv.at[self.index, r],
            device_id=(self.chip * 2 + 1 - self.core, self.z),
            device_id_type=MESH,
        )

    def to_owner(self, r):
        return pltpu.make_async_remote_copy(
            src_ref=self.slots.at[r],
            dst_ref=self.landing.at[r - 1],
            send_sem=self.send.at[self.index, r - 1],
            recv_sem=self.recv.at[self.index, r - 1],
            device_id=(flip(self.chip, r) * 2 + self.core, self.z),
            device_id_type=MESH,
        )

    def to_out(self, i, slot):
        return pltpu.make_async_copy(self.view(self.wide, slot), self.part(self.own_out, i), self.wide_sem.at[slot])

    def partners(self, n):
        r = self.order[n]
        owner = flip(self.chip, r) * 2 + 1 - self.core

        def body(i, _):
            slot = lax.rem(n * self.tiles + i, 2)
            y = self.block(owner, i)
            if n * self.tiles >= 2:
                self.to_pair(r, i, slot).wait_send()
            else:

                @pl.when(n * self.tiles + i >= 2)
                def _():
                    self.to_pair(r, i, slot).wait_send()

            self.stage[slot, 0 : self.height, 0 : self.breadth] = y.astype(BF16)
            self.to_pair(r, i, slot).start()
            return 0

        lax.fori_loop(0, self.tiles, body, 0)

    def own(self, n):
        r = self.order[n]
        owner = flip(self.chip, r) * 2 + self.core
        self.from_pair(r).wait_recv()

        def body(i, _):
            y = self.block(owner, i)
            at = aligned(i, self.tile)
            if self.rows_first:
                y = y + self.slots[r, :, at].astype(F32)
            else:
                y = y + self.slots[r, at, :].astype(F32)
            if r:
                if self.rows_first:
                    self.slots[r, :, at] = y.astype(BF16)
                else:
                    self.slots[r, at, :] = y.astype(BF16)
            else:
                slot = lax.rem(i, 2)

                @pl.when(i >= 2)
                def _():
                    self.to_out(i, slot).wait()

                self.wide[slot, 0 : self.height, 0 : self.breadth] = y
                self.to_out(i, slot).start()
            return 0

        lax.fori_loop(0, self.tiles, body, 0)
        if r:
            self.to_owner(r).start()
        else:
            for i in range(max(self.tiles - 2, 0), self.tiles):
                self.to_out(i, i % 2).wait()

    def run(self, before=lambda n: None):
        for n in range(self.chips):
            before(n)
            self.partners(n)
            if n:
                self.own(n - 1)
        self.own(self.chips - 1)
        total = self.chips * self.tiles
        for i in range(max(total - 2, 0), total):
            self.to_pair(0, 0, i % 2).wait_send()

    def finish(self):
        for r in range(1, self.chips):
            self.to_owner(r).wait_send()
            self.to_owner(r).wait_recv()


def greet_all(chips, count):
    dp, z = lax.axis_index("dp"), lax.axis_index("branch")
    core, chip = lax.rem(dp, 2), lax.div(dp, 2)
    barrier = pltpu.get_barrier_semaphore()
    for r in range(1, chips):
        pl.semaphore_signal(barrier, inc=1, device_id=(flip(chip, r) * 2 + core, z), device_id_type=MESH)
    pl.semaphore_signal(barrier, inc=1, device_id=(chip * 2 + 1 - core, z), device_id_type=MESH)
    for shift in range(1, count):
        pl.semaphore_signal(barrier, inc=1, device_id=(dp, lax.rem(z + shift, count)), device_id_type=MESH)
    pl.semaphore_wait(barrier, chips + count - 1)


def piece_of(extent):
    return next(n for n in (512, 256, 128) if extent % n == 0)


def backward_kernel(
    chips, count,
    gqkv, gf1, go, gf2, gcot, hid_t, q_in, k_in, v_in, att_t, act_t, dgelu, part_in, x_in,
    lse, gain, out_bias, table_c, table_s, seg_row, seg_col,
    block_out, input_grad, vec_out, own_qkv, own_f1, own_o, own_f2, land_qkv, land_f1, land_o, land_f2,
    g, pre, big, mid, qkv, att_grad, dk_acc, dv_acc, k_t, hid_stage, tmp, s_qkv, s_f1, s_o, s_f2, up_buf, dn_buf,
    st_row, st_col, wide_row, wide_col, ig_stage, vec, vec_pair, vec_chip, vec_z,
    load_sem, hid_sem, dg_sem, tmp_sem, out_sem, ig_sem, st_row_sem, st_col_sem, pair_recv, x_send, x_recv, wide_row_sem, wide_col_sem,
    zo_us, zo_ur, zo_ds, zo_dr, zh_us, zh_ur, zh_ds, zh_dr, free_up, free_dn, v_ps, v_pr, v_cs, v_cr, v_zs, v_zr,
):
    z = lax.axis_index("branch")
    dp = lax.axis_index("dp")
    core, chip = lax.rem(dp, 2), lax.div(dp, 2)
    length, width = g.shape
    rows = length // count
    hcols, units, third = go.shape[0], gf2.shape[0], go.shape[0]
    part_w = width // (2 * chips)
    last = count - 1
    mt, ft, wt = tile_of(length), tile_of(units), tile_of(width)
    f2_v, f1_v, o_v = big.at[0:units, 0:width], big.at[0:width, 0:units], big.at[0:hcols, 0:width]
    act_v, att_v, wqkv_v = mid.at[0:units, 0:length], mid.at[0:hcols, 0:length], mid.at[0:width, 0 : 3 * hcols]

    def load(src, dst, n):
        c = pltpu.make_async_copy(src, dst, load_sem.at[n])
        c.start()
        return c

    load_g = load(gcot, g, 0)
    load_act = load(act_t, act_v, 1)
    load_f2 = load(gf2, f2_v, 2)
    greet_all(chips, count)

    def rows_of(ref, d):
        return ref.at[aligned(d, rows), :]

    fold_out = Fold((up_buf, dn_buf), (zo_us, zo_ur, zo_ds, zo_dr), count, dp)
    fold_hid = Fold((up_buf, dn_buf), (zh_us, zh_ur, zh_ds, zh_dr), count, dp)
    for s in range(count - 1):
        fold_out.first(True, s, rows_of(part_in, last - s))
        fold_out.first(False, s, rows_of(part_in, s))

    def fetched(up, d):
        n = 0 if up else 1
        c = pltpu.make_async_copy(rows_of(part_in, d), tmp.at[n], tmp_sem.at[n])
        c.start()
        c.wait()
        return tmp.at[n]

    sems_row = (st_row_sem, pair_recv, x_send, x_recv, wide_row_sem)
    sems_col = (st_col_sem, pair_recv, x_send, x_recv, wide_col_sem)
    tile_f2, tile_o = piece_of(units), piece_of(hcols)
    tile_f1, tile_qkv = piece_of(units), piece_of(3 * hcols)

    def f2_block(owner, i):
        return dot_nn(act_v[aligned(i, tile_f2), :], g[:, aligned(owner, part_w)])

    def o_block(owner, i):
        return dot_nn(att_v[aligned(i, tile_o), :], g[:, aligned(owner, part_w)])

    def hid_copy(n, which, r, slot_core):
        owner = flip(chip, r) * 2 + slot_core
        return pltpu.make_async_copy(
            hid_t.at[aligned(owner, part_w), :], hid_stage.at[2 * which + n % 2], hid_sem.at[2 * which + n % 2]
        )

    state = {}

    def f1_block(owner, i):
        return dot_nn(hid_stage[state["at"]], pre[:, aligned(i, tile_f1)])

    def qkv_block(owner, i):
        return dot_nn(hid_stage[state["at"]], qkv[:, aligned(i, tile_qkv)])

    def run_rows(scatter):
        order = scatter.order
        hid_copy(0, 0, order[0], 1 - core).start()
        hid_copy(0, 1, order[0], core).start()
        for n in range(chips):
            if n + 1 < chips:
                hid_copy(n + 1, 0, order[n + 1], 1 - core).start()
            hid_copy(n, 0, order[n], 1 - core).wait()
            state["at"] = n % 2
            scatter.partners(n)
            if n:
                hid_copy(n, 1, order[n], core).start()
                hid_copy(n - 1, 1, order[n - 1], core).wait()
                state["at"] = 2 + (n - 1) % 2
                scatter.own(n - 1)
        hid_copy(chips - 1, 1, order[chips - 1], core).wait()
        state["at"] = 2 + (chips - 1) % 2
        scatter.own(chips - 1)
        total = chips * scatter.tiles
        for i in range(max(total - 2, 0), total):
            scatter.to_pair(0, 0, i % 2).wait_send()

    sc_f2 = Scatter(0, f2_block, tile_f2, False, s_f2, land_f2, own_f2, st_col, wide_col, chips, sems_col)
    sc_f1 = Scatter(1, f1_block, tile_f1, True, s_f1, land_f1, own_f1, st_row, wide_row, chips, sems_row)
    sc_o = Scatter(2, o_block, tile_o, False, s_o, land_o, own_o, st_col, wide_col, chips, sems_col)
    sc_qkv = Scatter(3, qkv_block, tile_qkv, True, s_qkv, land_qkv, own_qkv, st_row, wide_row, chips, sems_row)

    at_f1, at_ob = 3 * hcols, 3 * hcols + units
    at_gain, at_beta = at_ob + width, at_ob + 2 * width

    load_g.wait()
    load_act.wait()
    sc_f2.run()

    per_row = units // ft
    n_tiles = (length // mt) * per_row

    def dg_copy(i):
        n = lax.rem(i, 2)
        return pltpu.make_async_copy(
            dgelu.at[aligned(lax.div(i, per_row), mt), aligned(lax.rem(i, per_row), ft)],
            qkv.at[pl.ds(pl.multiple_of(n * mt, mt), mt), 0:ft],
            dg_sem.at[n],
        )

    load_f2.wait()
    load_att = load(att_t, att_v, 1)
    dg_copy(0).start()
    vec[...] = jnp.zeros_like(vec)

    def unit(i, _):
        rows_i, cols_i = aligned(lax.div(i, per_row), mt), aligned(lax.rem(i, per_row), ft)

        @pl.when(i + 1 < n_tiles)
        def _():
            dg_copy(i + 1).start()

        y = dot_nt(g[rows_i, :], f2_v[cols_i, :])
        dg_copy(i).wait()
        slot_rows = pl.ds(pl.multiple_of(lax.rem(i, 2) * mt, mt), mt)
        low = (y * qkv[slot_rows, 0:ft].astype(F32)).astype(BF16)
        pre[rows_i, cols_i] = low
        to = pl.ds(pl.multiple_of(at_f1 + lax.rem(i, per_row) * ft, LANES), ft)
        vec[:, to] += jnp.sum(low.astype(F32), axis=0, keepdims=True)
        return 0

    lax.fori_loop(0, n_tiles, unit, 0)
    load_o = load(go, o_v, 2)
    load_q = load(q_in, qkv.at[:, 0:third], 3)
    load_k = load(k_in, qkv.at[:, third : 2 * third], 4)
    load_v = load(v_in, qkv.at[:, 2 * third : 3 * third], 5)
    if count > 2:
        fold_out.pump(1, fetched, rows)
    run_rows(sc_f1)

    load_o.wait()
    load_att.wait()

    def att_back(i, _):
        rows_i = aligned(i, mt)
        att_grad[rows_i, :] = dot_nt(g[rows_i, :], o_v[...]).astype(BF16)
        return 0

    lax.fori_loop(0, length // mt, att_back, 0)
    load_f1 = load(gf1, f1_v, 2)
    sc_o.run()
    load_wqkv = load(gqkv, wqkv_v, 1)

    def cot_sum(i, _):
        vec[:, at_ob : at_ob + width] += jnp.sum(g[aligned(i, 64), :].astype(F32), axis=0, keepdims=True)
        return 0

    lax.fori_loop(0, length // 64, cot_sum, 0)
    load_q.wait()
    load_k.wait()
    load_v.wait()

    qb = tile_of(length, QBLOCK)
    pairs = hcols // LANES

    def turn_back(y, at):
        lane = lax.rem(lax.broadcasted_iota(jnp.int32, y.shape, 1), HEAD_DIM)
        other = jnp.where(
            lane < ROT // 2, pltpu.roll(y, LANES - ROT // 2, 1), pltpu.roll(y, ROT // 2, 1)
        )
        return y * table_c[at, :] - other * table_s[at, :]

    def attend(pair, _):
        q_cols = aligned(pair, LANES)
        k_cols, v_cols = aligned(pairs + pair, LANES), aligned(2 * pairs + pair, LANES)
        lane = lax.broadcasted_iota(jnp.int32, (1, LANES), 1)
        dk_acc[...] = jnp.zeros_like(dk_acc)
        dv_acc[...] = jnp.zeros_like(dv_acc)
        k_t[...] = qkv[:, k_cols].T
        for b in range(length // qb):
            here, reach = slice(b * qb, (b + 1) * qb), (b + 1) * qb
            before = b * qb
            q2, g2 = qkv[here, q_cols], att_grad[here, q_cols]
            ki = lax.broadcasted_iota(jnp.int32, (qb, qb), 0)
            qi = lax.broadcasted_iota(jnp.int32, (qb, qb), 1)
            seen_here = jnp.logical_or(
                jnp.logical_and(seg_col[here, :] == seg_row[:, here], ki <= qi), ki == qi
            )
            dq_t = []
            for h in range(2):
                mine = (lane // HEAD_DIM) == h
                qh, gh = jnp.where(mine, q2, BF16(0)), jnp.where(mine, g2, BF16(0))
                stat = lse[pl.ds(2 * pair + h, 1), here]
                spans = ([(0, before)] if before else []) + [(before, reach)]
                probs, grads = [], []
                delta = jnp.zeros((1, qb), F32)
                for lo, hi in spans:
                    seen = seen_here if lo == before else seg_col[lo:hi, :] == seg_row[:, here]
                    p = jnp.exp(jnp.where(seen, dot_nt(qkv[lo:hi, k_cols], qh), NEGATIVE) - stat)
                    pg = dot_nt(qkv[lo:hi, v_cols], gh)
                    delta = delta + jnp.sum(p * pg, axis=0, keepdims=True)
                    probs.append(p)
                    grads.append(pg)
                acc = jnp.zeros((HEAD_DIM, qb), F32)
                for (lo, hi), p, pg in zip(spans, probs, grads):
                    sg = (p * (pg - delta)).astype(BF16)
                    dv_acc[lo:hi, :] += dot_nn(p.astype(BF16), gh)
                    dk_acc[lo:hi, :] += dot_nn(sg, qh)
                    acc = acc + dot_nn(k_t[h * HEAD_DIM : (h + 1) * HEAD_DIM, lo:hi], sg)
                dq_t.append(acc)
            dq = jnp.concatenate(dq_t, axis=0).T * HEAD_DIM**-0.5
            qkv[here, q_cols] = turn_back(dq, here).astype(BF16)
        for b in range(length // qb):
            here = slice(b * qb, (b + 1) * qb)
            qkv[here, k_cols] = turn_back(dk_acc[here, :], here).astype(BF16)
            qkv[here, v_cols] = dv_acc[here, :].astype(BF16)
        for cols in (q_cols, k_cols, v_cols):
            vec[:, cols] = jnp.sum(qkv[:, cols].astype(F32), axis=0, keepdims=True)
        return 0

    first_pairs = max(pairs // 4, 1)
    lax.fori_loop(0, first_pairs, attend, 0)
    for k in range(2, count - 1):
        fold_out.pump(k, fetched, rows)
    lax.fori_loop(first_pairs, pairs, attend, 0)

    fold_out.arrive()
    load_x = pltpu.make_async_copy(x_in, tmp.at[0], tmp_sem.at[0])
    load_x.start()
    load_own = pltpu.make_async_copy(rows_of(part_in, z), tmp.at[1], tmp_sem.at[1])
    load_own.start()
    load_x.wait()
    load_own.wait()

    def finish_output(i, _):
        part = aligned(i, 32)
        y = fold_out.total(tmp[1, part, :].astype(F32), part)
        tmp[1, part, :] = (tmp[0, part, :].astype(F32) + y + out_bias[...]).astype(BF16)
        return 0

    lax.fori_loop(0, rows // 32, finish_output, 0)
    save_out = pltpu.make_async_copy(tmp.at[1], block_out, out_sem)
    save_out.start()
    fold_out.finish()

    @pl.when(z > 0)
    def _():
        pl.semaphore_signal(free_up, inc=1, device_id=(dp, z - 1), device_id_type=MESH)

    @pl.when(z < last)
    def _():
        pl.semaphore_signal(free_dn, inc=1, device_id=(dp, z + 1), device_id_type=MESH)

    load_f1.wait()
    load_wqkv.wait()

    def hidden_back(d):
        here = pl.ds(d * rows, rows)

        def body(i, _):
            cols_i = aligned(i, wt)
            g[here, cols_i] = (
                dot_nt(pre[here, :], f1_v[cols_i, :]) + dot_nt(qkv[here, :], wqkv_v[cols_i, :])
            ).astype(BF16)
            return 0

        lax.fori_loop(0, width // wt, body, 0)

    dests = [d for pair in zip(range(last, -1, -1), range(count)) for d in pair]
    dests = list(dict.fromkeys(dests))
    for n, d in enumerate(dests):
        hidden_back(d)
        if n == 0:

            @pl.when(z < last)
            def _():
                pl.semaphore_wait(free_up, 1)

            @pl.when(z > 0)
            def _():
                pl.semaphore_wait(free_dn, 1)

        if d > 0:
            fold_hid.first(True, last - d, rows_of(g, d))
        if d < last:
            fold_hid.first(False, d, rows_of(g, d))

    save_out.wait()
    load_cot = pltpu.make_async_copy(rows_of(gcot, z), tmp.at[1], tmp_sem.at[1])
    load_cot.start()
    run_rows(sc_qkv)
    for k in range(1, count - 1):
        fold_hid.pump(k, lambda up, d: rows_of(g, d), rows)
    fold_hid.arrive()
    load_cot.wait()

    step_rows = 32

    def ig_copy(i, slot):
        return pltpu.make_async_copy(ig_stage.at[slot], input_grad.at[aligned(i, step_rows), :], ig_sem.at[slot])

    def norm_back(i, _):
        part = aligned(i, step_rows)
        slot = lax.rem(i, 2)
        inputs = tmp[0, part, :].astype(F32)
        center = inputs - jnp.mean(inputs, axis=-1, keepdims=True)
        inverse = lax.rsqrt(jnp.mean(center * center, axis=-1, keepdims=True) + EPSILON)
        normed = center * inverse
        own = g[pl.ds(pl.multiple_of(z * rows + i * step_rows, step_rows), step_rows), :].astype(F32)
        y = fold_hid.total(own, part)
        vec[:, at_gain : at_gain + width] += jnp.sum(y * normed, axis=0, keepdims=True)
        vec[:, at_beta : at_beta + width] += jnp.sum(y, axis=0, keepdims=True)
        scaled = y * gain[...]
        result = tmp[1, part, :].astype(F32) + inverse * (
            scaled
            - jnp.mean(scaled, axis=-1, keepdims=True)
            - normed * jnp.mean(scaled * normed, axis=-1, keepdims=True)
        )

        @pl.when(i >= 2)
        def _():
            ig_copy(i, slot).wait()

        ig_stage[slot] = result
        ig_copy(i, slot).start()
        return 0

    steps = rows // step_rows
    lax.fori_loop(0, steps, norm_back, 0)

    to_pair = pltpu.make_async_remote_copy(
        src_ref=vec, dst_ref=vec_pair, send_sem=v_ps, recv_sem=v_pr,
        device_id=(chip * 2 + 1 - core, z), device_id_type=MESH,
    )
    to_pair.start()
    for i in range(max(steps - 2, 0), steps):
        ig_copy(i, i % 2).wait()
    to_pair.wait()
    vec_chip[chip] = vec[...] + vec_pair[...]

    def chip_copy(r, slot):
        return pltpu.make_async_remote_copy(
            src_ref=vec_chip.at[chip], dst_ref=vec_chip.at[slot], send_sem=v_cs.at[r - 1], recv_sem=v_cr.at[r - 1],
            device_id=(flip(chip, r) * 2 + core, z), device_id_type=MESH,
        )

    for r in range(1, chips):
        chip_copy(r, chip).start()
    for r in range(1, chips):
        chip_copy(r, flip(chip, r)).wait_recv()
    total = vec_chip[0]
    for c in range(1, chips):
        total = total + vec_chip[c]
    vec_out[:, 0:at_gain] = total[:, 0:at_gain]
    vec_z[z] = total[:, at_gain:]

    def z_copy(shift, slot):
        return pltpu.make_async_remote_copy(
            src_ref=vec_z.at[z], dst_ref=vec_z.at[slot], send_sem=v_zs.at[shift - 1], recv_sem=v_zr.at[shift - 1],
            device_id=(dp, lax.rem(z + shift, count)), device_id_type=MESH,
        )

    for shift in range(1, count):
        z_copy(shift, z).start()
    for shift in range(1, count):
        z_copy(shift, lax.rem(z + count - shift, count)).wait_recv()
    total = vec_z[0]
    for n in range(1, count):
        total = total + vec_z[n]
    vec_out[:, at_gain:] = total
    for r in range(1, chips):
        chip_copy(r, chip).wait_send()
    for shift in range(1, count):
        z_copy(shift, z).wait_send()
    fold_hid.finish()
    for s in (sc_f2, sc_f1, sc_o, sc_qkv):
        s.finish()


def run_backward(ndp, count, gathered, saved, x, lse, gain, out_bias, tables, seg_row, seg_col):
    chips = ndp // 2
    gqkv, gf1, go, gf2, gcot, hid_t = gathered
    length, width = gcot.shape
    rows, hcols, units = length // count, go.shape[0], gf2.shape[0]
    part_w = width // ndp
    heads = hcols // HEAD_DIM
    mt, ft = tile_of(length), tile_of(units)
    total = 3 * hcols + units + 3 * width
    anywhere = pl.BlockSpec(memory_space=pl.ANY)
    vmem = pl.BlockSpec(memory_space=pltpu.VMEM)
    low = lambda *shape: jax.ShapeDtypeStruct(shape, BF16)
    wide = lambda *shape: jax.ShapeDtypeStruct(shape, F32)
    outs = [
        low(rows, width), wide(rows, width), wide(1, total),
        wide(part_w, 3 * hcols), wide(part_w, units), wide(hcols, part_w), wide(units, part_w),
        low(chips - 1, part_w, 3 * hcols), low(chips - 1, part_w, units), low(chips - 1, hcols, part_w), low(chips - 1, units, part_w),
    ]
    v = lambda *shape: pltpu.VMEM(shape, BF16)
    w = lambda *shape: pltpu.VMEM(shape, F32)
    steps = max(count - 1, 1)
    dma = lambda *shape: pltpu.SemaphoreType.DMA(shape)
    row_tile = max(piece_of(units), piece_of(3 * hcols))
    col_tile = max(piece_of(units), piece_of(hcols))
    most = max(units, width)
    scratch = [
        v(length, width), v(length, units), v(most, most), v(max(most, hcols), max(3 * hcols, length)),
        v(length, 3 * hcols), v(length, hcols), w(length, LANES), w(length, LANES), v(LANES, length),
        v(4, part_w, length), v(2, rows, width),
        v(chips, part_w, 3 * hcols), v(chips, part_w, units), v(chips, hcols, part_w), v(chips, units, part_w),
        v(steps, rows, width), v(steps, rows, width),
        v(2, part_w, row_tile), v(2, col_tile, part_w), w(2, part_w, row_tile), w(2, col_tile, part_w),
        w(2, 32, width), w(1, total), w(1, total), w(chips, 1, total), w(count, 1, 2 * width),
        dma(6), dma(4), dma(2), dma(2), pltpu.SemaphoreType.DMA, dma(2), dma(2), dma(2),
        dma(4, chips), dma(4, chips - 1), dma(4, chips - 1), dma(2), dma(2),
        *[dma(steps) for _ in range(8)], pltpu.SemaphoreType.REGULAR, pltpu.SemaphoreType.REGULAR,
        pltpu.SemaphoreType.DMA, pltpu.SemaphoreType.DMA, dma(chips - 1), dma(chips - 1), dma(steps), dma(steps),
    ]
    return pl.pallas_call(
        functools.partial(backward_kernel, chips, count),
        out_shape=outs,
        in_specs=[anywhere] * 14 + [vmem] * 7,
        out_specs=[anywhere, anywhere, vmem] + [anywhere] * 8,
        scratch_shapes=scratch,
        compiler_params=pltpu.CompilerParams(
            collective_id=1, has_side_effects=True, vmem_limit_bytes=VMEM_LIMIT
        ),
        name="backward_scatter",
    )(*gathered, *saved, x, lse, gain, out_bias, *tables, seg_row, seg_col)


def rotary_tables(segments):
    length = segments.shape[0]
    places = jnp.arange(length, dtype=jnp.int32)
    starts = jnp.zeros((length,), jnp.int32)
    for value in range(4):
        first = jnp.min(jnp.where(segments == value, places, length))
        starts = jnp.where(segments == value, first, starts)
    half_rot = ROT // 2
    lane = jnp.arange(LANES, dtype=jnp.int32) % HEAD_DIM
    frequency = 10000.0 ** (-2.0 * (lane % half_rot).astype(F32) / ROT)
    angles = (places - starts).astype(F32)[:, None] * frequency
    turns = (lane < ROT)[None, :]
    cosine = jnp.where(turns, jnp.cos(angles), 1.0)
    sine = jnp.where(turns, jnp.sin(angles), 0.0)
    return cosine, jnp.where((lane < half_rot)[None, :], -sine, sine)


def on_device(
    ndp, count,
    block_input, segment_ids, out_cotangent, norm_gain, norm_bias, query_weight, key_weight, value_weight,
    query_bias, key_bias, value_bias, out_weight, fc1_weight, fc1_bias, fc2_weight, output_bias,
):
    x = block_input[0]
    cot = out_cotangent[0]
    seg = segment_ids[0]
    width = x.shape[1]
    tables = rotary_tables(seg)
    wqkv = jnp.concatenate([query_weight, key_weight, value_weight], axis=1)
    bqkv = jnp.concatenate([query_bias, key_bias, value_bias])[None, :]
    key_seg = jnp.where(seg == 0, -1, seg)
    gain = norm_gain[None, :]
    (gqkv, gf1, go, gf2, gcot, hid_t, q, k, v, att_t, lse, act_t, dgelu, part) = run_forward(
        ndp, count, x, gain, norm_bias[None, :], wqkv, fc1_weight, out_weight, fc2_weight, cot,
        bqkv, fc1_bias[None, :], tables, seg[:, None], key_seg[None, :],
    )
    (block_output, input_grad, vec, own_qkv, own_f1, own_o, own_f2, land_qkv, land_f1, land_o, land_f2) = run_backward(
        ndp, count, (gqkv, gf1, go, gf2, gcot, hid_t), (q, k, v, att_t, act_t, dgelu, part), x, lse,
        gain, output_bias[None, :], tables, seg[None, :], key_seg[:, None],
    )
    hcols, units = out_weight.shape[0], fc2_weight.shape[0]

    def summed(own, landed):
        for n in range(landed.shape[0]):
            own = own + landed[n].astype(F32)
        return own

    def third(i):
        cols = slice(i * hcols, (i + 1) * hcols)
        return summed(own_qkv[:, cols], land_qkv[:, :, cols])

    sizes = (hcols, hcols, hcols, units, width, width, width)
    pieces, at = [], 0
    for size in sizes:
        pieces.append(vec[0, at : at + size])
        at += size
    qb, kb, vb, f1b, ob, gain_grad, beta_grad = pieces
    return (
        block_output[None], input_grad[None], gain_grad, beta_grad,
        third(0), third(1), third(2), qb, kb, vb,
        summed(own_o, land_o), summed(own_f1, land_f1), f1b, summed(own_f2, land_f2), ob,
    )


def solution(mesh):
    tokens, vector, split = P("dp", "branch", None), P(), P("branch")
    rows_first, cols_first = P("dp", "branch"), P("branch", "dp")
    in_specs = (
        tokens, P("dp", None), tokens, vector, vector, rows_first, rows_first, rows_first,
        split, split, split, cols_first, rows_first, split, cols_first, vector,
    )
    out_specs = (
        tokens, tokens, vector, vector, rows_first, rows_first, rows_first, split, split, split,
        cols_first, rows_first, split, cols_first, vector,
    )
    return jax.shard_map(
        functools.partial(on_device, mesh.shape["dp"], mesh.shape["branch"]),
        mesh=mesh, in_specs=in_specs, out_specs=out_specs, check_vma=False,
    )
```

```python
import functools

import jax
import jax.numpy as jnp
from jax import lax
from jax.experimental import pallas as pl
from jax.experimental.pallas import tpu as pltpu
from jax.sharding import PartitionSpec as P

HEAD_DIM = 64
ROT = 32
EPSILON = 1e-05
NEGATIVE = -1e30
LANES = 128
TILE = 512
QBLOCK = 256
MESH = pl.DeviceIdType.MESH
BF16 = jnp.bfloat16
F32 = jnp.float32
GELU_C = 0.7978845608028654
GELU_A = 0.044715
VMEM_LIMIT = 60 * 1024 * 1024 + 512 * 1024


def flip(index, bits):
    out = index
    bit = 1
    while bit <= bits:
        if bits & bit:
            out = out + bit * (1 - 2 * lax.rem(lax.div(index, bit), 2))
        bit *= 2
    return out


def dot_nn(left, right):
    return jnp.dot(left, right, preferred_element_type=F32)


def dot_nt(left, right):
    return lax.dot_general(left, right, (((1,), (1,)), ((), ())), preferred_element_type=F32)


def tile_of(extent, most=TILE):
    return min(most, extent)


def aligned(index, step):
    return pl.ds(pl.multiple_of(index * step, step), step)


class Chain:
    def __init__(self, own_src, buf, rows, count, sems, dp):
        self.own_src, self.buf, self.rows, self.count = own_src, buf, rows, count
        self.sems, self.dp = sems, dp
        self.z = lax.axis_index("branch")

    def block(self, slot):
        return self.buf.at[aligned(slot, self.rows), :]

    def copy(self, up, step, slot, src=None):
        send, recv = self.sems[0 if up else 2], self.sems[1 if up else 3]
        return pltpu.make_async_remote_copy(
            src_ref=self.block(slot) if src is None else src,
            dst_ref=self.block(slot),
            send_sem=send.at[step],
            recv_sem=recv.at[step],
            device_id=(self.dp, self.z + 1 if up else self.z - 1),
            device_id_type=MESH,
        )

    def sends(self, up, step):
        z, last = self.z, self.count - 1
        if up:
            return jnp.logical_and(z >= step, z < last)
        return jnp.logical_and(z + step <= last, z > 0)

    def sent_slot(self, up, step):
        return self.z - step if up else self.z + step

    def start(self):
        for up in (False, True):

            @pl.when(self.sends(up, 0))
            def _(up=up):
                self.copy(up, 0, self.z, self.own_src).start()

    def pump(self, step):
        for up in (False, True):

            @pl.when(self.sends(up, step))
            def _(up=up):
                slot = self.sent_slot(up, step)
                self.copy(up, step - 1, slot).wait_recv()
                self.copy(up, step, slot).start()

    def by_distance(self, first, end, work):
        def visit(i, _):
            far = lax.div(i + 1, 2)
            above = lax.rem(i, 2) == 0
            slot = self.z + jnp.where(above, far, -far)

            @pl.when(jnp.logical_and(slot >= 0, slot <= self.count - 1))
            def _():
                for up in (False, True):
                    mine = jnp.logical_and(far > 0, above if not up else jnp.logical_not(above))

                    @pl.when(jnp.logical_and(mine, jnp.logical_not(self.sends(up, far))))
                    def _(up=up):
                        self.copy(up, far - 1, slot).wait_recv()

                work(slot)

            return 0

        lax.fori_loop(first, end, visit, 0)

    def finish(self):
        for step in range(self.count - 1):
            for up in (False, True):

                @pl.when(self.sends(up, step))
                def _(up=up, step=step):
                    self.copy(up, step, self.sent_slot(up, step), self.own_src if step == 0 else None).wait_send()


class Gather:
    def __init__(self, index, shard, full, by_rows, chips, sems):
        self.index, self.shard, self.full = index, shard, full
        self.by_rows, self.chips = by_rows, chips
        self.send, self.recv, self.relay_send, self.relay_recv, self.pair_send, self.pair_recv, self.own = sems
        dp = lax.axis_index("dp")
        self.z = lax.axis_index("branch")
        self.core = lax.rem(dp, 2)
        self.chip = lax.div(dp, 2)
        self.width = shard.shape[0 if by_rows else 1]
        self.relayed = chips == 4
        self.direct = (1, 2) if self.relayed else tuple(range(1, chips))

    def slot(self, dp):
        part = aligned(dp, self.width)
        return self.full.at[part, :] if self.by_rows else self.full.at[:, part]

    def half(self, dp, which):
        if self.by_rows:
            return self.full.at[aligned(2 * dp + which, self.width // 2), :]
        rows = self.shard.shape[0] // 2
        return self.full.at[pl.ds(which * rows, rows), aligned(dp, self.width)]

    def at(self, r, core):
        return flip(self.chip, r) * 2 + core

    def to_chip(self, r, landing):
        return pltpu.make_async_remote_copy(
            src_ref=self.shard,
            dst_ref=self.slot(landing),
            send_sem=self.send.at[self.index, r - 1],
            recv_sem=self.recv.at[self.index, r - 1],
            device_id=(self.at(r, self.core), self.z),
            device_id_type=MESH,
        )

    def relay(self, which, owner):
        return pltpu.make_async_remote_copy(
            src_ref=self.half(owner, which),
            dst_ref=self.half(owner, which),
            send_sem=self.relay_send.at[self.index, which],
            recv_sem=self.relay_recv.at[self.index, which],
            device_id=(self.at(2 - which, self.core), self.z),
            device_id_type=MESH,
        )

    def to_pair(self, r, landing):
        return pltpu.make_async_remote_copy(
            src_ref=self.shard if r == 0 else self.slot(self.at(r, self.core)),
            dst_ref=self.slot(landing),
            send_sem=self.pair_send.at[self.index, r],
            recv_sem=self.pair_recv.at[self.index, r],
            device_id=(self.chip * 2 + 1 - self.core, self.z),
            device_id_type=MESH,
        )

    def fetch(self):
        return pltpu.make_async_copy(self.shard, self.slot(self.at(0, self.core)), self.own.at[self.index])

    def start(self):
        for r in self.direct:
            self.to_chip(r, self.at(0, self.core)).start()

    def start_pair(self):
        self.to_pair(0, self.at(0, self.core)).start()
        self.fetch().start()

    def land(self):
        for r in self.direct:
            owner = self.at(r, self.core)
            self.to_chip(r, owner).wait_recv()
            if self.relayed:
                self.relay(r - 1, owner).start()
            self.to_pair(r, owner).start()

    def land_last(self):
        if self.relayed:
            owner = self.at(3, self.core)
            for which in range(2):
                self.relay(which, owner).wait_recv()
            self.to_pair(3, owner).start()

    def arrive(self):
        self.fetch().wait()
        for r in range(self.chips):
            self.to_pair(r, self.at(r, 1 - self.core)).wait_recv()

    def finish(self):
        for r in self.direct:
            self.to_chip(r, self.at(0, self.core)).wait_send()
            if self.relayed:
                self.relay(r - 1, self.at(r, self.core)).wait_send()
        for r in range(self.chips):
            self.to_pair(r, self.at(r, self.core)).wait_send()


def greet(chips, count):
    dp, z = lax.axis_index("dp"), lax.axis_index("branch")
    core, chip = lax.rem(dp, 2), lax.div(dp, 2)
    barrier = pltpu.get_barrier_semaphore()
    for r in range(1, chips):
        pl.semaphore_signal(barrier, inc=1, device_id=(flip(chip, r) * 2 + core, z), device_id_type=MESH)
    pl.semaphore_signal(barrier, inc=1, device_id=(chip * 2 + 1 - core, z), device_id_type=MESH)
    for shift in range(1, count):
        pl.semaphore_signal(barrier, inc=1, device_id=(dp, lax.rem(z + shift, count)), device_id_type=MESH)
    pl.semaphore_wait(barrier, chips + count - 1)


def swapped(y):
    lane = lax.rem(lax.broadcasted_iota(jnp.int32, y.shape, 1), HEAD_DIM)
    return jnp.where(lane < ROT // 2, pltpu.roll(y, LANES - ROT // 2, 1), pltpu.roll(y, ROT // 2, 1))


def forward_kernel(
    chips, count,
    x, gain, beta, bqkv, bf1, seg_row, frequency, wq, wk, wv, wf1, wo, wf2, cot,
    gqkv, gf1, gcot, hid_t, qkv_out, att_t_out, lse_out, act_t, pre_out, part_out, att_grad_out, table_c, table_s, seg_col, sums,
    hid, vqkv, vf1, vf2, vo, qkv, att, att_t, lse, act, dg, part, stage, g_rows, att_grad, tab_c, tab_s, segs,
    w_send, w_recv, r_send, r_recv, p_send, p_recv, own_sem,
    h_us, h_ur, h_ds, h_dr, c_us, c_ur, c_ds, c_dr, cot_sem, save_sem, st_sem,
):
    z = lax.axis_index("branch")
    dp = lax.axis_index("dp")
    rows, width = x.shape
    length = rows * count
    hcols = wo.shape[0]
    units = wf2.shape[0]
    sems = (w_send, w_recv, r_send, r_recv, p_send, p_recv, own_sem)
    g_qkv = [
        Gather(n, w, vqkv.at[:, n * hcols : (n + 1) * hcols], True, chips, sems) for n, w in enumerate((wq, wk, wv))
    ]
    g_f1 = Gather(3, wf1, vf1, True, chips, sems)
    g_o = Gather(4, wo, vo, False, chips, sems)
    g_f2 = Gather(5, wf2, vf2, False, chips, sems)
    h_chain = Chain(hid.at[aligned(z, rows), :], hid, rows, count, (h_us, h_ur, h_ds, h_dr), dp)
    c_chain = Chain(cot, gcot, rows, count, (c_us, c_ur, c_ds, c_dr), dp)
    saves = []

    def save(src, dst):
        c = pltpu.make_async_copy(src, dst, save_sem.at[len(saves)])
        c.start()
        saves.append(c)

    greet(chips, count)
    for g in (*g_qkv, g_f1):
        g.start()
    for g in (*g_qkv, g_f1, g_o, g_f2):
        g.start_pair()
    own_cot = g_rows.at[0:rows, :]
    fetch_cot = pltpu.make_async_copy(cot, own_cot, cot_sem.at[0])
    fetch_cot.start()

    step_rows = 32

    def norm(i, _):
        part_rows = aligned(i, step_rows)
        inputs = x[part_rows, :].astype(F32)
        center = inputs - jnp.mean(inputs, axis=-1, keepdims=True)
        inverse = lax.rsqrt(jnp.mean(center * center, axis=-1, keepdims=True) + EPSILON)
        where = pl.ds(pl.multiple_of(z * rows + i * step_rows, step_rows), step_rows)
        hid[where, :] = (center * inverse * gain[...] + beta[...]).astype(BF16)
        return 0

    lax.fori_loop(0, rows // step_rows, norm, 0)
    h_chain.start()
    fetch_cot.wait()
    save(own_cot, gcot.at[aligned(z, rows), :])

    row_segs = seg_row[...].astype(F32)
    places = lax.broadcasted_iota(jnp.int32, (1, length), 1).astype(F32)
    firsts = [
        jnp.min(jnp.where(row_segs == float(value), places, float(length)), axis=1, keepdims=True)
        for value in range(4)
    ]
    for c in range(length // LANES):
        here = slice(c * LANES, (c + 1) * LANES)
        seg = jnp.broadcast_to(row_segs[:, here], (LANES, LANES)).T
        segs[here, :] = seg
        start = jnp.zeros((LANES, LANES), F32)
        for value in range(4):
            start = jnp.where(seg == float(value), firsts[value], start)
        place = (lax.broadcasted_iota(jnp.int32, (LANES, LANES), 0) + c * LANES).astype(F32)
        angle = (place - start) * frequency[...]
        lane = lax.rem(lax.broadcasted_iota(jnp.int32, (LANES, LANES), 1), HEAD_DIM)
        sine = jnp.where(lane < ROT, jnp.sin(angle), 0.0)
        tab_c[here, :] = jnp.where(lane < ROT, jnp.cos(angle), 1.0)
        tab_s[here, :] = jnp.where(lane < ROT // 2, -sine, sine)
    key_row = jnp.where(row_segs == 0.0, -1.0, row_segs)
    save(tab_c, table_c)
    save(tab_s, table_s)
    save(segs, seg_col)

    for g in g_qkv:
        g.land()
    for g in (g_o, g_f2):
        g.start()
    if count > 2:
        h_chain.pump(1)
    g_f1.land()
    for s in range(2, count - 1):
        h_chain.pump(s)
    c_chain.start()
    for g in g_qkv:
        g.land_last()
    for g in g_qkv:
        g.arrive()
    save(vqkv, gqkv)

    ht, wt = tile_of(hcols), tile_of(width)

    def turn_copy(slot, j, cols_i):
        return pltpu.make_async_copy(
            stage.at[slot, pl.ds(0, wt), pl.ds(0, rows)], hid_t.at[cols_i, aligned(j, rows)], st_sem.at[slot]
        )

    def project(j):
        rows_j = aligned(j, rows)
        for which in range(3):
            for c in range(hcols // ht):
                at = which * hcols + c * ht
                y = dot_nn(hid[rows_j, :], vqkv[:, at : at + ht]) + bqkv[:, at : at + ht]
                for piece in range(ht // LANES):
                    part_y = y[:, piece * LANES : (piece + 1) * LANES]
                    if which < 2:
                        part_y = part_y * tab_c[rows_j, :] + swapped(part_y) * tab_s[rows_j, :]
                    low = part_y.astype(BF16)
                    if which == 0:
                        low = low * BF16(HEAD_DIM**-0.5)
                    qkv[rows_j, at + piece * LANES : at + (piece + 1) * LANES] = low

        def turn(i, _):
            cols_i, slot = aligned(i, wt), lax.rem(i, 2)

            @pl.when(i >= 2)
            def _():
                turn_copy(slot, j, cols_i).wait()

            stage[slot, 0:wt, 0:rows] = hid[rows_j, cols_i].T
            turn_copy(slot, j, cols_i).start()
            return 0

        n_turn = width // wt
        lax.fori_loop(0, n_turn, turn, 0)
        for i in range(max(n_turn - 2, 0), n_turn):
            turn_copy(i % 2, j, pl.ds(0, wt)).wait()

    h_chain.by_distance(0, 2 * count - 3, project)
    g_o.land()
    h_chain.by_distance(2 * count - 3, 2 * count - 1, project)
    save(qkv, qkv_out)
    g_f2.land()
    if count > 2:
        c_chain.pump(1)

    qb = tile_of(length, QBLOCK)
    pairs = hcols // LANES

    def attend(pair, _):
        cols = aligned(pair, LANES)
        k_cols, v_cols = aligned(pairs + pair, LANES), aligned(2 * pairs + pair, LANES)
        lane = lax.broadcasted_iota(jnp.int32, (1, LANES), 1)
        for b in range(length // qb):
            here = slice(b * qb, (b + 1) * qb)
            before = b * qb
            q2 = qkv[here, cols]
            seg_q = segs[here, 0:1]
            ki = lax.broadcasted_iota(jnp.int32, (qb, qb), 1)
            qi = lax.broadcasted_iota(jnp.int32, (qb, qb), 0)
            seen_here = jnp.logical_or(jnp.logical_and(seg_q == key_row[:, here], ki <= qi), ki == qi)
            out = jnp.zeros((qb, LANES), F32)
            stat = jnp.zeros((qb, LANES), F32)
            for h in range(2):
                mine = (lane // HEAD_DIM) == h
                qh = jnp.where(mine, q2, BF16(0))
                s_here = jnp.where(seen_here, dot_nt(qh, qkv[here, k_cols]), NEGATIVE)
                top = jnp.max(s_here, axis=-1, keepdims=True)
                if before:
                    s_before = jnp.where(
                        seg_q == key_row[:, :before], dot_nt(qh, qkv[:before, k_cols]), NEGATIVE
                    )
                    top = jnp.maximum(top, jnp.max(s_before, axis=-1, keepdims=True))
                e_here = jnp.exp(s_here - top)
                total = jnp.sum(e_here, axis=-1, keepdims=True)
                if before:
                    e_before = jnp.exp(s_before - top)
                    total = total + jnp.sum(e_before, axis=-1, keepdims=True)
                share = 1.0 / total
                o = dot_nn((e_here * share).astype(BF16), jnp.where(mine, qkv[here, v_cols], BF16(0)))
                if before:
                    o = o + dot_nn(
                        (e_before * share).astype(BF16), jnp.where(mine, qkv[:before, v_cols], BF16(0))
                    )
                out = out + o
                stat = jnp.where(mine, top + jnp.log(total), stat)
            att[here, cols] = out.astype(BF16)
            att_t[cols, here] = out.T.astype(BF16)
            turned = stat.T
            lse[pl.ds(2 * pair, 1), here] = turned[0:1, :]
            lse[pl.ds(2 * pair + 1, 1), here] = turned[HEAD_DIM : HEAD_DIM + 1, :]
        return 0

    half_pairs = pairs // 2
    lax.fori_loop(0, half_pairs, attend, 0)
    for s in range(2, count - 1):
        c_chain.pump(s)
    lax.fori_loop(half_pairs, pairs - 1, attend, 0)
    g_f1.land_last()
    lax.fori_loop(pairs - 1, pairs, attend, 0)
    save(att_t, att_t_out)
    save(lse, lse_out)
    g_f1.arrive()
    save(vf1, gf1)

    mt, ft = tile_of(length), tile_of(units)
    per_row = units // ft
    n_tiles = (length // mt) * per_row

    def staged(slot, rows_i, cols_i):
        return pltpu.make_async_copy(stage.at[slot, pl.ds(0, ft), :], act_t.at[cols_i, rows_i], st_sem.at[slot])

    def unit(i, _):
        rows_i, cols_i = aligned(lax.div(i, per_row), mt), aligned(lax.rem(i, per_row), ft)
        slot = lax.rem(i, 2)

        @pl.when(i >= 2)
        def _():
            staged(slot, rows_i, cols_i).wait()

        y = dot_nn(hid[rows_i, :], vf1[:, cols_i]) + bf1[:, cols_i]
        square = y * y
        t = jnp.tanh(GELU_C * (y + GELU_A * (y * square)))
        half = 0.5 * (1.0 + t)
        low = (y * half).astype(BF16)
        act[rows_i, cols_i] = low
        stage[slot, 0:ft, :] = low.T
        dg[rows_i, cols_i] = (
            half + 0.5 * y * (1.0 - t * t) * (GELU_C * (1.0 + 3.0 * GELU_A * square))
        ).astype(BF16)
        staged(slot, rows_i, cols_i).start()
        return 0

    half_tiles = n_tiles // 2
    lax.fori_loop(0, half_tiles, unit, 0)
    for g in (g_o, g_f2):
        g.land_last()
    lax.fori_loop(half_tiles, n_tiles, unit, 0)
    for i in range(max(n_tiles - 2, 0), n_tiles):
        staged(i % 2, pl.ds(0, mt), pl.ds(0, ft)).wait()
    for g in (g_o, g_f2):
        g.arrive()

    def output(i, _):
        rows_i, cols_i = aligned(lax.div(i, width // wt), mt), aligned(lax.rem(i, width // wt), wt)
        part[rows_i, cols_i] = (
            dot_nn(act[rows_i, :], vf2[:, cols_i]) + dot_nn(att[rows_i, :], vo[:, cols_i])
        ).astype(BF16)
        return 0

    lax.fori_loop(0, (length // mt) * (width // wt), output, 0)
    save(part, part_out)
    saves[0].wait()

    sums[...] = jnp.zeros_like(sums)

    def unit_back(j):
        rows_j = aligned(j, rows)
        fetch = pltpu.make_async_copy(gcot.at[rows_j, :], g_rows, cot_sem.at[0])
        fetch.start()
        fetch.wait()

        def body(i, _):
            cols_i = aligned(i, ft)
            low = (dot_nt(g_rows[...], vf2[cols_i, :]) * dg[rows_j, cols_i].astype(F32)).astype(BF16)
            dg[rows_j, cols_i] = low
            sums[:, cols_i] += jnp.sum(low.astype(F32), axis=0, keepdims=True)
            return 0

        lax.fori_loop(0, per_row, body, 0)
        att_grad[rows_j, :] = dot_nt(g_rows[...], vo[...]).astype(BF16)
        sums[:, units : units + width] += jnp.sum(g_rows[...].astype(F32), axis=0, keepdims=True)

    c_chain.by_distance(0, 2 * count - 1, unit_back)
    save(dg, pre_out)
    save(att_grad, att_grad_out)
    for g in (*g_qkv, g_f1, g_o, g_f2):
        g.finish()
    h_chain.finish()
    c_chain.finish()
    for c in saves[1:]:
        c.wait()


def run_forward(ndp, count, x, gain, beta, bqkv, bf1, seg_row, frequency, wq, wk, wv, wf1, wo, wf2, cot):
    chips = ndp // 2
    rows, width = x.shape
    length = rows * count
    hcols, units = wo.shape[0], wf2.shape[0]
    heads = hcols // HEAD_DIM
    mt, ft, wt = tile_of(length), tile_of(units), tile_of(width)
    anywhere = pl.BlockSpec(memory_space=pl.ANY)
    vmem = pl.BlockSpec(memory_space=pltpu.VMEM)
    low = lambda *shape: jax.ShapeDtypeStruct(shape, BF16)
    wide = lambda *shape: jax.ShapeDtypeStruct(shape, F32)
    outs = [
        low(width, 3 * hcols), low(width, units), low(length, width), low(width, length), low(length, 3 * hcols),
        low(hcols, length), wide(heads, length), low(units, length), low(length, units), low(length, width), low(length, hcols),
        wide(length, LANES), wide(length, LANES), wide(length, LANES), wide(1, units + width),
    ]
    v = lambda *shape: pltpu.VMEM(shape, BF16)
    w = lambda *shape: pltpu.VMEM(shape, F32)
    steps = max(count - 1, 1)
    dma = lambda *shape: pltpu.SemaphoreType.DMA(shape)
    scratch = [
        v(length, width), v(width, 3 * hcols), v(width, units), v(units, width), v(hcols, width),
        v(length, 3 * hcols), v(length, hcols), v(hcols, length), w(heads, length), v(length, units), v(length, units),
        v(length, width), v(2, max(ft, wt), mt), v(rows, width), v(length, hcols),
        w(length, LANES), w(length, LANES), w(length, LANES),
        dma(6, chips - 1), dma(6, chips - 1), dma(6, 2), dma(6, 2), dma(6, chips), dma(6, chips), dma(6),
        *[dma(steps) for _ in range(8)], dma(1), dma(16), dma(2),
    ]
    return pl.pallas_call(
        functools.partial(forward_kernel, chips, count),
        out_shape=outs,
        in_specs=[vmem] * 7 + [anywhere] * 7,
        out_specs=[anywhere] * (len(outs) - 1) + [vmem],
        scratch_shapes=scratch,
        compiler_params=pltpu.CompilerParams(
            collective_id=0, has_side_effects=True, vmem_limit_bytes=VMEM_LIMIT
        ),
        name="gather_forward",
    )(x, gain, beta, bqkv, bf1, seg_row, frequency, wq, wk, wv, wf1, wo, wf2, cot)


class Fold:
    def __init__(self, bufs, sems, count, dp):
        self.bufs, self.sems, self.count, self.dp = bufs, sems, count, dp
        self.z = lax.axis_index("branch")

    def place(self, up):
        return self.z if up else self.count - 1 - self.z

    def dest(self, up, step):
        return self.count - 1 - step if up else step

    def hop(self, up, step, src=None):
        buf = self.bufs[0 if up else 1]
        send, recv = self.sems[0 if up else 2], self.sems[1 if up else 3]
        return pltpu.make_async_remote_copy(
            src_ref=buf.at[step] if src is None else src,
            dst_ref=buf.at[step],
            send_sem=send.at[step],
            recv_sem=recv.at[step],
            device_id=(self.dp, self.z + 1 if up else self.z - 1),
            device_id_type=MESH,
        )

    def first(self, up, step, src):
        @pl.when(self.place(up) == 0)
        def _():
            self.hop(up, step, src).start()

    def pump(self, k, own_block, rows):
        for up in (False, True):
            place = self.place(up)

            @pl.when(jnp.logical_and(place >= 1, place <= k))
            def _(up=up, place=place):
                step = k - place
                own = own_block(up, self.dest(up, step))
                self.hop(up, step).wait_recv()
                buf = self.bufs[0 if up else 1]

                def add(i, _):
                    part = aligned(i, 32)
                    buf[step, part, :] = (buf[step, part, :].astype(F32) + own[part, :].astype(F32)).astype(BF16)
                    return 0

                lax.fori_loop(0, rows // 32, add, 0)
                self.hop(up, step).start()

    def last_step(self, up):
        return jnp.clip(self.count - 1 - self.place(up), 0, self.count - 2)

    def arrive(self):
        for up in (False, True):

            @pl.when(self.place(up) >= 1)
            def _(up=up):
                self.hop(up, self.last_step(up)).wait_recv()

    def total(self, own, part):
        out = own
        for up in (False, True):
            got = self.bufs[0 if up else 1][self.last_step(up), part, :].astype(F32)
            out = out + jnp.where(self.place(up) >= 1, got, 0.0)
        return out

    def finish(self):
        for step in range(self.count - 1):
            for up in (False, True):

                @pl.when(self.place(up) + step <= self.count - 2)
                def _(up=up, step=step):
                    self.hop(up, step).wait_send()


class Scatter:
    def __init__(self, index, block, tile, rows_first, slots, landing, own_out, stage, wide, chips, sems):
        self.index, self.block, self.tile, self.rows_first = index, block, tile, rows_first
        self.slots, self.landing, self.own_out, self.stage, self.wide = slots, landing, own_out, stage, wide
        self.chips = chips
        self.st_sem, self.pair_recv, self.send, self.recv, self.wide_sem = sems
        dp = lax.axis_index("dp")
        self.z = lax.axis_index("branch")
        self.core, self.chip = lax.rem(dp, 2), lax.div(dp, 2)
        self.tiles = slots.shape[2 if rows_first else 1] // tile
        self.height = slots.shape[1] if rows_first else tile
        self.breadth = tile if rows_first else slots.shape[2]
        self.order = [*range(1, chips), 0]

    def part(self, ref, i):
        at = aligned(i, self.tile)
        return ref.at[:, at] if self.rows_first else ref.at[at, :]

    def view(self, ref, slot):
        return ref.at[slot, pl.ds(0, self.height), pl.ds(0, self.breadth)]

    def to_pair(self, r, i, slot):
        return pltpu.make_async_remote_copy(
            src_ref=self.view(self.stage, slot),
            dst_ref=self.part(self.slots.at[r], i),
            send_sem=self.st_sem.at[slot],
            recv_sem=self.pair_recv.at[self.index, r],
            device_id=(self.chip * 2 + 1 - self.core, self.z),
            device_id_type=MESH,
        )

    def from_pair(self, r):
        return pltpu.make_async_remote_copy(
            src_ref=self.slots.at[r],
            dst_ref=self.slots.at[r],
            send_sem=self.st_sem.at[0],
            recv_sem=self.pair_recv.at[self.index, r],
            device_id=(self.chip * 2 + 1 - self.core, self.z),
            device_id_type=MESH,
        )

    def to_owner(self, r):
        return pltpu.make_async_remote_copy(
            src_ref=self.slots.at[r],
            dst_ref=self.landing.at[r - 1],
            send_sem=self.send.at[self.index, r - 1],
            recv_sem=self.recv.at[self.index, r - 1],
            device_id=(flip(self.chip, r) * 2 + self.core, self.z),
            device_id_type=MESH,
        )

    def to_out(self, i, slot):
        return pltpu.make_async_copy(self.view(self.wide, slot), self.part(self.own_out, i), self.wide_sem.at[slot])

    def partners(self, n):
        r = self.order[n]
        owner = flip(self.chip, r) * 2 + 1 - self.core

        def body(i, _):
            slot = lax.rem(n * self.tiles + i, 2)
            y = self.block(owner, i)
            if n * self.tiles >= 2:
                self.to_pair(r, i, slot).wait_send()
            else:

                @pl.when(n * self.tiles + i >= 2)
                def _():
                    self.to_pair(r, i, slot).wait_send()

            self.stage[slot, 0 : self.height, 0 : self.breadth] = y.astype(BF16)
            self.to_pair(r, i, slot).start()
            return 0

        lax.fori_loop(0, self.tiles, body, 0)

    def own(self, n):
        r = self.order[n]
        owner = flip(self.chip, r) * 2 + self.core
        self.from_pair(r).wait_recv()

        def body(i, _):
            y = self.block(owner, i)
            at = aligned(i, self.tile)
            if self.rows_first:
                y = y + self.slots[r, :, at].astype(F32)
            else:
                y = y + self.slots[r, at, :].astype(F32)
            if r:
                if self.rows_first:
                    self.slots[r, :, at] = y.astype(BF16)
                else:
                    self.slots[r, at, :] = y.astype(BF16)
            else:
                slot = lax.rem(i, 2)

                @pl.when(i >= 2)
                def _():
                    self.to_out(i, slot).wait()

                self.wide[slot, 0 : self.height, 0 : self.breadth] = y
                self.to_out(i, slot).start()
            return 0

        lax.fori_loop(0, self.tiles, body, 0)
        if r:
            self.to_owner(r).start()
        else:
            for i in range(max(self.tiles - 2, 0), self.tiles):
                self.to_out(i, i % 2).wait()

    def run(self, before=lambda n: None):
        for n in range(self.chips):
            before(n)
            self.partners(n)
            if n:
                self.own(n - 1)
        self.own(self.chips - 1)
        total = self.chips * self.tiles
        for i in range(max(total - 2, 0), total):
            self.to_pair(0, 0, i % 2).wait_send()

    def finish(self):
        for r in range(1, self.chips):
            self.to_owner(r).wait_send()
            self.to_owner(r).wait_recv()


def piece_of(extent):
    return next(n for n in (512, 256, 128) if extent % n == 0)


def backward_kernel(
    chips, count,
    gqkv, gf1, gcot, hid_t, qkv_in, att_t, act_t, pre_in, part_in, att_grad_in, x_in,
    lse, gain, out_bias, table_c, table_s, seg_row, seg_col, sums,
    block_out, input_grad, vec_out, own_qkv, own_f1, own_o, own_f2, land_qkv, land_f1, land_o, land_f2,
    g, pre, f1_v, mid, qkv, att_grad, dk_acc, dv_acc, k_t, hid_stage, tmp, s_qkv, s_f1, s_o, s_f2, up_buf, dn_buf,
    st_row, st_col, wide_row, wide_col, ig_stage, vec, vec_pair, vec_chip, vec_z,
    load_sem, hid_sem, tmp_sem, out_sem, ig_sem, st_row_sem, st_col_sem, pair_recv, x_send, x_recv, wide_row_sem, wide_col_sem,
    zo_us, zo_ur, zo_ds, zo_dr, zh_us, zh_ur, zh_ds, zh_dr, free_up, free_dn, v_ps, v_pr, v_cs, v_cr, v_zs, v_zr,
):
    z = lax.axis_index("branch")
    dp = lax.axis_index("dp")
    core, chip = lax.rem(dp, 2), lax.div(dp, 2)
    length, width = g.shape
    rows = length // count
    hcols, units = att_t.shape[0], act_t.shape[0]
    part_w = width // (2 * chips)
    last = count - 1
    wt = tile_of(width)
    act_v, att_v, wqkv_v = mid.at[0:units, 0:length], mid.at[0:hcols, 0:length], mid.at[0:width, 0 : 3 * hcols]

    def load(src, dst, n):
        c = pltpu.make_async_copy(src, dst, load_sem.at[n])
        c.start()
        return c

    load_g = load(gcot, g, 0)
    load_act = load(act_t, act_v, 1)
    load_qkv = load(qkv_in, qkv, 2)
    load_att_grad = load(att_grad_in, att_grad, 3)
    load_pre = load(pre_in, pre, 4)
    load_f1 = load(gf1, f1_v, 5)
    greet(chips, count)

    def rows_of(ref, d):
        return ref.at[aligned(d, rows), :]

    fold_out = Fold((up_buf, dn_buf), (zo_us, zo_ur, zo_ds, zo_dr), count, dp)
    fold_hid = Fold((up_buf, dn_buf), (zh_us, zh_ur, zh_ds, zh_dr), count, dp)
    for s in range(count - 1):
        fold_out.first(True, s, rows_of(part_in, last - s))
        fold_out.first(False, s, rows_of(part_in, s))

    def fetched(up, d):
        n = 0 if up else 1
        c = pltpu.make_async_copy(rows_of(part_in, d), tmp.at[n], tmp_sem.at[n])
        c.start()
        c.wait()
        return tmp.at[n]

    sems_row = (st_row_sem, pair_recv, x_send, x_recv, wide_row_sem)
    sems_col = (st_col_sem, pair_recv, x_send, x_recv, wide_col_sem)
    tile_f2, tile_o = piece_of(units), piece_of(hcols)
    tile_f1, tile_qkv = piece_of(units), piece_of(3 * hcols)

    def f2_block(owner, i):
        return dot_nn(act_v[aligned(i, tile_f2), :], g[:, aligned(owner, part_w)])

    def o_block(owner, i):
        return dot_nn(att_v[aligned(i, tile_o), :], g[:, aligned(owner, part_w)])

    def hid_copy(n, which, r, slot_core):
        owner = flip(chip, r) * 2 + slot_core
        return pltpu.make_async_copy(
            hid_t.at[aligned(owner, part_w), :], hid_stage.at[2 * which + n % 2], hid_sem.at[2 * which + n % 2]
        )

    state = {}

    def f1_block(owner, i):
        return dot_nn(hid_stage[state["at"]], pre[:, aligned(i, tile_f1)])

    def qkv_block(owner, i):
        return dot_nn(hid_stage[state["at"]], qkv[:, aligned(i, tile_qkv)])

    def run_rows(scatter):
        order = scatter.order
        hid_copy(0, 0, order[0], 1 - core).start()
        hid_copy(0, 1, order[0], core).start()
        for n in range(chips):
            if n + 1 < chips:
                hid_copy(n + 1, 0, order[n + 1], 1 - core).start()
            hid_copy(n, 0, order[n], 1 - core).wait()
            state["at"] = n % 2
            scatter.partners(n)
            if n:
                hid_copy(n, 1, order[n], core).start()
                hid_copy(n - 1, 1, order[n - 1], core).wait()
                state["at"] = 2 + (n - 1) % 2
                scatter.own(n - 1)
        hid_copy(chips - 1, 1, order[chips - 1], core).wait()
        state["at"] = 2 + (chips - 1) % 2
        scatter.own(chips - 1)
        total = chips * scatter.tiles
        for i in range(max(total - 2, 0), total):
            scatter.to_pair(0, 0, i % 2).wait_send()

    sc_f2 = Scatter(0, f2_block, tile_f2, False, s_f2, land_f2, own_f2, st_col, wide_col, chips, sems_col)
    sc_f1 = Scatter(1, f1_block, tile_f1, True, s_f1, land_f1, own_f1, st_row, wide_row, chips, sems_row)
    sc_o = Scatter(2, o_block, tile_o, False, s_o, land_o, own_o, st_col, wide_col, chips, sems_col)
    sc_qkv = Scatter(3, qkv_block, tile_qkv, True, s_qkv, land_qkv, own_qkv, st_row, wide_row, chips, sems_row)

    at_f1, at_gain = 3 * hcols, 3 * hcols + units + width
    at_beta = at_gain + width
    vec[...] = jnp.zeros_like(vec)
    vec[:, at_f1:at_gain] = sums[...]

    load_g.wait()
    load_act.wait()
    sc_f2.run()
    load_att = load(att_t, att_v, 1)
    load_qkv.wait()
    load_att_grad.wait()
    load_att.wait()
    sc_o.run()
    load_wqkv = load(gqkv, wqkv_v, 1)
    if count > 2:
        fold_out.pump(1, fetched, rows)

    qb = tile_of(length, QBLOCK)
    pairs = hcols // LANES
    row_segs = seg_row[...].astype(F32)

    def key_of(lo, hi):
        seg = seg_col[lo:hi, 0:1]
        return jnp.where(seg == 0.0, -1.0, seg)

    def turn_back(y, at):
        return y * table_c[at, :] - swapped(y) * table_s[at, :]

    def attend(pair, _):
        q_cols = aligned(pair, LANES)
        k_cols, v_cols = aligned(pairs + pair, LANES), aligned(2 * pairs + pair, LANES)
        lane = lax.broadcasted_iota(jnp.int32, (1, LANES), 1)
        dk_acc[...] = jnp.zeros_like(dk_acc)
        dv_acc[...] = jnp.zeros_like(dv_acc)
        k_t[...] = qkv[:, k_cols].T
        for b in range(length // qb):
            here, reach = slice(b * qb, (b + 1) * qb), (b + 1) * qb
            before = b * qb
            q2, g2 = qkv[here, q_cols], att_grad[here, q_cols]
            ki = lax.broadcasted_iota(jnp.int32, (qb, qb), 0)
            qi = lax.broadcasted_iota(jnp.int32, (qb, qb), 1)
            seen_here = jnp.logical_or(
                jnp.logical_and(key_of(before, reach) == row_segs[:, here], ki <= qi), ki == qi
            )
            dq_t = []
            for h in range(2):
                mine = (lane // HEAD_DIM) == h
                qh, gh = jnp.where(mine, q2, BF16(0)), jnp.where(mine, g2, BF16(0))
                stat = lse[pl.ds(2 * pair + h, 1), here]
                spans = ([(0, before)] if before else []) + [(before, reach)]
                probs, grads = [], []
                delta = jnp.zeros((1, qb), F32)
                for lo, hi in spans:
                    seen = seen_here if lo == before else key_of(lo, hi) == row_segs[:, here]
                    p = jnp.exp(jnp.where(seen, dot_nt(qkv[lo:hi, k_cols], qh), NEGATIVE) - stat)
                    pg = dot_nt(qkv[lo:hi, v_cols], gh)
                    delta = delta + jnp.sum(p * pg, axis=0, keepdims=True)
                    probs.append(p)
                    grads.append(pg)
                acc = jnp.zeros((HEAD_DIM, qb), F32)
                for (lo, hi), p, pg in zip(spans, probs, grads):
                    sg = (p * (pg - delta)).astype(BF16)
                    dv_acc[lo:hi, :] += dot_nn(p.astype(BF16), gh)
                    dk_acc[lo:hi, :] += dot_nn(sg, qh)
                    acc = acc + dot_nn(k_t[h * HEAD_DIM : (h + 1) * HEAD_DIM, lo:hi], sg)
                dq_t.append(acc)
            dq = jnp.concatenate(dq_t, axis=0).T * HEAD_DIM**-0.5
            qkv[here, q_cols] = turn_back(dq, here).astype(BF16)
        for b in range(length // qb):
            here = slice(b * qb, (b + 1) * qb)
            qkv[here, k_cols] = turn_back(dk_acc[here, :], here).astype(BF16)
            qkv[here, v_cols] = dv_acc[here, :].astype(BF16)
        for cols in (q_cols, k_cols, v_cols):
            vec[:, cols] = jnp.sum(qkv[:, cols].astype(F32), axis=0, keepdims=True)
        return 0

    half_pairs = pairs // 2
    lax.fori_loop(0, half_pairs, attend, 0)
    for k in range(2, count - 1):
        fold_out.pump(k, fetched, rows)
    lax.fori_loop(half_pairs, pairs, attend, 0)
    load_pre.wait()
    load_f1.wait()
    load_wqkv.wait()

    def hidden_back(d):
        here = pl.ds(d * rows, rows)

        def body(i, _):
            cols_i = aligned(i, wt)
            g[here, cols_i] = (
                dot_nt(pre[here, :], f1_v[cols_i, :]) + dot_nt(qkv[here, :], wqkv_v[cols_i, :])
            ).astype(BF16)
            return 0

        lax.fori_loop(0, width // wt, body, 0)

    def set_out(d):
        if d > 0:
            fold_hid.first(True, last - d, rows_of(g, d))
        if d < last:
            fold_hid.first(False, d, rows_of(g, d))

    dests = list(dict.fromkeys(d for both in zip(range(last, -1, -1), range(count)) for d in both))
    for d in dests[:2]:
        hidden_back(d)

    fold_out.arrive()
    load_x = pltpu.make_async_copy(x_in, tmp.at[0], tmp_sem.at[0])
    load_x.start()
    load_own = pltpu.make_async_copy(rows_of(part_in, z), tmp.at[1], tmp_sem.at[1])
    load_own.start()
    load_x.wait()
    load_own.wait()

    def finish_output(i, _):
        part = aligned(i, 32)
        y = fold_out.total(tmp[1, part, :].astype(F32), part)
        tmp[1, part, :] = (tmp[0, part, :].astype(F32) + y + out_bias[...]).astype(BF16)
        return 0

    lax.fori_loop(0, rows // 32, finish_output, 0)
    save_out = pltpu.make_async_copy(tmp.at[1], block_out, out_sem)
    save_out.start()
    fold_out.finish()

    @pl.when(z > 0)
    def _():
        pl.semaphore_signal(free_up, inc=1, device_id=(dp, z - 1), device_id_type=MESH)

    @pl.when(z < last)
    def _():
        pl.semaphore_signal(free_dn, inc=1, device_id=(dp, z + 1), device_id_type=MESH)

    @pl.when(z < last)
    def _():
        pl.semaphore_wait(free_up, 1)

    @pl.when(z > 0)
    def _():
        pl.semaphore_wait(free_dn, 1)

    for d in dests[:2]:
        set_out(d)
    run_rows(sc_f1)
    for d in dests[2:]:
        hidden_back(d)
        set_out(d)
    if count > 2:
        fold_hid.pump(1, lambda up, d: rows_of(g, d), rows)
    save_out.wait()
    load_cot = pltpu.make_async_copy(rows_of(gcot, z), tmp.at[1], tmp_sem.at[1])
    load_cot.start()
    run_rows(sc_qkv)
    for k in range(2, count - 1):
        fold_hid.pump(k, lambda up, d: rows_of(g, d), rows)
    fold_hid.arrive()
    load_cot.wait()

    step_rows = 32

    def ig_copy(i, slot):
        return pltpu.make_async_copy(ig_stage.at[slot], input_grad.at[aligned(i, step_rows), :], ig_sem.at[slot])

    def norm_back(i, _):
        part = aligned(i, step_rows)
        slot = lax.rem(i, 2)
        inputs = tmp[0, part, :].astype(F32)
        center = inputs - jnp.mean(inputs, axis=-1, keepdims=True)
        inverse = lax.rsqrt(jnp.mean(center * center, axis=-1, keepdims=True) + EPSILON)
        normed = center * inverse
        own = g[pl.ds(pl.multiple_of(z * rows + i * step_rows, step_rows), step_rows), :].astype(F32)
        y = fold_hid.total(own, part)
        vec[:, at_gain : at_gain + width] += jnp.sum(y * normed, axis=0, keepdims=True)
        vec[:, at_beta : at_beta + width] += jnp.sum(y, axis=0, keepdims=True)
        scaled = y * gain[...]
        result = tmp[1, part, :].astype(F32) + inverse * (
            scaled
            - jnp.mean(scaled, axis=-1, keepdims=True)
            - normed * jnp.mean(scaled * normed, axis=-1, keepdims=True)
        )

        @pl.when(i >= 2)
        def _():
            ig_copy(i, slot).wait()

        ig_stage[slot] = result
        ig_copy(i, slot).start()
        return 0

    steps = rows // step_rows
    lax.fori_loop(0, steps, norm_back, 0)

    to_pair = pltpu.make_async_remote_copy(
        src_ref=vec, dst_ref=vec_pair, send_sem=v_ps, recv_sem=v_pr,
        device_id=(chip * 2 + 1 - core, z), device_id_type=MESH,
    )
    to_pair.start()
    for i in range(max(steps - 2, 0), steps):
        ig_copy(i, i % 2).wait()
    to_pair.wait()
    vec_chip[chip] = vec[...] + vec_pair[...]

    def chip_copy(r, slot):
        return pltpu.make_async_remote_copy(
            src_ref=vec_chip.at[chip], dst_ref=vec_chip.at[slot], send_sem=v_cs.at[r - 1], recv_sem=v_cr.at[r - 1],
            device_id=(flip(chip, r) * 2 + core, z), device_id_type=MESH,
        )

    for r in range(1, chips):
        chip_copy(r, chip).start()
    for r in range(1, chips):
        chip_copy(r, flip(chip, r)).wait_recv()
    total = vec_chip[0]
    for c in range(1, chips):
        total = total + vec_chip[c]
    vec_out[:, 0:at_gain] = total[:, 0:at_gain]
    vec_z[z] = total[:, at_gain:]

    def z_copy(shift, slot):
        return pltpu.make_async_remote_copy(
            src_ref=vec_z.at[z], dst_ref=vec_z.at[slot], send_sem=v_zs.at[shift - 1], recv_sem=v_zr.at[shift - 1],
            device_id=(dp, lax.rem(z + shift, count)), device_id_type=MESH,
        )

    for shift in range(1, count):
        z_copy(shift, z).start()
    for shift in range(1, count):
        z_copy(shift, lax.rem(z + count - shift, count)).wait_recv()
    total = vec_z[0]
    for n in range(1, count):
        total = total + vec_z[n]
    vec_out[:, at_gain:] = total
    for r in range(1, chips):
        chip_copy(r, chip).wait_send()
    for shift in range(1, count):
        z_copy(shift, z).wait_send()
    fold_hid.finish()
    for s in (sc_f2, sc_f1, sc_o, sc_qkv):
        s.finish()


def run_backward(ndp, count, saved, x, lse, gain, out_bias, table_c, table_s, seg_row, seg_col, sums):
    chips = ndp // 2
    gqkv, gf1, gcot, hid_t, qkv, att_t = saved[:6]
    length, width = gcot.shape
    rows, hcols, units = length // count, att_t.shape[0], gf1.shape[1]
    part_w = width // ndp
    total = 3 * hcols + units + 3 * width
    anywhere = pl.BlockSpec(memory_space=pl.ANY)
    vmem = pl.BlockSpec(memory_space=pltpu.VMEM)
    low = lambda *shape: jax.ShapeDtypeStruct(shape, BF16)
    wide = lambda *shape: jax.ShapeDtypeStruct(shape, F32)
    outs = [
        low(rows, width), wide(rows, width), wide(1, total),
        wide(part_w, 3 * hcols), wide(part_w, units), wide(hcols, part_w), wide(units, part_w),
        low(chips - 1, part_w, 3 * hcols), low(chips - 1, part_w, units), low(chips - 1, hcols, part_w), low(chips - 1, units, part_w),
    ]
    v = lambda *shape: pltpu.VMEM(shape, BF16)
    w = lambda *shape: pltpu.VMEM(shape, F32)
    steps = max(count - 1, 1)
    dma = lambda *shape: pltpu.SemaphoreType.DMA(shape)
    row_tile = max(piece_of(units), piece_of(3 * hcols))
    col_tile = max(piece_of(units), piece_of(hcols))
    scratch = [
        v(length, width), v(length, units), v(width, units), v(max(units, width, hcols), max(3 * hcols, length)),
        v(length, 3 * hcols), v(length, hcols), w(length, LANES), w(length, LANES), v(LANES, length),
        v(4, part_w, length), v(2, rows, width),
        v(chips, part_w, 3 * hcols), v(chips, part_w, units), v(chips, hcols, part_w), v(chips, units, part_w),
        v(steps, rows, width), v(steps, rows, width),
        v(2, part_w, row_tile), v(2, col_tile, part_w), w(2, part_w, row_tile), w(2, col_tile, part_w),
        w(2, 32, width), w(1, total), w(1, total), w(chips, 1, total), w(count, 1, 2 * width),
        dma(6), dma(4), dma(2), pltpu.SemaphoreType.DMA, dma(2), dma(2), dma(2),
        dma(4, chips), dma(4, chips - 1), dma(4, chips - 1), dma(2), dma(2),
        *[dma(steps) for _ in range(8)], pltpu.SemaphoreType.REGULAR, pltpu.SemaphoreType.REGULAR,
        pltpu.SemaphoreType.DMA, pltpu.SemaphoreType.DMA, dma(chips - 1), dma(chips - 1), dma(steps), dma(steps),
    ]
    return pl.pallas_call(
        functools.partial(backward_kernel, chips, count),
        out_shape=outs,
        in_specs=[anywhere] * 11 + [vmem] * 8,
        out_specs=[anywhere, anywhere, vmem] + [anywhere] * 8,
        scratch_shapes=scratch,
        compiler_params=pltpu.CompilerParams(
            collective_id=1, has_side_effects=True, vmem_limit_bytes=VMEM_LIMIT
        ),
        name="backward_scatter",
    )(*saved, x, lse, gain, out_bias, table_c, table_s, seg_row, seg_col, sums)


def on_device(
    ndp, count,
    block_input, segment_ids, out_cotangent, norm_gain, norm_bias, query_weight, key_weight, value_weight,
    query_bias, key_bias, value_bias, out_weight, fc1_weight, fc1_bias, fc2_weight, output_bias,
):
    x = block_input[0]
    cot = out_cotangent[0]
    width = x.shape[1]
    half_rot = ROT // 2
    frequency = 10000.0 ** (-2.0 * (jnp.arange(LANES, dtype=jnp.int32) % half_rot).astype(F32) / ROT)
    bqkv = jnp.concatenate([query_bias, key_bias, value_bias])[None, :]
    gain, seg_row = norm_gain[None, :], segment_ids
    (gqkv, gf1, gcot, hid_t, qkv, att_t, lse, act_t, pre, part, att_grad, table_c, table_s, seg_col, sums) = run_forward(
        ndp, count, x, gain, norm_bias[None, :], bqkv, fc1_bias[None, :], seg_row, frequency[None, :],
        query_weight, key_weight, value_weight, fc1_weight, out_weight, fc2_weight, cot,
    )
    (block_output, input_grad, vec, own_qkv, own_f1, own_o, own_f2, land_qkv, land_f1, land_o, land_f2) = run_backward(
        ndp, count, (gqkv, gf1, gcot, hid_t, qkv, att_t, act_t, pre, part, att_grad), x, lse,
        gain, output_bias[None, :], table_c, table_s, seg_row, seg_col, sums,
    )
    hcols, units = out_weight.shape[0], fc2_weight.shape[0]

    def summed(own, landed):
        for n in range(landed.shape[0]):
            own = own + landed[n].astype(F32)
        return own

    def third(i):
        cols = slice(i * hcols, (i + 1) * hcols)
        return summed(own_qkv[:, cols], land_qkv[:, :, cols])

    sizes = (hcols, hcols, hcols, units, width, width, width)
    pieces, at = [], 0
    for size in sizes:
        pieces.append(vec[0, at : at + size])
        at += size
    qb, kb, vb, f1b, ob, gain_grad, beta_grad = pieces
    return (
        block_output[None], input_grad[None], gain_grad, beta_grad,
        third(0), third(1), third(2), qb, kb, vb,
        summed(own_o, land_o), summed(own_f1, land_f1), f1b, summed(own_f2, land_f2), ob,
    )


def solution(mesh):
    tokens, vector, split = P("dp", "branch", None), P(), P("branch")
    rows_first, cols_first = P("dp", "branch"), P("branch", "dp")
    in_specs = (
        tokens, P("dp", None), tokens, vector, vector, rows_first, rows_first, rows_first,
        split, split, split, cols_first, rows_first, split, cols_first, vector,
    )
    out_specs = (
        tokens, tokens, vector, vector, rows_first, rows_first, rows_first, split, split, split,
        cols_first, rows_first, split, cols_first, vector,
    )
    return jax.shard_map(
        functools.partial(on_device, mesh.shape["dp"], mesh.shape["branch"]),
        mesh=mesh, in_specs=in_specs, out_specs=out_specs, check_vma=False,
    )
```

```python
import functools

import jax
import jax.numpy as jnp
from jax import lax
from jax.experimental import pallas as pl
from jax.experimental.pallas import tpu as pltpu
from jax.sharding import PartitionSpec as P

HEAD_DIM = 64
ROT = 32
EPSILON = 1e-05
NEGATIVE = -1e30
LANES = 128
TILE = 512
QBLOCK = 256
MESH = pl.DeviceIdType.MESH
BF16 = jnp.bfloat16
F32 = jnp.float32
GELU_C = 0.7978845608028654
GELU_A = 0.044715
VMEM_LIMIT = 63 * 1024 * 1024 + 832 * 1024


def flip(index, bits):
    out = index
    bit = 1
    while bit <= bits:
        if bits & bit:
            out = out + bit * (1 - 2 * lax.rem(lax.div(index, bit), 2))
        bit *= 2
    return out


def dot_nn(left, right):
    return jnp.dot(left, right, preferred_element_type=F32)


def dot_nt(left, right):
    return lax.dot_general(left, right, (((1,), (1,)), ((), ())), preferred_element_type=F32)


def tile_of(extent, most=TILE):
    return min(most, extent)


def aligned(index, step):
    return pl.ds(pl.multiple_of(index * step, step), step)


class Chain:
    def __init__(self, own_src, buf, rows, count, sems, dp):
        self.own_src, self.buf, self.rows, self.count = own_src, buf, rows, count
        self.sems, self.dp = sems, dp
        self.z = lax.axis_index("branch")

    def block(self, slot):
        return self.buf.at[aligned(slot, self.rows), :]

    def copy(self, up, step, slot, src=None):
        send, recv = self.sems[0 if up else 2], self.sems[1 if up else 3]
        return pltpu.make_async_remote_copy(
            src_ref=self.block(slot) if src is None else src,
            dst_ref=self.block(slot),
            send_sem=send.at[step],
            recv_sem=recv.at[step],
            device_id=(self.dp, self.z + 1 if up else self.z - 1),
            device_id_type=MESH,
        )

    def sends(self, up, step):
        z, last = self.z, self.count - 1
        if up:
            return jnp.logical_and(z >= step, z < last)
        return jnp.logical_and(z + step <= last, z > 0)

    def sent_slot(self, up, step):
        return self.z - step if up else self.z + step

    def start(self):
        for up in (False, True):

            @pl.when(self.sends(up, 0))
            def _(up=up):
                self.copy(up, 0, self.z, self.own_src).start()

    def pump(self, step):
        for up in (False, True):

            @pl.when(self.sends(up, step))
            def _(up=up):
                slot = self.sent_slot(up, step)
                self.copy(up, step - 1, slot).wait_recv()
                self.copy(up, step, slot).start()

    def by_distance(self, first, end, work):
        def visit(i, _):
            far = lax.div(i + 1, 2)
            above = lax.rem(i, 2) == 0
            slot = self.z + jnp.where(above, far, -far)

            @pl.when(jnp.logical_and(slot >= 0, slot <= self.count - 1))
            def _():
                for up in (False, True):
                    mine = jnp.logical_and(far > 0, above if not up else jnp.logical_not(above))

                    @pl.when(jnp.logical_and(mine, jnp.logical_not(self.sends(up, far))))
                    def _(up=up):
                        self.copy(up, far - 1, slot).wait_recv()

                work(slot)

            return 0

        lax.fori_loop(first, end, visit, 0)

    def finish(self):
        for step in range(self.count - 1):
            for up in (False, True):

                @pl.when(self.sends(up, step))
                def _(up=up, step=step):
                    self.copy(up, step, self.sent_slot(up, step), self.own_src if step == 0 else None).wait_send()


class Gather:
    def __init__(self, index, shard, full, by_rows, chips, sems):
        self.index, self.shard, self.full = index, shard, full
        self.by_rows, self.chips = by_rows, chips
        self.send, self.recv, self.relay_send, self.relay_recv, self.pair_send, self.pair_recv, self.own = sems
        dp = lax.axis_index("dp")
        self.z = lax.axis_index("branch")
        self.core = lax.rem(dp, 2)
        self.chip = lax.div(dp, 2)
        self.width = shard.shape[0 if by_rows else 1]
        self.relayed = chips == 4
        self.direct = (1, 2) if self.relayed else tuple(range(1, chips))

    def slot(self, dp):
        part = aligned(dp, self.width)
        return self.full.at[part, :] if self.by_rows else self.full.at[:, part]

    def half(self, dp, which):
        if self.by_rows:
            return self.full.at[aligned(2 * dp + which, self.width // 2), :]
        rows = self.shard.shape[0] // 2
        return self.full.at[pl.ds(which * rows, rows), aligned(dp, self.width)]

    def at(self, r, core):
        return flip(self.chip, r) * 2 + core

    def to_chip(self, r, landing):
        return pltpu.make_async_remote_copy(
            src_ref=self.shard,
            dst_ref=self.slot(landing),
            send_sem=self.send.at[self.index, r - 1],
            recv_sem=self.recv.at[self.index, r - 1],
            device_id=(self.at(r, self.core), self.z),
            device_id_type=MESH,
        )

    def relay(self, which, owner):
        return pltpu.make_async_remote_copy(
            src_ref=self.half(owner, which),
            dst_ref=self.half(owner, which),
            send_sem=self.relay_send.at[self.index, which],
            recv_sem=self.relay_recv.at[self.index, which],
            device_id=(self.at(2 - which, self.core), self.z),
            device_id_type=MESH,
        )

    def to_pair(self, r, landing):
        return pltpu.make_async_remote_copy(
            src_ref=self.shard if r == 0 else self.slot(self.at(r, self.core)),
            dst_ref=self.slot(landing),
            send_sem=self.pair_send.at[self.index, r],
            recv_sem=self.pair_recv.at[self.index, r],
            device_id=(self.chip * 2 + 1 - self.core, self.z),
            device_id_type=MESH,
        )

    def fetch(self):
        return pltpu.make_async_copy(self.shard, self.slot(self.at(0, self.core)), self.own.at[self.index])

    def start(self):
        for r in self.direct:
            self.to_chip(r, self.at(0, self.core)).start()

    def start_pair(self):
        self.to_pair(0, self.at(0, self.core)).start()
        self.fetch().start()

    def land(self):
        for r in self.direct:
            owner = self.at(r, self.core)
            self.to_chip(r, owner).wait_recv()
            if self.relayed:
                self.relay(r - 1, owner).start()
            self.to_pair(r, owner).start()

    def land_last(self):
        if self.relayed:
            owner = self.at(3, self.core)
            for which in range(2):
                self.relay(which, owner).wait_recv()
            self.to_pair(3, owner).start()

    def arrive(self):
        self.fetch().wait()
        for r in range(self.chips):
            self.to_pair(r, self.at(r, 1 - self.core)).wait_recv()

    def finish(self):
        for r in self.direct:
            self.to_chip(r, self.at(0, self.core)).wait_send()
            if self.relayed:
                self.relay(r - 1, self.at(r, self.core)).wait_send()
        for r in range(self.chips):
            self.to_pair(r, self.at(r, self.core)).wait_send()


def greet(chips, count):
    dp, z = lax.axis_index("dp"), lax.axis_index("branch")
    core, chip = lax.rem(dp, 2), lax.div(dp, 2)
    barrier = pltpu.get_barrier_semaphore()
    for r in range(1, chips):
        pl.semaphore_signal(barrier, inc=1, device_id=(flip(chip, r) * 2 + core, z), device_id_type=MESH)
    pl.semaphore_signal(barrier, inc=1, device_id=(chip * 2 + 1 - core, z), device_id_type=MESH)
    for shift in range(1, count):
        pl.semaphore_signal(barrier, inc=1, device_id=(dp, lax.rem(z + shift, count)), device_id_type=MESH)
    pl.semaphore_wait(barrier, chips + count - 1)


def swapped(y):
    lane = lax.rem(lax.broadcasted_iota(jnp.int32, y.shape, 1), HEAD_DIM)
    return jnp.where(lane < ROT // 2, pltpu.roll(y, LANES - ROT // 2, 1), pltpu.roll(y, ROT // 2, 1))


class Fold:
    def __init__(self, bufs, sems, count, dp):
        self.bufs, self.sems, self.count, self.dp = bufs, sems, count, dp
        self.z = lax.axis_index("branch")

    def place(self, up):
        return self.z if up else self.count - 1 - self.z

    def dest(self, up, step):
        return self.count - 1 - step if up else step

    def hop(self, up, step, src=None):
        buf = self.bufs[0 if up else 1]
        send, recv = self.sems[0 if up else 2], self.sems[1 if up else 3]
        return pltpu.make_async_remote_copy(
            src_ref=buf.at[step] if src is None else src,
            dst_ref=buf.at[step],
            send_sem=send.at[step],
            recv_sem=recv.at[step],
            device_id=(self.dp, self.z + 1 if up else self.z - 1),
            device_id_type=MESH,
        )

    def first(self, up, step, src):
        @pl.when(self.place(up) == 0)
        def _():
            self.hop(up, step, src).start()

    def pump(self, k, own_block, rows):
        for up in (False, True):
            place = self.place(up)

            @pl.when(jnp.logical_and(place >= 1, place <= k))
            def _(up=up, place=place):
                step = k - place
                own = own_block(up, self.dest(up, step))
                self.hop(up, step).wait_recv()
                buf = self.bufs[0 if up else 1]

                def add(i, _):
                    part = aligned(i, 32)
                    buf[step, part, :] = (buf[step, part, :].astype(F32) + own[part, :].astype(F32)).astype(BF16)
                    return 0

                lax.fori_loop(0, rows // 32, add, 0)
                self.hop(up, step).start()

    def last_step(self, up):
        return jnp.clip(self.count - 1 - self.place(up), 0, self.count - 2)

    def arrive(self):
        for up in (False, True):

            @pl.when(self.place(up) >= 1)
            def _(up=up):
                self.hop(up, self.last_step(up)).wait_recv()

    def total(self, own, part):
        out = own
        for up in (False, True):
            got = self.bufs[0 if up else 1][self.last_step(up), part, :].astype(F32)
            out = out + jnp.where(self.place(up) >= 1, got, 0.0)
        return out

    def finish(self):
        for step in range(self.count - 1):
            for up in (False, True):

                @pl.when(self.place(up) + step <= self.count - 2)
                def _(up=up, step=step):
                    self.hop(up, step).wait_send()


class Scatter:
    def __init__(self, index, block, tile, rows_first, base, size, landing, own_out, stage, wide, chips, sems):
        self.index, self.block, self.tile, self.rows_first = index, block, tile, rows_first
        self.base, self.size, self.landing, self.own_out = base, size, landing, own_out
        self.stage, self.wide = stage, wide
        self.chips = chips
        self.st_sem, self.pair_recv, self.send, self.recv, self.wide_sem = sems
        dp = lax.axis_index("dp")
        self.z = lax.axis_index("branch")
        self.core, self.chip = lax.rem(dp, 2), lax.div(dp, 2)
        self.tiles = size[1 if rows_first else 0] // tile
        self.height = size[0] if rows_first else tile
        self.breadth = tile if rows_first else size[1]
        self.order = [*range(1, chips), 0]

    def slot(self, r):
        high, wide = self.size
        if self.rows_first:
            return self.base.at[r * high : (r + 1) * high, 0:wide]
        return self.base.at[0:high, r * wide : (r + 1) * wide]

    def slot_part(self, r, i):
        high, wide = self.size
        at = aligned(i, self.tile)
        return (pl.ds(r * high, high), at) if self.rows_first else (at, pl.ds(r * wide, wide))

    def part(self, ref, i):
        at = aligned(i, self.tile)
        return ref.at[:, at] if self.rows_first else ref.at[at, :]

    def view(self, ref, slot):
        return ref.at[slot, pl.ds(0, self.height), pl.ds(0, self.breadth)]

    def to_pair(self, r, i, slot):
        return pltpu.make_async_remote_copy(
            src_ref=self.view(self.stage, slot),
            dst_ref=self.base.at[self.slot_part(r, i)],
            send_sem=self.st_sem.at[slot],
            recv_sem=self.pair_recv.at[self.index, r],
            device_id=(self.chip * 2 + 1 - self.core, self.z),
            device_id_type=MESH,
        )

    def from_pair(self, r):
        return pltpu.make_async_remote_copy(
            src_ref=self.slot(r),
            dst_ref=self.slot(r),
            send_sem=self.st_sem.at[0],
            recv_sem=self.pair_recv.at[self.index, r],
            device_id=(self.chip * 2 + 1 - self.core, self.z),
            device_id_type=MESH,
        )

    def to_owner(self, r):
        return pltpu.make_async_remote_copy(
            src_ref=self.slot(r),
            dst_ref=self.landing.at[r - 1],
            send_sem=self.send.at[self.index, r - 1],
            recv_sem=self.recv.at[self.index, r - 1],
            device_id=(flip(self.chip, r) * 2 + self.core, self.z),
            device_id_type=MESH,
        )

    def to_out(self, i):
        source = self.wide.at[0 : self.height, 0 : self.breadth]
        return pltpu.make_async_copy(source, self.part(self.own_out, i), self.wide_sem)

    def partners(self, n):
        r = self.order[n]
        owner = flip(self.chip, r) * 2 + 1 - self.core

        def body(i, _):
            slot = lax.rem(n * self.tiles + i, 2)
            y = self.block(owner, i)
            if n * self.tiles >= 2:
                self.to_pair(r, i, slot).wait_send()
            else:

                @pl.when(n * self.tiles + i >= 2)
                def _():
                    self.to_pair(r, i, slot).wait_send()

            self.stage[slot, 0 : self.height, 0 : self.breadth] = y.astype(BF16)
            self.to_pair(r, i, slot).start()
            return 0

        lax.fori_loop(0, self.tiles, body, 0)

    def own(self, n):
        r = self.order[n]
        owner = flip(self.chip, r) * 2 + self.core
        self.from_pair(r).wait_recv()

        def body(i, _):
            y = self.block(owner, i)
            at = self.slot_part(r, i)
            y = y + self.base[at].astype(F32)
            if r:
                self.base[at] = y.astype(BF16)
            else:
                @pl.when(i >= 1)
                def _():
                    self.to_out(i).wait()

                self.wide[0 : self.height, 0 : self.breadth] = y
                self.to_out(i).start()
            return 0

        lax.fori_loop(0, self.tiles, body, 0)
        if r:
            self.to_owner(r).start()
        else:
            self.to_out(self.tiles - 1).wait()

    def run(self, before=lambda n: None):
        for n in range(self.chips):
            before(n)
            self.partners(n)
            if n:
                self.own(n - 1)
        self.own(self.chips - 1)
        self.drain()

    def drain(self):
        total = self.chips * self.tiles
        for i in range(max(total - 2, 0), total):
            self.to_pair(0, 0, i % 2).wait_send()

    def sent(self):
        for r in range(1, self.chips):
            self.to_owner(r).wait_send()

    def finish(self):
        for r in range(1, self.chips):
            self.to_owner(r).wait_recv()


def piece_of(extent):
    return next(n for n in (512, 256, 128) if extent % n == 0)


def block_kernel(
    chips, count,
    x, gain, beta, bqkv, bf1, out_bias, seg_row, frequency, wq, wk, wv, wf1, wo, wf2, cot,
    block_out, input_grad, vec_out, own_qkv, own_f1, own_o, own_f2, land_qkv, land_f1, land_o, land_f2, hid_t, act_t,
    hid, vqkv, vf1, vf2, vo, qkv, att, att_t, lse, act, dg, g, stage, tab_c, tab_s, segs,
    dk_acc, dv_acc, k_t, up_buf, dn_buf, wide_row, wide_col, ig_stage, vec, vec_pair, vec_chip, vec_z,
    w_send, w_recv, r_send, r_recv, p_send, p_recv, own_sem,
    h_us, h_ur, h_ds, h_dr, c_us, c_ur, c_ds, c_dr, cot_sem, st_sem,
    act_sem, hid_sem, out_sem, ig_sem, st_row_sem, st_col_sem, pair_recv, x_send, x_recv, wide_row_sem, wide_col_sem,
    zo_us, zo_ur, zo_ds, zo_dr, zh_us, zh_ur, zh_ds, zh_dr, free_up, free_dn, pair_free, hid_free,
    v_ps, v_pr, v_cs, v_cr, v_zs, v_zr,
):
    z = lax.axis_index("branch")
    dp = lax.axis_index("dp")
    core, chip = lax.rem(dp, 2), lax.div(dp, 2)
    rows, width = x.shape
    length = rows * count
    hcols = wo.shape[0]
    units = wf2.shape[0]
    part_w = width // (2 * chips)
    last = count - 1
    sems = (w_send, w_recv, r_send, r_recv, p_send, p_recv, own_sem)
    g_qkv = [
        Gather(n, w, vqkv.at[:, n * hcols : (n + 1) * hcols], True, chips, sems) for n, w in enumerate((wq, wk, wv))
    ]
    g_f1 = Gather(3, wf1, vf1, True, chips, sems)
    g_o = Gather(4, wo, vo, False, chips, sems)
    g_f2 = Gather(5, wf2, vf2, False, chips, sems)
    h_chain = Chain(hid.at[aligned(z, rows), :], hid, rows, count, (h_us, h_ur, h_ds, h_dr), dp)
    c_chain = Chain(cot, g, rows, count, (c_us, c_ur, c_ds, c_dr), dp)
    part = hid
    act_v = vf2.at[0:units, width // 2 : width // 2 + length]

    def rows_of(ref, d):
        return ref.at[aligned(d, rows), :]

    fold_out = Fold((up_buf, dn_buf), (zo_us, zo_ur, zo_ds, zo_dr), count, dp)
    fold_hid = Fold((up_buf, dn_buf), (zh_us, zh_ur, zh_ds, zh_dr), count, dp)

    at_f1, at_ob, at_gain = 3 * hcols, 3 * hcols + units, 3 * hcols + units + width
    at_beta = at_gain + width

    def hand_over(free):
        pl.semaphore_signal(free, inc=1, device_id=(chip * 2 + 1 - core, z), device_id_type=MESH)
        pl.semaphore_wait(free, 1)

    sems_row = (st_row_sem, pair_recv, x_send, x_recv, wide_row_sem)
    sems_col = (st_col_sem, pair_recv, x_send, x_recv, wide_col_sem)
    tile_f2, tile_o = piece_of(units), piece_of(hcols)
    tile_f1, tile_qkv = piece_of(units), piece_of(3 * hcols)

    def f2_block(owner, i):
        return dot_nn(act_v[aligned(i, tile_f2), :], g[:, aligned(owner, part_w)])

    def o_block(owner, i):
        return dot_nn(att_t[aligned(i, tile_o), :], g[:, aligned(owner, part_w)])

    def hid_part(n):
        return vo.at[(n % 2) * part_w : (n % 2 + 1) * part_w, width // 2 : width // 2 + length]

    def hid_copy(n, owner):
        return pltpu.make_async_copy(hid_t.at[aligned(owner, part_w), :], hid_part(n), hid_sem.at[n % 2])

    state = {}

    def f1_block(owner, i):
        return dot_nn(hid_part(state["at"])[...], dg[:, aligned(i, tile_f1)])

    def qkv_block(owner, i):
        return dot_nn(hid_part(state["at"])[...], qkv[:, aligned(i, tile_qkv)])

    def run_rows(scatter, between=None):
        turns = [(True, 0)]
        for n in range(1, chips):
            turns += [(True, n), (False, n - 1)]
        turns.append((False, chips - 1))
        owners = [flip(chip, scatter.order[n]) * 2 + (1 - core if pair else core) for pair, n in turns]
        hid_copy(0, owners[0]).start()
        for i, (pair, n) in enumerate(turns):
            if i + 1 < len(turns):
                hid_copy(i + 1, owners[i + 1]).start()
            hid_copy(i, owners[i]).wait()
            state["at"] = i
            (scatter.partners if pair else scatter.own)(n)
            if between is not None and i == len(turns) // 2:
                between()
        scatter.drain()

    sc_f2 = Scatter(0, f2_block, tile_f2, False, vf2, (units, part_w), land_f2, own_f2, stage, wide_col, chips, sems_col)
    sc_f1 = Scatter(1, f1_block, tile_f1, True, act, (part_w, units), land_f1, own_f1, stage, wide_row, chips, sems_row)
    sc_o = Scatter(2, o_block, tile_o, False, vo, (hcols, part_w), land_o, own_o, stage, wide_col, chips, sems_col)
    sc_qkv = Scatter(3, qkv_block, tile_qkv, True, hid, (part_w, 3 * hcols), land_qkv, own_qkv, stage, wide_row, chips, sems_row)

    greet(chips, count)
    for gw in (*g_qkv, g_f1):
        gw.start()
    for gw in (*g_qkv, g_f1, g_o, g_f2):
        gw.start_pair()
    fetch_cot = pltpu.make_async_copy(cot, g.at[aligned(z, rows), :], cot_sem)
    fetch_cot.start()

    step_rows = 32

    def norm(i, _):
        part_rows = aligned(i, step_rows)
        inputs = x[part_rows, :].astype(F32)
        center = inputs - jnp.mean(inputs, axis=-1, keepdims=True)
        inverse = lax.rsqrt(jnp.mean(center * center, axis=-1, keepdims=True) + EPSILON)
        where = pl.ds(pl.multiple_of(z * rows + i * step_rows, step_rows), step_rows)
        hid[where, :] = (center * inverse * gain[...] + beta[...]).astype(BF16)
        return 0

    lax.fori_loop(0, rows // step_rows, norm, 0)
    h_chain.start()
    vec[...] = jnp.zeros_like(vec)

    row_segs = seg_row[...].astype(F32)
    places = lax.broadcasted_iota(jnp.int32, (1, length), 1).astype(F32)
    firsts = [
        jnp.min(jnp.where(row_segs == float(value), places, float(length)), axis=1, keepdims=True)
        for value in range(4)
    ]
    for c in range(length // LANES):
        here = slice(c * LANES, (c + 1) * LANES)
        seg = jnp.broadcast_to(row_segs[:, here], (LANES, LANES)).T
        segs[here, :] = seg.astype(BF16)
        start = jnp.zeros((LANES, LANES), F32)
        for value in range(4):
            start = jnp.where(seg == float(value), firsts[value], start)
        place = (lax.broadcasted_iota(jnp.int32, (LANES, LANES), 0) + c * LANES).astype(F32)
        angle = (place - start) * frequency[...]
        lane = lax.rem(lax.broadcasted_iota(jnp.int32, (LANES, LANES), 1), HEAD_DIM)
        sine = jnp.where(lane < ROT, jnp.sin(angle), 0.0)
        tab_c[here, :] = jnp.where(lane < ROT, jnp.cos(angle), 1.0)
        tab_s[here, :] = jnp.where(lane < ROT // 2, -sine, sine)
    key_row = jnp.where(row_segs == 0.0, -1.0, row_segs)

    for gw in g_qkv:
        gw.land()
    if count > 2:
        h_chain.pump(1)
    g_f1.land()
    for gw in (g_o, g_f2):
        gw.start()
    for s in range(2, count - 1):
        h_chain.pump(s)
    c_chain.start()
    for gw in g_qkv:
        gw.land_last()
    for gw in g_qkv:
        gw.arrive()

    ht, wt = tile_of(hcols), tile_of(width)

    def turn_copy(slot, j, cols_i):
        return pltpu.make_async_copy(
            stage.at[slot, pl.ds(0, wt), pl.ds(0, rows)], hid_t.at[cols_i, aligned(j, rows)], st_sem.at[slot]
        )

    def project(j):
        rows_j = aligned(j, rows)
        for which in range(3):
            for c in range(hcols // ht):
                at = which * hcols + c * ht
                y = dot_nn(hid[rows_j, :], vqkv[:, at : at + ht]) + bqkv[:, at : at + ht]
                for piece in range(ht // LANES):
                    part_y = y[:, piece * LANES : (piece + 1) * LANES]
                    if which < 2:
                        part_y = part_y * tab_c[rows_j, :] + swapped(part_y) * tab_s[rows_j, :]
                    low = part_y.astype(BF16)
                    if which == 0:
                        low = low * BF16(HEAD_DIM**-0.5)
                    qkv[rows_j, at + piece * LANES : at + (piece + 1) * LANES] = low

        def turn(i, _):
            cols_i, slot = aligned(i, wt), lax.rem(i, 2)

            @pl.when(i >= 2)
            def _():
                turn_copy(slot, j, cols_i).wait()

            stage[slot, 0:wt, 0:rows] = hid[rows_j, cols_i].T
            turn_copy(slot, j, cols_i).start()
            return 0

        n_turn = width // wt
        lax.fori_loop(0, n_turn, turn, 0)
        for i in range(max(n_turn - 2, 0), n_turn):
            turn_copy(i % 2, j, pl.ds(0, wt)).wait()

    h_chain.by_distance(0, 2 * count - 3, project)
    g_o.land()
    h_chain.by_distance(2 * count - 3, 2 * count - 1, project)
    g_f2.land()
    if count > 2:
        c_chain.pump(1)

    qb = tile_of(length, QBLOCK)
    pairs = hcols // LANES

    def attend(pair, _):
        cols = aligned(pair, LANES)
        k_cols, v_cols = aligned(pairs + pair, LANES), aligned(2 * pairs + pair, LANES)
        lane = lax.broadcasted_iota(jnp.int32, (1, LANES), 1)
        for b in range(length // qb):
            here = slice(b * qb, (b + 1) * qb)
            before = b * qb
            q2 = qkv[here, cols]
            seg_q = segs[here, 0:1].astype(F32)
            ki = lax.broadcasted_iota(jnp.int32, (qb, qb), 1)
            qi = lax.broadcasted_iota(jnp.int32, (qb, qb), 0)
            seen_here = jnp.logical_or(jnp.logical_and(seg_q == key_row[:, here], ki <= qi), ki == qi)
            out = jnp.zeros((qb, LANES), F32)
            stat = jnp.zeros((qb, LANES), F32)
            for h in range(2):
                mine = (lane // HEAD_DIM) == h
                qh = jnp.where(mine, q2, BF16(0))
                s_here = jnp.where(seen_here, dot_nt(qh, qkv[here, k_cols]), NEGATIVE)
                top = jnp.max(s_here, axis=-1, keepdims=True)
                if before:
                    s_before = jnp.where(
                        seg_q == key_row[:, :before], dot_nt(qh, qkv[:before, k_cols]), NEGATIVE
                    )
                    top = jnp.maximum(top, jnp.max(s_before, axis=-1, keepdims=True))
                e_here = jnp.exp(s_here - top)
                total = jnp.sum(e_here, axis=-1, keepdims=True)
                if before:
                    e_before = jnp.exp(s_before - top)
                    total = total + jnp.sum(e_before, axis=-1, keepdims=True)
                share = 1.0 / total
                o = dot_nn((e_here * share).astype(BF16), jnp.where(mine, qkv[here, v_cols], BF16(0)))
                if before:
                    o = o + dot_nn(
                        (e_before * share).astype(BF16), jnp.where(mine, qkv[:before, v_cols], BF16(0))
                    )
                out = out + o
                stat = jnp.where(mine, top + jnp.log(total), stat)
            att[here, cols] = out.astype(BF16)
            att_t[cols, here] = out.T.astype(BF16)
            turned = stat.T
            lse[pl.ds(2 * pair, 1), here] = turned[0:1, :]
            lse[pl.ds(2 * pair + 1, 1), here] = turned[HEAD_DIM : HEAD_DIM + 1, :]
        return 0

    half_pairs = pairs // 2
    lax.fori_loop(0, half_pairs, attend, 0)
    for s in range(2, count - 1):
        c_chain.pump(s)
    lax.fori_loop(half_pairs, pairs - 1, attend, 0)
    g_f1.land_last()
    lax.fori_loop(pairs - 1, pairs, attend, 0)
    g_f1.arrive()

    mt, ft = tile_of(length), tile_of(units)
    per_row = units // ft
    n_tiles = (length // mt) * per_row

    def staged(slot, rows_i, cols_i):
        return pltpu.make_async_copy(stage.at[slot, pl.ds(0, ft), :], act_t.at[cols_i, rows_i], st_sem.at[slot])

    def unit(i, _):
        rows_i, cols_i = aligned(lax.div(i, per_row), mt), aligned(lax.rem(i, per_row), ft)
        slot = lax.rem(i, 2)

        @pl.when(i >= 2)
        def _():
            staged(slot, rows_i, cols_i).wait()

        y = dot_nn(hid[rows_i, :], vf1[:, cols_i]) + bf1[:, cols_i]
        square = y * y
        t = jnp.tanh(GELU_C * (y + GELU_A * (y * square)))
        half = 0.5 * (1.0 + t)
        low = (y * half).astype(BF16)
        act[rows_i, cols_i] = low
        stage[slot, 0:ft, :] = low.T
        dg[rows_i, cols_i] = (
            half + 0.5 * y * (1.0 - t * t) * (GELU_C * (1.0 + 3.0 * GELU_A * square))
        ).astype(BF16)
        staged(slot, rows_i, cols_i).start()
        return 0

    half_tiles = n_tiles // 2
    lax.fori_loop(0, half_tiles, unit, 0)
    for gw in (g_o, g_f2):
        gw.land_last()
    lax.fori_loop(half_tiles, n_tiles, unit, 0)
    for i in range(max(n_tiles - 2, 0), n_tiles):
        staged(i % 2, pl.ds(0, mt), pl.ds(0, ft)).wait()
    for gw in (g_o, g_f2):
        gw.arrive()

    h_chain.finish()

    def output(i, _):
        rows_i, cols_i = aligned(lax.div(i, width // wt), mt), aligned(lax.rem(i, width // wt), wt)
        part[rows_i, cols_i] = (
            dot_nn(act[rows_i, :], vf2[:, cols_i]) + dot_nn(att[rows_i, :], vo[:, cols_i])
        ).astype(BF16)
        return 0

    lax.fori_loop(0, (length // mt) * (width // wt), output, 0)
    for st in range(count - 1):
        fold_out.first(True, st, rows_of(part, last - st))
        fold_out.first(False, st, rows_of(part, st))
    fetch_cot.wait()


    def unit_back(j):
        rows_j = aligned(j, rows)
        def body(i, _):
            cols_i = aligned(i, ft)
            low = (dot_nt(g[rows_j, :], vf2[cols_i, :]) * dg[rows_j, cols_i].astype(F32)).astype(BF16)
            dg[rows_j, cols_i] = low
            to = pl.ds(pl.multiple_of(at_f1 + i * ft, LANES), ft)
            vec[:, to] += jnp.sum(low.astype(F32), axis=0, keepdims=True)
            return 0

        lax.fori_loop(0, per_row, body, 0)
        att[rows_j, :] = dot_nt(g[rows_j, :], vo[...]).astype(BF16)
        vec[:, at_ob:at_gain] += jnp.sum(g[rows_j, :].astype(F32), axis=0, keepdims=True)

    c_chain.by_distance(0, 2 * count - 1, unit_back)
    g_o.finish()
    g_f2.finish()
    c_chain.finish()
    load_act = pltpu.make_async_copy(act_t, act_v, act_sem)
    load_act.start()
    hand_over(pair_free)
    own_part = lambda up, d: rows_of(part, d)
    load_act.wait()
    if count > 2:
        fold_out.pump(1, own_part, rows)
    sc_f2.run()
    sc_o.run()
    for k in range(2, count - 1):
        fold_out.pump(k, own_part, rows)


    def key_of(lo, hi):
        seg = segs[lo:hi, 0:1].astype(F32)
        return jnp.where(seg == 0.0, -1.0, seg)

    def turn_back(y, at):
        return y * tab_c[at, :] - swapped(y) * tab_s[at, :]

    def attend_back(pair, _):
        q_cols = aligned(pair, LANES)
        k_cols, v_cols = aligned(pairs + pair, LANES), aligned(2 * pairs + pair, LANES)
        lane = lax.broadcasted_iota(jnp.int32, (1, LANES), 1)
        dk_acc[...] = jnp.zeros_like(dk_acc)
        dv_acc[...] = jnp.zeros_like(dv_acc)
        k_t[...] = qkv[:, k_cols].T
        for b in range(length // qb):
            here, reach = slice(b * qb, (b + 1) * qb), (b + 1) * qb
            before = b * qb
            q2, g2 = qkv[here, q_cols], att[here, q_cols]
            ki = lax.broadcasted_iota(jnp.int32, (qb, qb), 0)
            qi = lax.broadcasted_iota(jnp.int32, (qb, qb), 1)
            seen_here = jnp.logical_or(
                jnp.logical_and(key_of(before, reach) == row_segs[:, here], ki <= qi), ki == qi
            )
            dq_t = []
            for h in range(2):
                mine = (lane // HEAD_DIM) == h
                qh, gh = jnp.where(mine, q2, BF16(0)), jnp.where(mine, g2, BF16(0))
                stat = lse[pl.ds(2 * pair + h, 1), here]
                spans = ([(0, before)] if before else []) + [(before, reach)]
                probs, grads = [], []
                delta = jnp.zeros((1, qb), F32)
                for lo, hi in spans:
                    seen = seen_here if lo == before else key_of(lo, hi) == row_segs[:, here]
                    p = jnp.exp(jnp.where(seen, dot_nt(qkv[lo:hi, k_cols], qh), NEGATIVE) - stat)
                    pg = dot_nt(qkv[lo:hi, v_cols], gh)
                    delta = delta + jnp.sum(p * pg, axis=0, keepdims=True)
                    probs.append(p)
                    grads.append(pg)
                acc = jnp.zeros((HEAD_DIM, qb), F32)
                for (lo, hi), p, pg in zip(spans, probs, grads):
                    sg = (p * (pg - delta)).astype(BF16)
                    dv_acc[lo:hi, :] += dot_nn(p.astype(BF16), gh)
                    dk_acc[lo:hi, :] += dot_nn(sg, qh)
                    acc = acc + dot_nn(k_t[h * HEAD_DIM : (h + 1) * HEAD_DIM, lo:hi], sg)
                dq_t.append(acc)
            dq = jnp.concatenate(dq_t, axis=0).T * HEAD_DIM**-0.5
            qkv[here, q_cols] = turn_back(dq, here).astype(BF16)
        for b in range(length // qb):
            here = slice(b * qb, (b + 1) * qb)
            qkv[here, k_cols] = turn_back(dk_acc[here, :], here).astype(BF16)
            qkv[here, v_cols] = dv_acc[here, :].astype(BF16)
        for cols in (q_cols, k_cols, v_cols):
            vec[:, cols] = jnp.sum(qkv[:, cols].astype(F32), axis=0, keepdims=True)
        return 0

    lax.fori_loop(0, pairs, attend_back, 0)

    def hidden_back(d):
        here = pl.ds(d * rows, rows)

        def body(i, _):
            cols_i = aligned(i, wt)
            g[here, cols_i] = (
                dot_nt(dg[here, :], vf1[cols_i, :]) + dot_nt(qkv[here, :], vqkv[cols_i, :])
            ).astype(BF16)
            return 0

        lax.fori_loop(0, width // wt, body, 0)

    def set_out(d):
        if d > 0:
            fold_hid.first(True, last - d, rows_of(g, d))
        if d < last:
            fold_hid.first(False, d, rows_of(g, d))

    dests = list(dict.fromkeys(d for both in zip(range(last, -1, -1), range(count)) for d in both))
    fold_out.arrive()
    def finish_output(i, _):
        part = aligned(i, 32)
        at = pl.ds(pl.multiple_of(z * rows + i * 32, 32), 32)
        y = fold_out.total(hid[at, :].astype(F32), part)
        hid[at, :] = (x[part, :].astype(F32) + y + out_bias[...]).astype(BF16)
        return 0

    lax.fori_loop(0, rows // 32, finish_output, 0)
    save_out = pltpu.make_async_copy(hid.at[aligned(z, rows), :], block_out, out_sem)
    save_out.start()
    fold_out.finish()

    @pl.when(z > 0)
    def _():
        pl.semaphore_signal(free_up, inc=1, device_id=(dp, z - 1), device_id_type=MESH)

    @pl.when(z < last)
    def _():
        pl.semaphore_signal(free_dn, inc=1, device_id=(dp, z + 1), device_id_type=MESH)

    @pl.when(z < last)
    def _():
        pl.semaphore_wait(free_up, 1)

    @pl.when(z > 0)
    def _():
        pl.semaphore_wait(free_dn, 1)

    for d in dests:
        hidden_back(d)
        set_out(d)
    own_grad = lambda up, d: rows_of(g, d)
    run_rows(sc_f1, (lambda: fold_hid.pump(1, own_grad, rows)) if count > 2 else None)
    save_out.wait()
    hand_over(hid_free)
    run_rows(sc_qkv)
    sc_f2.sent()
    load_cot = pltpu.make_async_copy(cot, vf2.at[0:rows, 0:width], cot_sem)
    load_cot.start()
    for k in range(2, count - 1):
        fold_hid.pump(k, own_grad, rows)
    fold_hid.arrive()
    load_cot.wait()

    step_rows = 16

    def ig_copy(i, slot):
        return pltpu.make_async_copy(ig_stage.at[slot], input_grad.at[aligned(i, step_rows), :], ig_sem.at[slot])

    def norm_back(i, _):
        part = aligned(i, step_rows)
        slot = lax.rem(i, 2)
        inputs = x[part, :].astype(F32)
        center = inputs - jnp.mean(inputs, axis=-1, keepdims=True)
        inverse = lax.rsqrt(jnp.mean(center * center, axis=-1, keepdims=True) + EPSILON)
        normed = center * inverse
        own = g[pl.ds(pl.multiple_of(z * rows + i * step_rows, step_rows), step_rows), :].astype(F32)
        y = fold_hid.total(own, part)
        vec[:, at_gain : at_gain + width] += jnp.sum(y * normed, axis=0, keepdims=True)
        vec[:, at_beta : at_beta + width] += jnp.sum(y, axis=0, keepdims=True)
        scaled = y * gain[...]
        result = vf2[part, :].astype(F32) + inverse * (
            scaled
            - jnp.mean(scaled, axis=-1, keepdims=True)
            - normed * jnp.mean(scaled * normed, axis=-1, keepdims=True)
        )

        @pl.when(i >= 2)
        def _():
            ig_copy(i, slot).wait()

        ig_stage[slot] = result
        ig_copy(i, slot).start()
        return 0

    steps = rows // step_rows
    lax.fori_loop(0, steps, norm_back, 0)

    to_pair = pltpu.make_async_remote_copy(
        src_ref=vec, dst_ref=vec_pair, send_sem=v_ps, recv_sem=v_pr,
        device_id=(chip * 2 + 1 - core, z), device_id_type=MESH,
    )
    to_pair.start()
    for i in range(max(steps - 2, 0), steps):
        ig_copy(i, i % 2).wait()
    to_pair.wait()
    vec_chip[chip] = vec[...] + vec_pair[...]

    def chip_copy(r, slot):
        return pltpu.make_async_remote_copy(
            src_ref=vec_chip.at[chip], dst_ref=vec_chip.at[slot], send_sem=v_cs.at[r - 1], recv_sem=v_cr.at[r - 1],
            device_id=(flip(chip, r) * 2 + core, z), device_id_type=MESH,
        )

    for r in range(1, chips):
        chip_copy(r, chip).start()
    for r in range(1, chips):
        chip_copy(r, flip(chip, r)).wait_recv()
    total = vec_chip[0]
    for c in range(1, chips):
        total = total + vec_chip[c]
    vec_out[:, 0:at_gain] = total[:, 0:at_gain]
    vec_z[z] = total[:, at_gain:]

    def z_copy(shift, slot):
        return pltpu.make_async_remote_copy(
            src_ref=vec_z.at[z], dst_ref=vec_z.at[slot], send_sem=v_zs.at[shift - 1], recv_sem=v_zr.at[shift - 1],
            device_id=(dp, lax.rem(z + shift, count)), device_id_type=MESH,
        )

    for shift in range(1, count):
        z_copy(shift, z).start()
    for shift in range(1, count):
        z_copy(shift, lax.rem(z + count - shift, count)).wait_recv()
    total = vec_z[0]
    for n in range(1, count):
        total = total + vec_z[n]
    vec_out[:, at_gain:] = total
    for r in range(1, chips):
        chip_copy(r, chip).wait_send()
    for shift in range(1, count):
        z_copy(shift, z).wait_send()
    fold_hid.finish()
    for s in (sc_f1, sc_o, sc_qkv):
        s.sent()
    for s in (sc_f2, sc_f1, sc_o, sc_qkv):
        s.finish()
    for gw in (*g_qkv, g_f1):
        gw.finish()


def run_block(ndp, count, x, gain, beta, bqkv, bf1, out_bias, seg_row, frequency, wq, wk, wv, wf1, wo, wf2, cot):
    chips = ndp // 2
    rows, width = x.shape
    length = rows * count
    hcols, units = wo.shape[0], wf2.shape[0]
    part_w = width // ndp
    total = 3 * hcols + units + 3 * width
    heads = hcols // HEAD_DIM
    mt, ft, wt = tile_of(length), tile_of(units), tile_of(width)
    anywhere = pl.BlockSpec(memory_space=pl.ANY)
    vmem = pl.BlockSpec(memory_space=pltpu.VMEM)
    low = lambda *shape: jax.ShapeDtypeStruct(shape, BF16)
    wide = lambda *shape: jax.ShapeDtypeStruct(shape, F32)
    outs = [
        low(rows, width), wide(rows, width), wide(1, total),
        wide(part_w, 3 * hcols), wide(part_w, units), wide(hcols, part_w), wide(units, part_w),
        low(chips - 1, part_w, 3 * hcols), low(chips - 1, part_w, units), low(chips - 1, hcols, part_w), low(chips - 1, units, part_w),
        low(width, length), low(units, length),
    ]
    v = lambda *shape: pltpu.VMEM(shape, BF16)
    w = lambda *shape: pltpu.VMEM(shape, F32)
    steps = max(count - 1, 1)
    dma = lambda *shape: pltpu.SemaphoreType.DMA(shape)
    one, plain = pltpu.SemaphoreType.DMA, pltpu.SemaphoreType.REGULAR
    row_tile = max(piece_of(units), piece_of(3 * hcols))
    col_tile = max(piece_of(units), piece_of(hcols))
    scratch = [
        v(length, width), v(width, 3 * hcols), v(width, units), v(units, width), v(hcols, width),
        v(length, 3 * hcols), v(length, hcols), v(hcols, length), w(heads, length), v(length, units), v(length, units),
        v(length, width), v(2, max(ft, wt, part_w), max(mt, part_w)), w(length, LANES), w(length, LANES), v(length, LANES),
        w(length, LANES), w(length, LANES), v(LANES, length), v(steps, rows, width), v(steps, rows, width),
        w(part_w, row_tile), w(col_tile, part_w),
        w(2, 16, width), w(1, total), w(1, total), w(chips, 1, total), w(count, 1, 2 * width),
        dma(6, chips - 1), dma(6, chips - 1), dma(6, 2), dma(6, 2), dma(6, chips), dma(6, chips), dma(6),
        *[dma(steps) for _ in range(8)], one, dma(2),
        one, dma(2), one, dma(2), dma(2), dma(2),
        dma(4, chips), dma(4, chips - 1), dma(4, chips - 1), one, one,
        *[dma(steps) for _ in range(8)], plain, plain, plain, plain,
        one, one, dma(chips - 1), dma(chips - 1), dma(steps), dma(steps),
    ]
    return pl.pallas_call(
        functools.partial(block_kernel, chips, count),
        out_shape=outs,
        in_specs=[vmem] * 8 + [anywhere] * 7,
        out_specs=[anywhere, anywhere, vmem] + [anywhere] * 10,
        scratch_shapes=scratch,
        compiler_params=pltpu.CompilerParams(
            collective_id=0, has_side_effects=True, vmem_limit_bytes=VMEM_LIMIT
        ),
        name="block_step",
    )(x, gain, beta, bqkv, bf1, out_bias, seg_row, frequency, wq, wk, wv, wf1, wo, wf2, cot)[:11]


def on_device(
    ndp, count,
    block_input, segment_ids, out_cotangent, norm_gain, norm_bias, query_weight, key_weight, value_weight,
    query_bias, key_bias, value_bias, out_weight, fc1_weight, fc1_bias, fc2_weight, output_bias,
):
    x = block_input[0]
    cot = out_cotangent[0]
    width = x.shape[1]
    half_rot = ROT // 2
    frequency = 10000.0 ** (-2.0 * (jnp.arange(LANES, dtype=jnp.int32) % half_rot).astype(F32) / ROT)
    bqkv = jnp.concatenate([query_bias, key_bias, value_bias])[None, :]
    gain, seg_row = norm_gain[None, :], segment_ids
    (block_output, input_grad, vec, own_qkv, own_f1, own_o, own_f2, land_qkv, land_f1, land_o, land_f2) = run_block(
        ndp, count, x, gain, norm_bias[None, :], bqkv, fc1_bias[None, :], output_bias[None, :], seg_row,
        frequency[None, :], query_weight, key_weight, value_weight, fc1_weight, out_weight, fc2_weight, cot,
    )
    hcols, units = out_weight.shape[0], fc2_weight.shape[0]

    def summed(own, landed):
        for n in range(landed.shape[0]):
            own = own + landed[n].astype(F32)
        return own

    def third(i):
        cols = slice(i * hcols, (i + 1) * hcols)
        return summed(own_qkv[:, cols], land_qkv[:, :, cols])

    sizes = (hcols, hcols, hcols, units, width, width, width)
    pieces, at = [], 0
    for size in sizes:
        pieces.append(vec[0, at : at + size])
        at += size
    qb, kb, vb, f1b, ob, gain_grad, beta_grad = pieces
    return (
        block_output[None], input_grad[None], gain_grad, beta_grad,
        third(0), third(1), third(2), qb, kb, vb,
        summed(own_o, land_o), summed(own_f1, land_f1), f1b, summed(own_f2, land_f2), ob,
    )


def solution(mesh):
    tokens, vector, split = P("dp", "branch", None), P(), P("branch")
    rows_first, cols_first = P("dp", "branch"), P("branch", "dp")
    in_specs = (
        tokens, P("dp", None), tokens, vector, vector, rows_first, rows_first, rows_first,
        split, split, split, cols_first, rows_first, split, cols_first, vector,
    )
    out_specs = (
        tokens, tokens, vector, vector, rows_first, rows_first, rows_first, split, split, split,
        cols_first, rows_first, split, cols_first, vector,
    )
    return jax.shard_map(
        functools.partial(on_device, mesh.shape["dp"], mesh.shape["branch"]),
        mesh=mesh, in_specs=in_specs, out_specs=out_specs, check_vma=False,
    )
```

```python
import functools

import jax
import jax.numpy as jnp
from jax import lax
from jax.experimental import pallas as pl
from jax.experimental.pallas import tpu as pltpu
from jax.sharding import PartitionSpec as P

HEAD_DIM = 64
ROT = 32
EPSILON = 1e-05
NEGATIVE = -1e30
LANES = 128
TILE = 512
QBLOCK = 256
MESH = pl.DeviceIdType.MESH
BF16 = jnp.bfloat16
F32 = jnp.float32
GELU_C = 0.7978845608028654
GELU_A = 0.044715
VMEM_LIMIT = 63 * 1024 * 1024 + 832 * 1024


def flip(index, bits):
    out = index
    bit = 1
    while bit <= bits:
        if bits & bit:
            out = out + bit * (1 - 2 * lax.rem(lax.div(index, bit), 2))
        bit *= 2
    return out


def dot_nn(left, right):
    return jnp.dot(left, right, preferred_element_type=F32)


def dot_nt(left, right):
    return lax.dot_general(left, right, (((1,), (1,)), ((), ())), preferred_element_type=F32)


def tile_of(extent, most=TILE):
    return min(most, extent)


def aligned(index, step):
    return pl.ds(pl.multiple_of(index * step, step), step)


class Chain:
    def __init__(self, own_src, buf, rows, count, sems, dp):
        self.own_src, self.buf, self.rows, self.count = own_src, buf, rows, count
        self.sems, self.dp = sems, dp
        self.z = lax.axis_index("branch")

    def block(self, slot):
        return self.buf.at[aligned(slot, self.rows), :]

    def copy(self, up, step, slot, src=None):
        send, recv = self.sems[0 if up else 2], self.sems[1 if up else 3]
        return pltpu.make_async_remote_copy(
            src_ref=self.block(slot) if src is None else src,
            dst_ref=self.block(slot),
            send_sem=send.at[step],
            recv_sem=recv.at[step],
            device_id=(self.dp, self.z + 1 if up else self.z - 1),
            device_id_type=MESH,
        )

    def sends(self, up, step):
        z, last = self.z, self.count - 1
        if up:
            return jnp.logical_and(z >= step, z < last)
        return jnp.logical_and(z + step <= last, z > 0)

    def sent_slot(self, up, step):
        return self.z - step if up else self.z + step

    def start(self):
        for up in (False, True):

            @pl.when(self.sends(up, 0))
            def _(up=up):
                self.copy(up, 0, self.z, self.own_src).start()

    def pump(self, step):
        for up in (False, True):

            @pl.when(self.sends(up, step))
            def _(up=up):
                slot = self.sent_slot(up, step)
                self.copy(up, step - 1, slot).wait_recv()
                self.copy(up, step, slot).start()

    def by_distance(self, first, end, work):
        def visit(i, _):
            far = lax.div(i + 1, 2)
            above = lax.rem(i, 2) == 0
            slot = self.z + jnp.where(above, far, -far)

            @pl.when(jnp.logical_and(slot >= 0, slot <= self.count - 1))
            def _():
                for up in (False, True):
                    mine = jnp.logical_and(far > 0, above if not up else jnp.logical_not(above))

                    @pl.when(jnp.logical_and(mine, jnp.logical_not(self.sends(up, far))))
                    def _(up=up):
                        self.copy(up, far - 1, slot).wait_recv()

                work(slot)

            return 0

        lax.fori_loop(first, end, visit, 0)

    def finish(self):
        for step in range(self.count - 1):
            for up in (False, True):

                @pl.when(self.sends(up, step))
                def _(up=up, step=step):
                    self.copy(up, step, self.sent_slot(up, step), self.own_src if step == 0 else None).wait_send()


class Gather:
    def __init__(self, index, shard, full, by_rows, chips, sems):
        self.index, self.shard, self.full = index, shard, full
        self.by_rows, self.chips = by_rows, chips
        self.send, self.recv, self.relay_send, self.relay_recv, self.pair_send, self.pair_recv, self.own = sems
        dp = lax.axis_index("dp")
        self.z = lax.axis_index("branch")
        self.core = lax.rem(dp, 2)
        self.chip = lax.div(dp, 2)
        self.width = shard.shape[0 if by_rows else 1]
        self.relayed = chips == 4
        self.direct = (1, 2) if self.relayed else tuple(range(1, chips))

    def slot(self, dp):
        part = aligned(dp, self.width)
        return self.full.at[part, :] if self.by_rows else self.full.at[:, part]

    def half(self, dp, which):
        if self.by_rows:
            return self.full.at[aligned(2 * dp + which, self.width // 2), :]
        rows = self.shard.shape[0] // 2
        return self.full.at[pl.ds(which * rows, rows), aligned(dp, self.width)]

    def at(self, r, core):
        return flip(self.chip, r) * 2 + core

    def to_chip(self, r, landing):
        return pltpu.make_async_remote_copy(
            src_ref=self.shard,
            dst_ref=self.slot(landing),
            send_sem=self.send.at[self.index, r - 1],
            recv_sem=self.recv.at[self.index, r - 1],
            device_id=(self.at(r, self.core), self.z),
            device_id_type=MESH,
        )

    def relay(self, which, owner):
        return pltpu.make_async_remote_copy(
            src_ref=self.half(owner, which),
            dst_ref=self.half(owner, which),
            send_sem=self.relay_send.at[self.index, which],
            recv_sem=self.relay_recv.at[self.index, which],
            device_id=(self.at(2 - which, self.core), self.z),
            device_id_type=MESH,
        )

    def to_pair(self, r, landing):
        return pltpu.make_async_remote_copy(
            src_ref=self.shard if r == 0 else self.slot(self.at(r, self.core)),
            dst_ref=self.slot(landing),
            send_sem=self.pair_send.at[self.index, r],
            recv_sem=self.pair_recv.at[self.index, r],
            device_id=(self.chip * 2 + 1 - self.core, self.z),
            device_id_type=MESH,
        )

    def fetch(self):
        return pltpu.make_async_copy(self.shard, self.slot(self.at(0, self.core)), self.own.at[self.index])

    def start(self):
        for r in self.direct:
            self.to_chip(r, self.at(0, self.core)).start()

    def start_pair(self):
        self.to_pair(0, self.at(0, self.core)).start()
        self.fetch().start()

    def land(self):
        for r in self.direct:
            owner = self.at(r, self.core)
            self.to_chip(r, owner).wait_recv()
            if self.relayed:
                self.relay(r - 1, owner).start()
            self.to_pair(r, owner).start()

    def land_last(self):
        if self.relayed:
            owner = self.at(3, self.core)
            for which in range(2):
                self.relay(which, owner).wait_recv()
            self.to_pair(3, owner).start()

    def arrive(self):
        self.fetch().wait()
        for r in range(self.chips):
            self.to_pair(r, self.at(r, 1 - self.core)).wait_recv()

    def finish(self):
        for r in self.direct:
            self.to_chip(r, self.at(0, self.core)).wait_send()
            if self.relayed:
                self.relay(r - 1, self.at(r, self.core)).wait_send()
        for r in range(self.chips):
            self.to_pair(r, self.at(r, self.core)).wait_send()


def greet(chips, count):
    dp, z = lax.axis_index("dp"), lax.axis_index("branch")
    core, chip = lax.rem(dp, 2), lax.div(dp, 2)
    barrier = pltpu.get_barrier_semaphore()
    for r in range(1, chips):
        pl.semaphore_signal(barrier, inc=1, device_id=(flip(chip, r) * 2 + core, z), device_id_type=MESH)
    pl.semaphore_signal(barrier, inc=1, device_id=(chip * 2 + 1 - core, z), device_id_type=MESH)
    for shift in range(1, count):
        pl.semaphore_signal(barrier, inc=1, device_id=(dp, lax.rem(z + shift, count)), device_id_type=MESH)
    pl.semaphore_wait(barrier, chips + count - 1)


def swapped(y):
    lane = lax.rem(lax.broadcasted_iota(jnp.int32, y.shape, 1), HEAD_DIM)
    return jnp.where(lane < ROT // 2, pltpu.roll(y, LANES - ROT // 2, 1), pltpu.roll(y, ROT // 2, 1))


class Fold:
    def __init__(self, bufs, sems, count, dp):
        self.bufs, self.sems, self.count, self.dp = bufs, sems, count, dp
        self.z = lax.axis_index("branch")

    def place(self, up):
        return self.z if up else self.count - 1 - self.z

    def dest(self, up, step):
        return self.count - 1 - step if up else step

    def hop(self, up, step, half, src=None):
        buf = self.bufs[0 if up else 1]
        send, recv = self.sems[0 if up else 2], self.sems[1 if up else 3]
        rows = pl.ds(half * (buf.shape[1] // 2), buf.shape[1] // 2)
        return pltpu.make_async_remote_copy(
            src_ref=buf.at[step, rows, :] if src is None else src.at[rows, :],
            dst_ref=buf.at[step, rows, :],
            send_sem=send.at[step, half],
            recv_sem=recv.at[step, half],
            device_id=(self.dp, self.z + 1 if up else self.z - 1),
            device_id_type=MESH,
        )

    def first(self, up, step, src):
        @pl.when(self.place(up) == 0)
        def _():
            for half in range(2):
                self.hop(up, step, half, src).start()

    def pump(self, k, own_block, rows):
        for up in (False, True):
            place = self.place(up)

            @pl.when(jnp.logical_and(place >= 1, place <= k))
            def _(up=up, place=place):
                step = k - place
                own = own_block(up, self.dest(up, step))
                buf = self.bufs[0 if up else 1]
                for half in range(2):
                    self.hop(up, step, half).wait_recv()

                    def add(i, _):
                        part = aligned(i, 32)
                        buf[step, part, :] = (buf[step, part, :].astype(F32) + own[part, :].astype(F32)).astype(BF16)
                        return 0

                    lax.fori_loop(half * (rows // 64), (half + 1) * (rows // 64), add, 0)
                    self.hop(up, step, half).start()

    def last_step(self, up):
        return jnp.clip(self.count - 1 - self.place(up), 0, self.count - 2)

    def arrive(self):
        for up in (False, True):

            @pl.when(self.place(up) >= 1)
            def _(up=up):
                for half in range(2):
                    self.hop(up, self.last_step(up), half).wait_recv()

    def total(self, own, part):
        out = own
        for up in (False, True):
            got = self.bufs[0 if up else 1][self.last_step(up), part, :].astype(F32)
            out = out + jnp.where(self.place(up) >= 1, got, 0.0)
        return out

    def finish(self):
        for step in range(self.count - 1):
            for up in (False, True):

                @pl.when(self.place(up) + step <= self.count - 2)
                def _(up=up, step=step):
                    for half in range(2):
                        self.hop(up, step, half).wait_send()


class Scatter:
    def __init__(self, index, block, tile, rows_first, base, size, relays, landing, own_out, stage, wide, chips, sems):
        self.index, self.block, self.tile, self.rows_first = index, block, tile, rows_first
        self.base, self.size, self.landing, self.own_out = base, size, landing, own_out
        self.stage, self.wide = stage, wide
        self.chips = chips
        self.relays = relays
        self.st_sem, self.pair_recv, self.send, self.recv, self.wide_sem, self.r_send, self.r_recv, self.r_load = sems
        dp = lax.axis_index("dp")
        self.z = lax.axis_index("branch")
        self.core, self.chip = lax.rem(dp, 2), lax.div(dp, 2)
        self.tiles = size[1 if rows_first else 0] // tile
        self.height = size[0] if rows_first else tile
        self.breadth = tile if rows_first else size[1]
        self.relayed = chips == 4
        self.order = [3, 1, 2, 0] if self.relayed else [*range(1, chips), 0]

    def slot(self, r):
        high, wide = self.size
        if self.rows_first:
            return self.base.at[r * high : (r + 1) * high, 0:wide]
        return self.base.at[0:high, r * wide : (r + 1) * wide]

    def slot_part(self, r, i):
        high, wide = self.size
        at = aligned(i, self.tile)
        return (pl.ds(r * high, high), at) if self.rows_first else (at, pl.ds(r * wide, wide))

    def part(self, ref, i):
        at = aligned(i, self.tile)
        return ref.at[:, at] if self.rows_first else ref.at[at, :]

    def view(self, ref, slot):
        return ref.at[slot, pl.ds(0, self.height), pl.ds(0, self.breadth)]

    def to_pair(self, r, i, slot):
        return pltpu.make_async_remote_copy(
            src_ref=self.view(self.stage, slot),
            dst_ref=self.base.at[self.slot_part(r, i)],
            send_sem=self.st_sem.at[slot],
            recv_sem=self.pair_recv.at[self.index, r],
            device_id=(self.chip * 2 + 1 - self.core, self.z),
            device_id_type=MESH,
        )

    def from_pair(self, r):
        return pltpu.make_async_remote_copy(
            src_ref=self.slot(r),
            dst_ref=self.slot(r),
            send_sem=self.st_sem.at[0],
            recv_sem=self.pair_recv.at[self.index, r],
            device_id=(self.chip * 2 + 1 - self.core, self.z),
            device_id_type=MESH,
        )

    def half(self, r, which):
        high, wide = self.size
        if self.rows_first:
            return self.base.at[pl.ds(r * high + which * (high // 2), high // 2), 0:wide]
        return self.base.at[pl.ds(which * (high // 2), high // 2), r * wide : (r + 1) * wide]

    def to_owner(self, r, which=None):
        high = self.size[0]
        at = (r - 1) if which is None else 2 * (r - 1) + which
        rows = pl.ds(0, high) if which is None else pl.ds(which * (high // 2), high // 2)
        return pltpu.make_async_remote_copy(
            src_ref=self.slot(r) if which is None else self.half(r, which),
            dst_ref=self.landing.at[r - 1, rows, :],
            send_sem=self.send.at[self.index, at],
            recv_sem=self.recv.at[self.index, at],
            device_id=(flip(self.chip, r) * 2 + self.core, self.z),
            device_id_type=MESH,
        )

    def to_relay(self, which):
        return pltpu.make_async_remote_copy(
            src_ref=self.half(3, which),
            dst_ref=self.relays.at[which],
            send_sem=self.r_send.at[self.index, which],
            recv_sem=self.r_recv.at[self.index, which],
            device_id=(flip(self.chip, 1 + which) * 2 + self.core, self.z),
            device_id_type=MESH,
        )

    def relay(self):
        if not self.relayed:
            return
        high, wide = self.size
        tall = high // 2 if self.rows_first else min(self.tile, high // 2)
        broad = self.tile if self.rows_first else wide
        pieces = wide // broad if self.rows_first else (high // 2) // tall
        for which in range(2):
            r = 2 - which
            self.to_relay(which).wait_recv()

            def fetch(i):
                rows = pl.ds(0, tall) if self.rows_first else aligned(i, tall)
                cols = aligned(i, broad) if self.rows_first else pl.ds(0, wide)
                slot = lax.rem(i, 2)
                return pltpu.make_async_copy(
                    self.relays.at[which, rows, cols],
                    self.stage.at[slot, pl.ds(0, tall), pl.ds(0, broad)],
                    self.r_load.at[slot],
                )

            def body(i, _):
                @pl.when(i + 1 < pieces)
                def _():
                    fetch(i + 1).start()

                fetch(i).wait()
                if self.rows_first:
                    at = (pl.ds(r * high + which * tall, tall), aligned(i, broad))
                else:
                    top = which * (high // 2)
                    at = (pl.ds(pl.multiple_of(top + i * tall, tall), tall), pl.ds(r * wide, wide))
                got = self.stage[lax.rem(i, 2), 0:tall, 0:broad].astype(F32)
                self.base[at] = (self.base[at].astype(F32) + got).astype(BF16)
                return 0

            fetch(0).start()
            lax.fori_loop(0, pieces, body, 0)
            self.to_owner(r, which).start()

    def to_out(self, i):
        source = self.wide.at[0 : self.height, 0 : self.breadth]
        return pltpu.make_async_copy(source, self.part(self.own_out, i), self.wide_sem)

    def partners(self, n):
        r = self.order[n]
        owner = flip(self.chip, r) * 2 + 1 - self.core

        def body(i, _):
            slot = lax.rem(n * self.tiles + i, 2)
            y = self.block(owner, i)
            if n * self.tiles >= 2:
                self.to_pair(r, i, slot).wait_send()
            else:

                @pl.when(n * self.tiles + i >= 2)
                def _():
                    self.to_pair(r, i, slot).wait_send()

            self.stage[slot, 0 : self.height, 0 : self.breadth] = y.astype(BF16)
            self.to_pair(r, i, slot).start()
            return 0

        lax.fori_loop(0, self.tiles, body, 0)

    def own(self, n):
        r = self.order[n]
        owner = flip(self.chip, r) * 2 + self.core
        self.from_pair(r).wait_recv()

        def body(i, _):
            y = self.block(owner, i)
            at = self.slot_part(r, i)
            y = y + self.base[at].astype(F32)
            if r:
                self.base[at] = y.astype(BF16)
            else:
                @pl.when(i >= 1)
                def _():
                    self.to_out(i).wait()

                self.wide[0 : self.height, 0 : self.breadth] = y
                self.to_out(i).start()
            return 0

        lax.fori_loop(0, self.tiles, body, 0)
        if r and not self.relayed:
            self.to_owner(r).start()
        elif r == 3:
            self.to_relay(0).start()
            self.to_relay(1).start()
        elif r:
            self.to_owner(r, r - 1).start()
        else:
            self.to_out(self.tiles - 1).wait()

    def run(self, before=lambda n: None):
        for n in range(self.chips):
            before(n)
            self.partners(n)
            if n:
                self.own(n - 1)
        self.own(self.chips - 1)
        self.drain()

    def drain(self):
        total = self.chips * self.tiles
        for i in range(max(total - 2, 0), total):
            self.to_pair(0, 0, i % 2).wait_send()

    def all(self):
        if self.relayed:
            return [self.to_owner(r, which) for r in (1, 2) for which in range(2)]
        return [self.to_owner(r) for r in range(1, self.chips)]

    def sent(self):
        for c in self.all() + ([self.to_relay(0), self.to_relay(1)] if self.relayed else []):
            c.wait_send()

    def finish(self):
        for c in self.all():
            c.wait_recv()


def piece_of(extent):
    return next(n for n in (512, 256, 128) if extent % n == 0)


def block_kernel(
    chips, count,
    x, gain, beta, bqkv, bf1, out_bias, seg_row, frequency, wq, wk, wv, wf1, wo, wf2, cot,
    block_out, input_grad, vec_out, own_qkv, own_f1, own_o, own_f2, land_qkv, land_f1, land_o, land_f2, hid_t, act_t, rel_qkv, rel_f1, rel_o, rel_f2,
    hid, vqkv, vf1, vf2, vo, qkv, att, att_t, lse, act, dg, g, stage, tab_c, tab_s, segs,
    dk_acc, dv_acc, k_t, up_buf, dn_buf, wide_row, wide_col, ig_stage, vec, vec_pair, vec_chip, vec_z,
    w_send, w_recv, r_send, r_recv, p_send, p_recv, own_sem,
    h_us, h_ur, h_ds, h_dr, c_us, c_ur, c_ds, c_dr, cot_sem, st_sem,
    act_sem, hid_sem, out_sem, ig_sem, st_row_sem, st_col_sem, pair_recv, x_send, x_recv, wide_row_sem, wide_col_sem, rl_send, rl_recv, rl_load,
    zo_us, zo_ur, zo_ds, zo_dr, zh_us, zh_ur, zh_ds, zh_dr, free_up, free_dn, pair_free, hid_free,
    v_ps, v_pr, v_cs, v_cr, v_zs, v_zr,
):
    z = lax.axis_index("branch")
    dp = lax.axis_index("dp")
    core, chip = lax.rem(dp, 2), lax.div(dp, 2)
    rows, width = x.shape
    length = rows * count
    hcols = wo.shape[0]
    units = wf2.shape[0]
    part_w = width // (2 * chips)
    last = count - 1
    sems = (w_send, w_recv, r_send, r_recv, p_send, p_recv, own_sem)
    g_qkv = [
        Gather(n, w, vqkv.at[:, n * hcols : (n + 1) * hcols], True, chips, sems) for n, w in enumerate((wq, wk, wv))
    ]
    g_f1 = Gather(3, wf1, vf1, True, chips, sems)
    g_o = Gather(4, wo, vo, False, chips, sems)
    g_f2 = Gather(5, wf2, vf2, False, chips, sems)
    h_chain = Chain(hid.at[aligned(z, rows), :], hid, rows, count, (h_us, h_ur, h_ds, h_dr), dp)
    c_chain = Chain(cot, g, rows, count, (c_us, c_ur, c_ds, c_dr), dp)
    part = hid
    act_v = vf2.at[0:units, width // 2 : width // 2 + length]

    def rows_of(ref, d):
        return ref.at[aligned(d, rows), :]

    fold_out = Fold((up_buf, dn_buf), (zo_us, zo_ur, zo_ds, zo_dr), count, dp)
    fold_hid = Fold((up_buf, dn_buf), (zh_us, zh_ur, zh_ds, zh_dr), count, dp)

    at_f1, at_ob, at_gain = 3 * hcols, 3 * hcols + units, 3 * hcols + units + width
    at_beta = at_gain + width

    def hand_over(free):
        pl.semaphore_signal(free, inc=1, device_id=(chip * 2 + 1 - core, z), device_id_type=MESH)
        pl.semaphore_wait(free, 1)

    sems_row = (st_row_sem, pair_recv, x_send, x_recv, wide_row_sem, rl_send, rl_recv, rl_load)
    sems_col = (st_col_sem, pair_recv, x_send, x_recv, wide_col_sem, rl_send, rl_recv, rl_load)
    tile_f2, tile_o = piece_of(units), piece_of(hcols)
    tile_f1, tile_qkv = piece_of(units), piece_of(3 * hcols)

    def f2_block(owner, i):
        return dot_nn(act_v[aligned(i, tile_f2), :], g[:, aligned(owner, part_w)])

    def o_block(owner, i):
        return dot_nn(att_t[aligned(i, tile_o), :], g[:, aligned(owner, part_w)])

    def hid_part(n):
        return vo.at[(n % 2) * part_w : (n % 2 + 1) * part_w, width // 2 : width // 2 + length]

    def hid_copy(n, owner):
        return pltpu.make_async_copy(hid_t.at[aligned(owner, part_w), :], hid_part(n), hid_sem.at[n % 2])

    state = {}

    def f1_block(owner, i):
        return dot_nn(hid_part(state["at"])[...], dg[:, aligned(i, tile_f1)])

    def qkv_block(owner, i):
        return dot_nn(hid_part(state["at"])[...], qkv[:, aligned(i, tile_qkv)])

    def run_rows(scatter, between=None):
        turns = [(True, 0)]
        for n in range(1, chips):
            turns += [(True, n), (False, n - 1)]
        turns.append((False, chips - 1))
        owners = [flip(chip, scatter.order[n]) * 2 + (1 - core if pair else core) for pair, n in turns]
        hid_copy(0, owners[0]).start()
        for i, (pair, n) in enumerate(turns):
            if i + 1 < len(turns):
                hid_copy(i + 1, owners[i + 1]).start()
            hid_copy(i, owners[i]).wait()
            state["at"] = i
            (scatter.partners if pair else scatter.own)(n)
            if between is not None and i == len(turns) // 2:
                between()
        scatter.drain()

    sc_f2 = Scatter(0, f2_block, tile_f2, False, vf2, (units, part_w), rel_f2, land_f2, own_f2, stage, wide_col, chips, sems_col)
    sc_f1 = Scatter(1, f1_block, tile_f1, True, act, (part_w, units), rel_f1, land_f1, own_f1, stage, wide_row, chips, sems_row)
    sc_o = Scatter(2, o_block, tile_o, False, vo, (hcols, part_w), rel_o, land_o, own_o, stage, wide_col, chips, sems_col)
    sc_qkv = Scatter(3, qkv_block, tile_qkv, True, hid, (part_w, 3 * hcols), rel_qkv, land_qkv, own_qkv, stage, wide_row, chips, sems_row)

    greet(chips, count)
    for gw in (*g_qkv, g_f1):
        gw.start()
    for gw in (*g_qkv, g_f1, g_o, g_f2):
        gw.start_pair()
    fetch_cot = pltpu.make_async_copy(cot, g.at[aligned(z, rows), :], cot_sem)
    fetch_cot.start()

    step_rows = 32

    def norm(i, _):
        part_rows = aligned(i, step_rows)
        inputs = x[part_rows, :].astype(F32)
        center = inputs - jnp.mean(inputs, axis=-1, keepdims=True)
        inverse = lax.rsqrt(jnp.mean(center * center, axis=-1, keepdims=True) + EPSILON)
        where = pl.ds(pl.multiple_of(z * rows + i * step_rows, step_rows), step_rows)
        hid[where, :] = (center * inverse * gain[...] + beta[...]).astype(BF16)
        return 0

    lax.fori_loop(0, rows // step_rows, norm, 0)
    h_chain.start()
    vec[...] = jnp.zeros_like(vec)

    row_segs = seg_row[...].astype(F32)
    places = lax.broadcasted_iota(jnp.int32, (1, length), 1).astype(F32)
    firsts = [
        jnp.min(jnp.where(row_segs == float(value), places, float(length)), axis=1, keepdims=True)
        for value in range(4)
    ]
    for c in range(length // LANES):
        here = slice(c * LANES, (c + 1) * LANES)
        seg = jnp.broadcast_to(row_segs[:, here], (LANES, LANES)).T
        segs[here, :] = seg.astype(BF16)
        start = jnp.zeros((LANES, LANES), F32)
        for value in range(4):
            start = jnp.where(seg == float(value), firsts[value], start)
        place = (lax.broadcasted_iota(jnp.int32, (LANES, LANES), 0) + c * LANES).astype(F32)
        angle = (place - start) * frequency[...]
        lane = lax.rem(lax.broadcasted_iota(jnp.int32, (LANES, LANES), 1), HEAD_DIM)
        sine = jnp.where(lane < ROT, jnp.sin(angle), 0.0)
        tab_c[here, :] = jnp.where(lane < ROT, jnp.cos(angle), 1.0)
        tab_s[here, :] = jnp.where(lane < ROT // 2, -sine, sine)
    key_row = jnp.where(row_segs == 0.0, -1.0, row_segs)

    for gw in g_qkv:
        gw.land()
    if count > 2:
        h_chain.pump(1)
    g_f1.land()
    for gw in (g_o, g_f2):
        gw.start()
    for s in range(2, count - 1):
        h_chain.pump(s)
    c_chain.start()
    for gw in g_qkv:
        gw.land_last()
    for gw in g_qkv:
        gw.arrive()

    ht, wt = tile_of(hcols), tile_of(width)

    def turn_copy(slot, j, cols_i):
        return pltpu.make_async_copy(
            stage.at[slot, pl.ds(0, wt), pl.ds(0, rows)], hid_t.at[cols_i, aligned(j, rows)], st_sem.at[slot]
        )

    def project(j):
        rows_j = aligned(j, rows)
        for which in range(3):
            for c in range(hcols // ht):
                at = which * hcols + c * ht
                y = dot_nn(hid[rows_j, :], vqkv[:, at : at + ht]) + bqkv[:, at : at + ht]
                for piece in range(ht // LANES):
                    part_y = y[:, piece * LANES : (piece + 1) * LANES]
                    if which < 2:
                        part_y = part_y * tab_c[rows_j, :] + swapped(part_y) * tab_s[rows_j, :]
                    low = part_y.astype(BF16)
                    if which == 0:
                        low = low * BF16(HEAD_DIM**-0.5)
                    qkv[rows_j, at + piece * LANES : at + (piece + 1) * LANES] = low

        def turn(i, _):
            cols_i, slot = aligned(i, wt), lax.rem(i, 2)

            @pl.when(i >= 2)
            def _():
                turn_copy(slot, j, cols_i).wait()

            stage[slot, 0:wt, 0:rows] = hid[rows_j, cols_i].T
            turn_copy(slot, j, cols_i).start()
            return 0

        n_turn = width // wt
        lax.fori_loop(0, n_turn, turn, 0)
        for i in range(max(n_turn - 2, 0), n_turn):
            turn_copy(i % 2, j, pl.ds(0, wt)).wait()

    h_chain.by_distance(0, 2 * count - 3, project)
    g_o.land()
    h_chain.by_distance(2 * count - 3, 2 * count - 1, project)
    g_f2.land()
    if count > 2:
        c_chain.pump(1)

    qb = tile_of(length, QBLOCK)
    pairs = hcols // LANES

    def attend(pair, _):
        cols = aligned(pair, LANES)
        k_cols, v_cols = aligned(pairs + pair, LANES), aligned(2 * pairs + pair, LANES)
        lane = lax.broadcasted_iota(jnp.int32, (1, LANES), 1)
        for b in range(length // qb):
            here = slice(b * qb, (b + 1) * qb)
            before = b * qb
            q2 = qkv[here, cols]
            seg_q = segs[here, 0:1].astype(F32)
            ki = lax.broadcasted_iota(jnp.int32, (qb, qb), 1)
            qi = lax.broadcasted_iota(jnp.int32, (qb, qb), 0)
            seen_here = jnp.logical_or(jnp.logical_and(seg_q == key_row[:, here], ki <= qi), ki == qi)
            out = jnp.zeros((qb, LANES), F32)
            stat = jnp.zeros((qb, LANES), F32)
            for h in range(2):
                mine = (lane // HEAD_DIM) == h
                qh = jnp.where(mine, q2, BF16(0))
                s_here = jnp.where(seen_here, dot_nt(qh, qkv[here, k_cols]), NEGATIVE)
                top = jnp.max(s_here, axis=-1, keepdims=True)
                if before:
                    s_before = jnp.where(
                        seg_q == key_row[:, :before], dot_nt(qh, qkv[:before, k_cols]), NEGATIVE
                    )
                    top = jnp.maximum(top, jnp.max(s_before, axis=-1, keepdims=True))
                e_here = jnp.exp(s_here - top)
                total = jnp.sum(e_here, axis=-1, keepdims=True)
                if before:
                    e_before = jnp.exp(s_before - top)
                    total = total + jnp.sum(e_before, axis=-1, keepdims=True)
                share = 1.0 / total
                o = dot_nn((e_here * share).astype(BF16), jnp.where(mine, qkv[here, v_cols], BF16(0)))
                if before:
                    o = o + dot_nn(
                        (e_before * share).astype(BF16), jnp.where(mine, qkv[:before, v_cols], BF16(0))
                    )
                out = out + o
                stat = jnp.where(mine, top + jnp.log(total), stat)
            att[here, cols] = out.astype(BF16)
            att_t[cols, here] = out.T.astype(BF16)
            turned = stat.T
            lse[pl.ds(2 * pair, 1), here] = turned[0:1, :]
            lse[pl.ds(2 * pair + 1, 1), here] = turned[HEAD_DIM : HEAD_DIM + 1, :]
        return 0

    half_pairs = pairs // 2
    lax.fori_loop(0, half_pairs, attend, 0)
    for s in range(2, count - 1):
        c_chain.pump(s)
    lax.fori_loop(half_pairs, pairs - 1, attend, 0)
    g_f1.land_last()
    lax.fori_loop(pairs - 1, pairs, attend, 0)
    g_f1.arrive()

    mt, ft = tile_of(length), tile_of(units)
    per_row = units // ft
    n_tiles = (length // mt) * per_row

    def staged(slot, rows_i, cols_i):
        return pltpu.make_async_copy(stage.at[slot, pl.ds(0, ft), :], act_t.at[cols_i, rows_i], st_sem.at[slot])

    def unit(i, _):
        rows_i, cols_i = aligned(lax.div(i, per_row), mt), aligned(lax.rem(i, per_row), ft)
        slot = lax.rem(i, 2)

        @pl.when(i >= 2)
        def _():
            staged(slot, rows_i, cols_i).wait()

        y = dot_nn(hid[rows_i, :], vf1[:, cols_i]) + bf1[:, cols_i]
        square = y * y
        t = jnp.tanh(GELU_C * (y + GELU_A * (y * square)))
        half = 0.5 * (1.0 + t)
        low = (y * half).astype(BF16)
        act[rows_i, cols_i] = low
        stage[slot, 0:ft, :] = low.T
        dg[rows_i, cols_i] = (
            half + 0.5 * y * (1.0 - t * t) * (GELU_C * (1.0 + 3.0 * GELU_A * square))
        ).astype(BF16)
        staged(slot, rows_i, cols_i).start()
        return 0

    half_tiles = n_tiles // 2
    lax.fori_loop(0, half_tiles, unit, 0)
    for gw in (g_o, g_f2):
        gw.land_last()
    lax.fori_loop(half_tiles, n_tiles, unit, 0)
    for i in range(max(n_tiles - 2, 0), n_tiles):
        staged(i % 2, pl.ds(0, mt), pl.ds(0, ft)).wait()
    for gw in (g_o, g_f2):
        gw.arrive()

    h_chain.finish()

    def output(i, _):
        rows_i, cols_i = aligned(lax.div(i, width // wt), mt), aligned(lax.rem(i, width // wt), wt)
        part[rows_i, cols_i] = (
            dot_nn(act[rows_i, :], vf2[:, cols_i]) + dot_nn(att[rows_i, :], vo[:, cols_i])
        ).astype(BF16)
        return 0

    lax.fori_loop(0, (length // mt) * (width // wt), output, 0)
    for st in range(count - 1):
        fold_out.first(True, st, rows_of(part, last - st))
        fold_out.first(False, st, rows_of(part, st))
    fetch_cot.wait()


    def unit_back(j):
        rows_j = aligned(j, rows)
        def body(i, _):
            cols_i = aligned(i, ft)
            low = (dot_nt(g[rows_j, :], vf2[cols_i, :]) * dg[rows_j, cols_i].astype(F32)).astype(BF16)
            dg[rows_j, cols_i] = low
            to = pl.ds(pl.multiple_of(at_f1 + i * ft, LANES), ft)
            vec[:, to] += jnp.sum(low.astype(F32), axis=0, keepdims=True)
            return 0

        lax.fori_loop(0, per_row, body, 0)
        att[rows_j, :] = dot_nt(g[rows_j, :], vo[...]).astype(BF16)
        vec[:, at_ob:at_gain] += jnp.sum(g[rows_j, :].astype(F32), axis=0, keepdims=True)

    c_chain.by_distance(0, 2 * count - 1, unit_back)
    g_o.finish()
    g_f2.finish()
    c_chain.finish()
    load_act = pltpu.make_async_copy(act_t, act_v, act_sem)
    load_act.start()
    hand_over(pair_free)
    own_part = lambda up, d: rows_of(part, d)
    load_act.wait()
    if count > 2:
        fold_out.pump(1, own_part, rows)
    sc_f2.run()
    sc_o.run()
    for k in range(2, count - 1):
        fold_out.pump(k, own_part, rows)


    def key_of(lo, hi):
        seg = segs[lo:hi, 0:1].astype(F32)
        return jnp.where(seg == 0.0, -1.0, seg)

    def turn_back(y, at):
        return y * tab_c[at, :] - swapped(y) * tab_s[at, :]

    def attend_back(pair, _):
        q_cols = aligned(pair, LANES)
        k_cols, v_cols = aligned(pairs + pair, LANES), aligned(2 * pairs + pair, LANES)
        lane = lax.broadcasted_iota(jnp.int32, (1, LANES), 1)
        dk_acc[...] = jnp.zeros_like(dk_acc)
        dv_acc[...] = jnp.zeros_like(dv_acc)
        k_t[...] = qkv[:, k_cols].T
        for b in range(length // qb):
            here, reach = slice(b * qb, (b + 1) * qb), (b + 1) * qb
            before = b * qb
            q2, g2 = qkv[here, q_cols], att[here, q_cols]
            ki = lax.broadcasted_iota(jnp.int32, (qb, qb), 0)
            qi = lax.broadcasted_iota(jnp.int32, (qb, qb), 1)
            seen_here = jnp.logical_or(
                jnp.logical_and(key_of(before, reach) == row_segs[:, here], ki <= qi), ki == qi
            )
            dq_t = []
            for h in range(2):
                mine = (lane // HEAD_DIM) == h
                qh, gh = jnp.where(mine, q2, BF16(0)), jnp.where(mine, g2, BF16(0))
                stat = lse[pl.ds(2 * pair + h, 1), here]
                spans = ([(0, before)] if before else []) + [(before, reach)]
                probs, grads = [], []
                delta = jnp.zeros((1, qb), F32)
                for lo, hi in spans:
                    seen = seen_here if lo == before else key_of(lo, hi) == row_segs[:, here]
                    p = jnp.exp(jnp.where(seen, dot_nt(qkv[lo:hi, k_cols], qh), NEGATIVE) - stat)
                    pg = dot_nt(qkv[lo:hi, v_cols], gh)
                    delta = delta + jnp.sum(p * pg, axis=0, keepdims=True)
                    probs.append(p)
                    grads.append(pg)
                acc = jnp.zeros((HEAD_DIM, qb), F32)
                for (lo, hi), p, pg in zip(spans, probs, grads):
                    sg = (p * (pg - delta)).astype(BF16)
                    dv_acc[lo:hi, :] += dot_nn(p.astype(BF16), gh)
                    dk_acc[lo:hi, :] += dot_nn(sg, qh)
                    acc = acc + dot_nn(k_t[h * HEAD_DIM : (h + 1) * HEAD_DIM, lo:hi], sg)
                dq_t.append(acc)
            dq = jnp.concatenate(dq_t, axis=0).T * HEAD_DIM**-0.5
            qkv[here, q_cols] = turn_back(dq, here).astype(BF16)
        for b in range(length // qb):
            here = slice(b * qb, (b + 1) * qb)
            qkv[here, k_cols] = turn_back(dk_acc[here, :], here).astype(BF16)
            qkv[here, v_cols] = dv_acc[here, :].astype(BF16)
        for cols in (q_cols, k_cols, v_cols):
            vec[:, cols] = jnp.sum(qkv[:, cols].astype(F32), axis=0, keepdims=True)
        return 0

    lax.fori_loop(0, pairs, attend_back, 0)

    def hidden_back(d):
        here = pl.ds(d * rows, rows)

        def body(i, _):
            cols_i = aligned(i, wt)
            g[here, cols_i] = (
                dot_nt(dg[here, :], vf1[cols_i, :]) + dot_nt(qkv[here, :], vqkv[cols_i, :])
            ).astype(BF16)
            return 0

        lax.fori_loop(0, width // wt, body, 0)

    def set_out(d):
        if d > 0:
            fold_hid.first(True, last - d, rows_of(g, d))
        if d < last:
            fold_hid.first(False, d, rows_of(g, d))

    dests = list(dict.fromkeys(d for both in zip(range(last, -1, -1), range(count)) for d in both))
    for d in dests[:2]:
        hidden_back(d)

    fold_out.arrive()
    def finish_output(i, _):
        part = aligned(i, 32)
        at = pl.ds(pl.multiple_of(z * rows + i * 32, 32), 32)
        y = fold_out.total(hid[at, :].astype(F32), part)
        hid[at, :] = (x[part, :].astype(F32) + y + out_bias[...]).astype(BF16)
        return 0

    lax.fori_loop(0, rows // 32, finish_output, 0)
    save_out = pltpu.make_async_copy(hid.at[aligned(z, rows), :], block_out, out_sem)
    save_out.start()
    fold_out.finish()

    @pl.when(z > 0)
    def _():
        pl.semaphore_signal(free_up, inc=1, device_id=(dp, z - 1), device_id_type=MESH)

    @pl.when(z < last)
    def _():
        pl.semaphore_signal(free_dn, inc=1, device_id=(dp, z + 1), device_id_type=MESH)

    @pl.when(z < last)
    def _():
        pl.semaphore_wait(free_up, 1)

    @pl.when(z > 0)
    def _():
        pl.semaphore_wait(free_dn, 1)

    for d in dests[:2]:
        set_out(d)
    sc_f2.relay()
    sc_o.relay()
    for d in dests[2:]:
        hidden_back(d)
        set_out(d)
    own_grad = lambda up, d: rows_of(g, d)

    def pump_hidden(lo, hi):
        for k in range(lo, hi):
            fold_hid.pump(k, own_grad, rows)

    pump_hidden(1, min(2, count - 1))
    run_rows(sc_f1)
    save_out.wait()
    hand_over(hid_free)
    run_rows(sc_qkv, lambda: pump_hidden(2, count - 1))
    sc_f1.relay()
    sc_f2.sent()
    load_cot = pltpu.make_async_copy(cot, vf2.at[0:rows, 0:width], cot_sem)
    load_cot.start()
    sc_qkv.relay()
    fold_hid.arrive()
    load_cot.wait()

    step_rows = 16

    def ig_copy(i, slot):
        return pltpu.make_async_copy(ig_stage.at[slot], input_grad.at[aligned(i, step_rows), :], ig_sem.at[slot])

    def norm_back(i, _):
        part = aligned(i, step_rows)
        slot = lax.rem(i, 2)
        inputs = x[part, :].astype(F32)
        center = inputs - jnp.mean(inputs, axis=-1, keepdims=True)
        inverse = lax.rsqrt(jnp.mean(center * center, axis=-1, keepdims=True) + EPSILON)
        normed = center * inverse
        own = g[pl.ds(pl.multiple_of(z * rows + i * step_rows, step_rows), step_rows), :].astype(F32)
        y = fold_hid.total(own, part)
        vec[:, at_gain : at_gain + width] += jnp.sum(y * normed, axis=0, keepdims=True)
        vec[:, at_beta : at_beta + width] += jnp.sum(y, axis=0, keepdims=True)
        scaled = y * gain[...]
        result = vf2[part, :].astype(F32) + inverse * (
            scaled
            - jnp.mean(scaled, axis=-1, keepdims=True)
            - normed * jnp.mean(scaled * normed, axis=-1, keepdims=True)
        )

        @pl.when(i >= 2)
        def _():
            ig_copy(i, slot).wait()

        ig_stage[slot] = result
        ig_copy(i, slot).start()
        return 0

    steps = rows // step_rows
    lax.fori_loop(0, steps, norm_back, 0)

    to_pair = pltpu.make_async_remote_copy(
        src_ref=vec, dst_ref=vec_pair, send_sem=v_ps, recv_sem=v_pr,
        device_id=(chip * 2 + 1 - core, z), device_id_type=MESH,
    )
    to_pair.start()
    for i in range(max(steps - 2, 0), steps):
        ig_copy(i, i % 2).wait()
    to_pair.wait()
    vec_chip[chip] = vec[...] + vec_pair[...]

    def chip_copy(r, slot):
        return pltpu.make_async_remote_copy(
            src_ref=vec_chip.at[chip], dst_ref=vec_chip.at[slot], send_sem=v_cs.at[r - 1], recv_sem=v_cr.at[r - 1],
            device_id=(flip(chip, r) * 2 + core, z), device_id_type=MESH,
        )

    for r in range(1, chips):
        chip_copy(r, chip).start()
    for r in range(1, chips):
        chip_copy(r, flip(chip, r)).wait_recv()
    total = vec_chip[0]
    for c in range(1, chips):
        total = total + vec_chip[c]
    vec_out[:, 0:at_gain] = total[:, 0:at_gain]
    vec_z[z] = total[:, at_gain:]

    def z_copy(shift, slot):
        return pltpu.make_async_remote_copy(
            src_ref=vec_z.at[z], dst_ref=vec_z.at[slot], send_sem=v_zs.at[shift - 1], recv_sem=v_zr.at[shift - 1],
            device_id=(dp, lax.rem(z + shift, count)), device_id_type=MESH,
        )

    for shift in range(1, count):
        z_copy(shift, z).start()
    for shift in range(1, count):
        z_copy(shift, lax.rem(z + count - shift, count)).wait_recv()
    total = vec_z[0]
    for n in range(1, count):
        total = total + vec_z[n]
    vec_out[:, at_gain:] = total
    for r in range(1, chips):
        chip_copy(r, chip).wait_send()
    for shift in range(1, count):
        z_copy(shift, z).wait_send()
    fold_hid.finish()
    for s in (sc_f1, sc_o, sc_qkv):
        s.sent()
    for s in (sc_f2, sc_f1, sc_o, sc_qkv):
        s.finish()
    for gw in (*g_qkv, g_f1):
        gw.finish()


def run_block(ndp, count, x, gain, beta, bqkv, bf1, out_bias, seg_row, frequency, wq, wk, wv, wf1, wo, wf2, cot):
    chips = ndp // 2
    rows, width = x.shape
    length = rows * count
    hcols, units = wo.shape[0], wf2.shape[0]
    part_w = width // ndp
    total = 3 * hcols + units + 3 * width
    lands = 2 if chips == 4 else chips - 1
    heads = hcols // HEAD_DIM
    mt, ft, wt = tile_of(length), tile_of(units), tile_of(width)
    anywhere = pl.BlockSpec(memory_space=pl.ANY)
    vmem = pl.BlockSpec(memory_space=pltpu.VMEM)
    low = lambda *shape: jax.ShapeDtypeStruct(shape, BF16)
    wide = lambda *shape: jax.ShapeDtypeStruct(shape, F32)
    outs = [
        low(rows, width), wide(rows, width), wide(1, total),
        wide(part_w, 3 * hcols), wide(part_w, units), wide(hcols, part_w), wide(units, part_w),
        low(lands, part_w, 3 * hcols), low(lands, part_w, units), low(lands, hcols, part_w), low(lands, units, part_w),
        low(width, length), low(units, length),
        low(2, part_w // 2, 3 * hcols), low(2, part_w // 2, units), low(2, hcols // 2, part_w), low(2, units // 2, part_w),
    ]
    v = lambda *shape: pltpu.VMEM(shape, BF16)
    w = lambda *shape: pltpu.VMEM(shape, F32)
    steps = max(count - 1, 1)
    dma = lambda *shape: pltpu.SemaphoreType.DMA(shape)
    one, plain = pltpu.SemaphoreType.DMA, pltpu.SemaphoreType.REGULAR
    row_tile = max(piece_of(units), piece_of(3 * hcols))
    col_tile = max(piece_of(units), piece_of(hcols))
    scratch = [
        v(length, width), v(width, 3 * hcols), v(width, units), v(units, width), v(hcols, width),
        v(length, 3 * hcols), v(length, hcols), v(hcols, length), w(heads, length), v(length, units), v(length, units),
        v(length, width), v(2, max(ft, wt, part_w), max(mt, part_w)), w(length, LANES), w(length, LANES), v(length, LANES),
        w(length, LANES), w(length, LANES), v(LANES, length), v(steps, rows, width), v(steps, rows, width),
        w(part_w, row_tile), w(col_tile, part_w),
        w(2, 16, width), w(1, total), w(1, total), w(chips, 1, total), w(count, 1, 2 * width),
        dma(6, chips - 1), dma(6, chips - 1), dma(6, 2), dma(6, 2), dma(6, chips), dma(6, chips), dma(6),
        *[dma(steps) for _ in range(8)], one, dma(2),
        one, dma(2), one, dma(2), dma(2), dma(2),
        dma(4, chips), dma(4, max(chips - 1, 4)), dma(4, max(chips - 1, 4)), one, one, dma(4, 2), dma(4, 2), dma(2),
        *[dma(steps, 2) for _ in range(8)], plain, plain, plain, plain,
        one, one, dma(chips - 1), dma(chips - 1), dma(steps), dma(steps),
    ]
    return pl.pallas_call(
        functools.partial(block_kernel, chips, count),
        out_shape=outs,
        in_specs=[vmem] * 8 + [anywhere] * 7,
        out_specs=[anywhere, anywhere, vmem] + [anywhere] * 14,
        scratch_shapes=scratch,
        compiler_params=pltpu.CompilerParams(
            collective_id=0, has_side_effects=True, vmem_limit_bytes=VMEM_LIMIT
        ),
        name="block_step",
    )(x, gain, beta, bqkv, bf1, out_bias, seg_row, frequency, wq, wk, wv, wf1, wo, wf2, cot)[:11]


def on_device(
    ndp, count,
    block_input, segment_ids, out_cotangent, norm_gain, norm_bias, query_weight, key_weight, value_weight,
    query_bias, key_bias, value_bias, out_weight, fc1_weight, fc1_bias, fc2_weight, output_bias,
):
    x = block_input[0]
    cot = out_cotangent[0]
    width = x.shape[1]
    half_rot = ROT // 2
    frequency = 10000.0 ** (-2.0 * (jnp.arange(LANES, dtype=jnp.int32) % half_rot).astype(F32) / ROT)
    bqkv = jnp.concatenate([query_bias, key_bias, value_bias])[None, :]
    gain, seg_row = norm_gain[None, :], segment_ids
    (block_output, input_grad, vec, own_qkv, own_f1, own_o, own_f2, land_qkv, land_f1, land_o, land_f2) = run_block(
        ndp, count, x, gain, norm_bias[None, :], bqkv, fc1_bias[None, :], output_bias[None, :], seg_row,
        frequency[None, :], query_weight, key_weight, value_weight, fc1_weight, out_weight, fc2_weight, cot,
    )
    hcols, units = out_weight.shape[0], fc2_weight.shape[0]

    def summed(own, landed):
        for n in range(landed.shape[0]):
            own = own + landed[n].astype(F32)
        return own

    def third(i):
        cols = slice(i * hcols, (i + 1) * hcols)
        return summed(own_qkv[:, cols], land_qkv[:, :, cols])

    sizes = (hcols, hcols, hcols, units, width, width, width)
    pieces, at = [], 0
    for size in sizes:
        pieces.append(vec[0, at : at + size])
        at += size
    qb, kb, vb, f1b, ob, gain_grad, beta_grad = pieces
    return (
        block_output[None], input_grad[None], gain_grad, beta_grad,
        third(0), third(1), third(2), qb, kb, vb,
        summed(own_o, land_o), summed(own_f1, land_f1), f1b, summed(own_f2, land_f2), ob,
    )


def solution(mesh):
    tokens, vector, split = P("dp", "branch", None), P(), P("branch")
    rows_first, cols_first = P("dp", "branch"), P("branch", "dp")
    in_specs = (
        tokens, P("dp", None), tokens, vector, vector, rows_first, rows_first, rows_first,
        split, split, split, cols_first, rows_first, split, cols_first, vector,
    )
    out_specs = (
        tokens, tokens, vector, vector, rows_first, rows_first, rows_first, split, split, split,
        cols_first, rows_first, split, cols_first, vector,
    )
    return jax.shard_map(
        functools.partial(on_device, mesh.shape["dp"], mesh.shape["branch"]),
        mesh=mesh, in_specs=in_specs, out_specs=out_specs, check_vma=False,
    )
```

```python
import functools

import jax
import jax.numpy as jnp
from jax import lax
from jax.experimental import pallas as pl
from jax.experimental.pallas import tpu as pltpu
from jax.sharding import PartitionSpec as P

HEAD_DIM = 64
ROT = 32
EPSILON = 1e-05
NEGATIVE = -1e30
LANES = 128
TILE = 512
QBLOCK = 256
MESH = pl.DeviceIdType.MESH
BF16 = jnp.bfloat16
F32 = jnp.float32
GELU_C = 0.7978845608028654
GELU_A = 0.044715
VMEM_LIMIT = 63 * 1024 * 1024 + 832 * 1024


def flip(index, bits):
    out = index
    bit = 1
    while bit <= bits:
        if bits & bit:
            out = out + bit * (1 - 2 * lax.rem(lax.div(index, bit), 2))
        bit *= 2
    return out


def dot_nn(left, right):
    return jnp.dot(left, right, preferred_element_type=F32)


def dot_nt(left, right):
    return lax.dot_general(left, right, (((1,), (1,)), ((), ())), preferred_element_type=F32)


def tile_of(extent, most=TILE):
    return min(most, extent)


def aligned(index, step):
    return pl.ds(pl.multiple_of(index * step, step), step)


class Chain:
    def __init__(self, own_src, buf, rows, count, sems, dp):
        self.own_src, self.buf, self.rows, self.count = own_src, buf, rows, count
        self.sems, self.dp = sems, dp
        self.z = lax.axis_index("branch")

    def block(self, slot):
        return self.buf.at[aligned(slot, self.rows), :]

    def copy(self, up, step, slot, src=None):
        send, recv = self.sems[0 if up else 2], self.sems[1 if up else 3]
        return pltpu.make_async_remote_copy(
            src_ref=self.block(slot) if src is None else src,
            dst_ref=self.block(slot),
            send_sem=send.at[step],
            recv_sem=recv.at[step],
            device_id=(self.dp, self.z + 1 if up else self.z - 1),
            device_id_type=MESH,
        )

    def sends(self, up, step):
        z, last = self.z, self.count - 1
        if up:
            return jnp.logical_and(z >= step, z < last)
        return jnp.logical_and(z + step <= last, z > 0)

    def sent_slot(self, up, step):
        return self.z - step if up else self.z + step

    def start(self):
        for up in (False, True):

            @pl.when(self.sends(up, 0))
            def _(up=up):
                self.copy(up, 0, self.z, self.own_src).start()

    def pump(self, step):
        for up in (False, True):

            @pl.when(self.sends(up, step))
            def _(up=up):
                slot = self.sent_slot(up, step)
                self.copy(up, step - 1, slot).wait_recv()
                self.copy(up, step, slot).start()

    def by_distance(self, first, end, work):
        def visit(i, _):
            far = lax.div(i + 1, 2)
            above = lax.rem(i, 2) == 0
            slot = self.z + jnp.where(above, far, -far)

            @pl.when(jnp.logical_and(slot >= 0, slot <= self.count - 1))
            def _():
                for up in (False, True):
                    mine = jnp.logical_and(far > 0, above if not up else jnp.logical_not(above))

                    @pl.when(jnp.logical_and(mine, jnp.logical_not(self.sends(up, far))))
                    def _(up=up):
                        self.copy(up, far - 1, slot).wait_recv()

                work(slot)

            return 0

        lax.fori_loop(first, end, visit, 0)

    def finish(self):
        for step in range(self.count - 1):
            for up in (False, True):

                @pl.when(self.sends(up, step))
                def _(up=up, step=step):
                    self.copy(up, step, self.sent_slot(up, step), self.own_src if step == 0 else None).wait_send()


class Gather:
    def __init__(self, index, shard, full, by_rows, chips, sems):
        self.index, self.shard, self.full = index, shard, full
        self.by_rows, self.chips = by_rows, chips
        self.send, self.recv, self.relay_send, self.relay_recv, self.pair_send, self.pair_recv, self.own = sems
        dp = lax.axis_index("dp")
        self.z = lax.axis_index("branch")
        self.core = lax.rem(dp, 2)
        self.chip = lax.div(dp, 2)
        self.width = shard.shape[0 if by_rows else 1]
        self.relayed = chips == 4
        self.direct = (1, 2) if self.relayed else tuple(range(1, chips))

    def slot(self, dp):
        part = aligned(dp, self.width)
        return self.full.at[part, :] if self.by_rows else self.full.at[:, part]

    def half(self, dp, which):
        if self.by_rows:
            return self.full.at[aligned(2 * dp + which, self.width // 2), :]
        rows = self.shard.shape[0] // 2
        return self.full.at[pl.ds(which * rows, rows), aligned(dp, self.width)]

    def at(self, r, core):
        return flip(self.chip, r) * 2 + core

    def to_chip(self, r, landing):
        return pltpu.make_async_remote_copy(
            src_ref=self.shard,
            dst_ref=self.slot(landing),
            send_sem=self.send.at[self.index, r - 1],
            recv_sem=self.recv.at[self.index, r - 1],
            device_id=(self.at(r, self.core), self.z),
            device_id_type=MESH,
        )

    def relay(self, which, owner):
        return pltpu.make_async_remote_copy(
            src_ref=self.half(owner, which),
            dst_ref=self.half(owner, which),
            send_sem=self.relay_send.at[self.index, which],
            recv_sem=self.relay_recv.at[self.index, which],
            device_id=(self.at(2 - which, self.core), self.z),
            device_id_type=MESH,
        )

    def to_pair(self, r, landing):
        return pltpu.make_async_remote_copy(
            src_ref=self.shard if r == 0 else self.slot(self.at(r, self.core)),
            dst_ref=self.slot(landing),
            send_sem=self.pair_send.at[self.index, r],
            recv_sem=self.pair_recv.at[self.index, r],
            device_id=(self.chip * 2 + 1 - self.core, self.z),
            device_id_type=MESH,
        )

    def fetch(self):
        return pltpu.make_async_copy(self.shard, self.slot(self.at(0, self.core)), self.own.at[self.index])

    def start(self):
        for r in self.direct:
            self.to_chip(r, self.at(0, self.core)).start()

    def start_pair(self):
        self.to_pair(0, self.at(0, self.core)).start()
        self.fetch().start()

    def land(self):
        for r in self.direct:
            owner = self.at(r, self.core)
            self.to_chip(r, owner).wait_recv()
            if self.relayed:
                self.relay(r - 1, owner).start()
            self.to_pair(r, owner).start()

    def land_last(self):
        if self.relayed:
            owner = self.at(3, self.core)
            for which in range(2):
                self.relay(which, owner).wait_recv()
            self.to_pair(3, owner).start()

    def arrive(self):
        self.fetch().wait()
        for r in range(self.chips):
            self.to_pair(r, self.at(r, 1 - self.core)).wait_recv()

    def finish(self):
        for r in self.direct:
            self.to_chip(r, self.at(0, self.core)).wait_send()
            if self.relayed:
                self.relay(r - 1, self.at(r, self.core)).wait_send()
        for r in range(self.chips):
            self.to_pair(r, self.at(r, self.core)).wait_send()


def greet(chips, count):
    dp, z = lax.axis_index("dp"), lax.axis_index("branch")
    core, chip = lax.rem(dp, 2), lax.div(dp, 2)
    barrier = pltpu.get_barrier_semaphore()
    for r in range(1, chips):
        pl.semaphore_signal(barrier, inc=1, device_id=(flip(chip, r) * 2 + core, z), device_id_type=MESH)
    pl.semaphore_signal(barrier, inc=1, device_id=(chip * 2 + 1 - core, z), device_id_type=MESH)
    for shift in range(1, count):
        pl.semaphore_signal(barrier, inc=1, device_id=(dp, lax.rem(z + shift, count)), device_id_type=MESH)
    pl.semaphore_wait(barrier, chips + count - 1)


def swapped(y):
    lane = lax.rem(lax.broadcasted_iota(jnp.int32, y.shape, 1), HEAD_DIM)
    return jnp.where(lane < ROT // 2, pltpu.roll(y, LANES - ROT // 2, 1), pltpu.roll(y, ROT // 2, 1))


class Fold:
    def __init__(self, bufs, sems, count, dp):
        self.bufs, self.sems, self.count, self.dp = bufs, sems, count, dp
        self.z = lax.axis_index("branch")

    def place(self, up):
        return self.z if up else self.count - 1 - self.z

    def dest(self, up, step):
        return self.count - 1 - step if up else step

    def hop(self, up, step, half, src=None):
        buf = self.bufs[0 if up else 1]
        send, recv = self.sems[0 if up else 2], self.sems[1 if up else 3]
        rows = pl.ds(half * (buf.shape[1] // 2), buf.shape[1] // 2)
        return pltpu.make_async_remote_copy(
            src_ref=buf.at[step, rows, :] if src is None else src.at[rows, :],
            dst_ref=buf.at[step, rows, :],
            send_sem=send.at[step, half],
            recv_sem=recv.at[step, half],
            device_id=(self.dp, self.z + 1 if up else self.z - 1),
            device_id_type=MESH,
        )

    def first(self, up, step, src):
        @pl.when(self.place(up) == 0)
        def _():
            for half in range(2):
                self.hop(up, step, half, src).start()

    def pump(self, k, own_block, rows):
        for up in (False, True):
            place = self.place(up)

            @pl.when(jnp.logical_and(place >= 1, place <= k))
            def _(up=up, place=place):
                step = k - place
                own = own_block(up, self.dest(up, step))
                buf = self.bufs[0 if up else 1]
                for half in range(2):
                    self.hop(up, step, half).wait_recv()

                    def add(i, _):
                        part = aligned(i, 32)
                        buf[step, part, :] = (buf[step, part, :].astype(F32) + own[part, :].astype(F32)).astype(BF16)
                        return 0

                    lax.fori_loop(half * (rows // 64), (half + 1) * (rows // 64), add, 0)
                    self.hop(up, step, half).start()

    def last_step(self, up):
        return jnp.clip(self.count - 1 - self.place(up), 0, self.count - 2)

    def arrive(self):
        for up in (False, True):

            @pl.when(self.place(up) >= 1)
            def _(up=up):
                for half in range(2):
                    self.hop(up, self.last_step(up), half).wait_recv()

    def total(self, own, part):
        out = own
        for up in (False, True):
            got = self.bufs[0 if up else 1][self.last_step(up), part, :].astype(F32)
            out = out + jnp.where(self.place(up) >= 1, got, 0.0)
        return out

    def finish(self):
        for step in range(self.count - 1):
            for up in (False, True):

                @pl.when(self.place(up) + step <= self.count - 2)
                def _(up=up, step=step):
                    for half in range(2):
                        self.hop(up, step, half).wait_send()


class Scatter:
    def __init__(self, index, block, tile, rows_first, base, size, relays, landing, own_out, stage, wide, chips, sems):
        self.index, self.block, self.tile, self.rows_first = index, block, tile, rows_first
        self.base, self.size, self.landing, self.own_out = base, size, landing, own_out
        self.stage, self.wide = stage, wide
        self.chips = chips
        self.relays = relays
        self.st_sem, self.pair_recv, self.send, self.recv, self.wide_sem, self.r_send, self.r_recv, self.r_load = sems
        dp = lax.axis_index("dp")
        self.z = lax.axis_index("branch")
        self.core, self.chip = lax.rem(dp, 2), lax.div(dp, 2)
        self.tiles = size[1 if rows_first else 0] // tile
        self.height = size[0] if rows_first else tile
        self.breadth = tile if rows_first else size[1]
        self.relayed = chips == 4
        self.order = [3, 1, 2, 0] if self.relayed else [*range(1, chips), 0]

    def slot(self, r):
        high, wide = self.size
        if self.rows_first:
            return self.base.at[r * high : (r + 1) * high, 0:wide]
        return self.base.at[0:high, r * wide : (r + 1) * wide]

    def slot_part(self, r, i):
        high, wide = self.size
        at = aligned(i, self.tile)
        return (pl.ds(r * high, high), at) if self.rows_first else (at, pl.ds(r * wide, wide))

    def part(self, ref, i):
        at = aligned(i, self.tile)
        return ref.at[:, at] if self.rows_first else ref.at[at, :]

    def view(self, ref, slot):
        return ref.at[slot, pl.ds(0, self.height), pl.ds(0, self.breadth)]

    def to_pair(self, r, i, slot):
        return pltpu.make_async_remote_copy(
            src_ref=self.view(self.stage, slot),
            dst_ref=self.base.at[self.slot_part(r, i)],
            send_sem=self.st_sem.at[slot],
            recv_sem=self.pair_recv.at[self.index, r],
            device_id=(self.chip * 2 + 1 - self.core, self.z),
            device_id_type=MESH,
        )

    def from_pair(self, r):
        return pltpu.make_async_remote_copy(
            src_ref=self.slot(r),
            dst_ref=self.slot(r),
            send_sem=self.st_sem.at[0],
            recv_sem=self.pair_recv.at[self.index, r],
            device_id=(self.chip * 2 + 1 - self.core, self.z),
            device_id_type=MESH,
        )

    def half(self, r, which):
        high, wide = self.size
        if self.rows_first:
            return self.base.at[pl.ds(r * high + which * (high // 2), high // 2), 0:wide]
        return self.base.at[pl.ds(which * (high // 2), high // 2), r * wide : (r + 1) * wide]

    def to_owner(self, r, which=None):
        high = self.size[0]
        at = (r - 1) if which is None else 2 * (r - 1) + which
        rows = pl.ds(0, high) if which is None else pl.ds(which * (high // 2), high // 2)
        return pltpu.make_async_remote_copy(
            src_ref=self.slot(r) if which is None else self.half(r, which),
            dst_ref=self.landing.at[r - 1, rows, :],
            send_sem=self.send.at[self.index, at],
            recv_sem=self.recv.at[self.index, at],
            device_id=(flip(self.chip, r) * 2 + self.core, self.z),
            device_id_type=MESH,
        )

    def to_relay(self, which):
        return pltpu.make_async_remote_copy(
            src_ref=self.half(3, which),
            dst_ref=self.relays.at[which],
            send_sem=self.r_send.at[self.index, which],
            recv_sem=self.r_recv.at[self.index, which],
            device_id=(flip(self.chip, 1 + which) * 2 + self.core, self.z),
            device_id_type=MESH,
        )

    def relay(self):
        if not self.relayed:
            return
        high, wide = self.size
        tall = high // 2 if self.rows_first else min(self.tile, high // 2)
        broad = self.tile if self.rows_first else wide
        pieces = wide // broad if self.rows_first else (high // 2) // tall
        for which in range(2):
            r = 2 - which
            self.to_relay(which).wait_recv()

            def fetch(i):
                rows = pl.ds(0, tall) if self.rows_first else aligned(i, tall)
                cols = aligned(i, broad) if self.rows_first else pl.ds(0, wide)
                slot = lax.rem(i, 2)
                return pltpu.make_async_copy(
                    self.relays.at[which, rows, cols],
                    self.stage.at[slot, pl.ds(0, tall), pl.ds(0, broad)],
                    self.r_load.at[slot],
                )

            def body(i, _):
                @pl.when(i + 1 < pieces)
                def _():
                    fetch(i + 1).start()

                fetch(i).wait()
                if self.rows_first:
                    at = (pl.ds(r * high + which * tall, tall), aligned(i, broad))
                else:
                    top = which * (high // 2)
                    at = (pl.ds(pl.multiple_of(top + i * tall, tall), tall), pl.ds(r * wide, wide))
                got = self.stage[lax.rem(i, 2), 0:tall, 0:broad].astype(F32)
                self.base[at] = (self.base[at].astype(F32) + got).astype(BF16)
                return 0

            fetch(0).start()
            lax.fori_loop(0, pieces, body, 0)
            self.to_owner(r, which).start()

    def to_out(self, i):
        source = self.wide.at[0 : self.height, 0 : self.breadth]
        return pltpu.make_async_copy(source, self.part(self.own_out, i), self.wide_sem)

    def partners(self, n):
        r = self.order[n]
        owner = flip(self.chip, r) * 2 + 1 - self.core

        def body(i, _):
            slot = lax.rem(n * self.tiles + i, 2)
            y = self.block(owner, i)
            if n * self.tiles >= 2:
                self.to_pair(r, i, slot).wait_send()
            else:

                @pl.when(n * self.tiles + i >= 2)
                def _():
                    self.to_pair(r, i, slot).wait_send()

            self.stage[slot, 0 : self.height, 0 : self.breadth] = y.astype(BF16)
            self.to_pair(r, i, slot).start()
            return 0

        lax.fori_loop(0, self.tiles, body, 0)

    def own(self, n):
        r = self.order[n]
        owner = flip(self.chip, r) * 2 + self.core
        self.from_pair(r).wait_recv()

        def body(i, _):
            y = self.block(owner, i)
            at = self.slot_part(r, i)
            y = y + self.base[at].astype(F32)
            if r:
                self.base[at] = y.astype(BF16)
            else:
                @pl.when(i >= 1)
                def _():
                    self.to_out(i).wait()

                self.wide[0 : self.height, 0 : self.breadth] = y
                self.to_out(i).start()
            return 0

        lax.fori_loop(0, self.tiles, body, 0)
        if r and not self.relayed:
            self.to_owner(r).start()
        elif r == 3:
            self.to_relay(0).start()
            self.to_relay(1).start()
        elif r:
            self.to_owner(r, r - 1).start()
        else:
            self.to_out(self.tiles - 1).wait()

    def run(self, before=lambda n: None):
        for n in range(self.chips):
            before(n)
            self.partners(n)
            if n:
                self.own(n - 1)
        self.own(self.chips - 1)
        self.drain()

    def drain(self):
        total = self.chips * self.tiles
        for i in range(max(total - 2, 0), total):
            self.to_pair(0, 0, i % 2).wait_send()

    def all(self):
        if self.relayed:
            return [self.to_owner(r, which) for r in (1, 2) for which in range(2)]
        return [self.to_owner(r) for r in range(1, self.chips)]

    def sent(self):
        for c in self.all() + ([self.to_relay(0), self.to_relay(1)] if self.relayed else []):
            c.wait_send()

    def finish(self):
        for c in self.all():
            c.wait_recv()


def piece_of(extent):
    return next(n for n in (512, 256, 128) if extent % n == 0)


def block_kernel(
    chips, count,
    x, gain, beta, bqkv, bf1, out_bias, seg_row, frequency, wq, wk, wv, wf1, wo, wf2, cot,
    block_out, input_grad, vec_out, own_qkv, own_f1, own_o, own_f2, land_qkv, land_f1, land_o, land_f2, hid_t, act_t, rel_qkv, rel_f1, rel_o, rel_f2,
    hid, vqkv, vf1, vf2, vo, qkv, att, att_t, lse, act, dg, g, stage, tab_c, tab_s, segs,
    dk_acc, dv_acc, k_t, up_buf, dn_buf, wide_row, wide_col, ig_stage, vec, vec_pair, vec_chip, vec_z,
    w_send, w_recv, r_send, r_recv, p_send, p_recv, own_sem,
    h_us, h_ur, h_ds, h_dr, c_us, c_ur, c_ds, c_dr, cot_sem, st_sem,
    act_sem, hid_sem, out_sem, ig_sem, st_row_sem, st_col_sem, pair_recv, x_send, x_recv, wide_row_sem, wide_col_sem, rl_send, rl_recv, rl_load,
    zo_us, zo_ur, zo_ds, zo_dr, zh_us, zh_ur, zh_ds, zh_dr, free_up, free_dn, pair_free, hid_free,
    v_ps, v_pr, v_cs, v_cr, v_zs, v_zr,
):
    z = lax.axis_index("branch")
    dp = lax.axis_index("dp")
    core, chip = lax.rem(dp, 2), lax.div(dp, 2)
    rows, width = x.shape
    length = rows * count
    hcols = wo.shape[0]
    units = wf2.shape[0]
    part_w = width // (2 * chips)
    last = count - 1
    sems = (w_send, w_recv, r_send, r_recv, p_send, p_recv, own_sem)
    g_qkv = [
        Gather(n, w, vqkv.at[:, n * hcols : (n + 1) * hcols], True, chips, sems) for n, w in enumerate((wq, wk, wv))
    ]
    g_f1 = Gather(3, wf1, vf1, True, chips, sems)
    g_o = Gather(4, wo, vo, False, chips, sems)
    g_f2 = Gather(5, wf2, vf2, False, chips, sems)
    h_chain = Chain(hid.at[aligned(z, rows), :], hid, rows, count, (h_us, h_ur, h_ds, h_dr), dp)
    c_chain = Chain(cot, g, rows, count, (c_us, c_ur, c_ds, c_dr), dp)
    part = hid
    act_v = vf2.at[0:units, width // 2 : width // 2 + length]

    def rows_of(ref, d):
        return ref.at[aligned(d, rows), :]

    fold_out = Fold((up_buf, dn_buf), (zo_us, zo_ur, zo_ds, zo_dr), count, dp)
    fold_hid = Fold((up_buf, dn_buf), (zh_us, zh_ur, zh_ds, zh_dr), count, dp)

    at_f1, at_ob, at_gain = 3 * hcols, 3 * hcols + units, 3 * hcols + units + width
    at_beta = at_gain + width

    def hand_over(free):
        pl.semaphore_signal(free, inc=1, device_id=(chip * 2 + 1 - core, z), device_id_type=MESH)
        pl.semaphore_wait(free, 1)

    sems_row = (st_row_sem, pair_recv, x_send, x_recv, wide_row_sem, rl_send, rl_recv, rl_load)
    sems_col = (st_col_sem, pair_recv, x_send, x_recv, wide_col_sem, rl_send, rl_recv, rl_load)
    tile_f2, tile_o = piece_of(units), piece_of(hcols)
    tile_f1, tile_qkv = piece_of(units), piece_of(3 * hcols)

    def f2_block(owner, i):
        return dot_nn(act_v[aligned(i, tile_f2), :], g[:, aligned(owner, part_w)])

    def o_block(owner, i):
        return dot_nn(att_t[aligned(i, tile_o), :], g[:, aligned(owner, part_w)])

    def hid_part(n):
        return vo.at[(n % 2) * part_w : (n % 2 + 1) * part_w, width // 2 : width // 2 + length]

    def hid_copy(n, owner):
        return pltpu.make_async_copy(hid_t.at[aligned(owner, part_w), :], hid_part(n), hid_sem.at[n % 2])

    state = {}

    def f1_block(owner, i):
        return dot_nn(hid_part(state["at"])[...], dg[:, aligned(i, tile_f1)])

    def qkv_block(owner, i):
        return dot_nn(hid_part(state["at"])[...], qkv[:, aligned(i, tile_qkv)])

    def run_rows(scatter, between=None):
        turns = [(True, 0)]
        for n in range(1, chips):
            turns += [(True, n), (False, n - 1)]
        turns.append((False, chips - 1))
        owners = [flip(chip, scatter.order[n]) * 2 + (1 - core if pair else core) for pair, n in turns]
        hid_copy(0, owners[0]).start()
        for i, (pair, n) in enumerate(turns):
            if i + 1 < len(turns):
                hid_copy(i + 1, owners[i + 1]).start()
            hid_copy(i, owners[i]).wait()
            state["at"] = i
            (scatter.partners if pair else scatter.own)(n)
            if between is not None and i == len(turns) // 2:
                between()
        scatter.drain()

    sc_f2 = Scatter(0, f2_block, tile_f2, False, vf2, (units, part_w), rel_f2, land_f2, own_f2, stage, wide_col, chips, sems_col)
    sc_f1 = Scatter(1, f1_block, tile_f1, True, act, (part_w, units), rel_f1, land_f1, own_f1, stage, wide_row, chips, sems_row)
    sc_o = Scatter(2, o_block, tile_o, False, vo, (hcols, part_w), rel_o, land_o, own_o, stage, wide_col, chips, sems_col)
    sc_qkv = Scatter(3, qkv_block, tile_qkv, True, hid, (part_w, 3 * hcols), rel_qkv, land_qkv, own_qkv, stage, wide_row, chips, sems_row)

    greet(chips, count)
    for gw in (*g_qkv, g_f1):
        gw.start()
    for gw in (*g_qkv, g_f1, g_o, g_f2):
        gw.start_pair()
    fetch_cot = pltpu.make_async_copy(cot, g.at[aligned(z, rows), :], cot_sem)
    fetch_cot.start()

    step_rows = 32

    def norm(i, _):
        part_rows = aligned(i, step_rows)
        inputs = x[part_rows, :].astype(F32)
        center = inputs - jnp.mean(inputs, axis=-1, keepdims=True)
        inverse = lax.rsqrt(jnp.mean(center * center, axis=-1, keepdims=True) + EPSILON)
        where = pl.ds(pl.multiple_of(z * rows + i * step_rows, step_rows), step_rows)
        hid[where, :] = (center * inverse * gain[...] + beta[...]).astype(BF16)
        return 0

    lax.fori_loop(0, rows // step_rows, norm, 0)
    h_chain.start()
    vec[...] = jnp.zeros_like(vec)

    row_segs = seg_row[...].astype(F32)
    places = lax.broadcasted_iota(jnp.int32, (1, length), 1).astype(F32)
    firsts = [
        jnp.min(jnp.where(row_segs == float(value), places, float(length)), axis=1, keepdims=True)
        for value in range(4)
    ]
    for c in range(length // LANES):
        here = slice(c * LANES, (c + 1) * LANES)
        seg = jnp.broadcast_to(row_segs[:, here], (LANES, LANES)).T
        segs[here, :] = seg.astype(BF16)
        start = jnp.zeros((LANES, LANES), F32)
        for value in range(4):
            start = jnp.where(seg == float(value), firsts[value], start)
        place = (lax.broadcasted_iota(jnp.int32, (LANES, LANES), 0) + c * LANES).astype(F32)
        angle = (place - start) * frequency[...]
        lane = lax.rem(lax.broadcasted_iota(jnp.int32, (LANES, LANES), 1), HEAD_DIM)
        sine = jnp.where(lane < ROT, jnp.sin(angle), 0.0)
        tab_c[here, :] = jnp.where(lane < ROT, jnp.cos(angle), 1.0)
        tab_s[here, :] = jnp.where(lane < ROT // 2, -sine, sine)
    key_row = jnp.where(row_segs == 0.0, -1.0, row_segs)

    for gw in g_qkv:
        gw.land()
    if count > 2:
        h_chain.pump(1)
    g_f1.land()
    for gw in (g_o, g_f2):
        gw.start()
    for s in range(2, count - 1):
        h_chain.pump(s)
    c_chain.start()
    for gw in g_qkv:
        gw.land_last()
    for gw in g_qkv:
        gw.arrive()

    ht, wt = tile_of(hcols), tile_of(width)

    def turn_copy(slot, j, cols_i):
        return pltpu.make_async_copy(
            stage.at[slot, pl.ds(0, wt), pl.ds(0, rows)], hid_t.at[cols_i, aligned(j, rows)], st_sem.at[slot]
        )

    def project(j):
        rows_j = aligned(j, rows)
        for which in range(3):
            for c in range(hcols // ht):
                at = which * hcols + c * ht
                y = dot_nn(hid[rows_j, :], vqkv[:, at : at + ht]) + bqkv[:, at : at + ht]
                for piece in range(ht // LANES):
                    part_y = y[:, piece * LANES : (piece + 1) * LANES]
                    if which < 2:
                        part_y = part_y * tab_c[rows_j, :] + swapped(part_y) * tab_s[rows_j, :]
                    low = part_y.astype(BF16)
                    if which == 0:
                        low = low * BF16(HEAD_DIM**-0.5)
                    qkv[rows_j, at + piece * LANES : at + (piece + 1) * LANES] = low

        def turn(i, _):
            cols_i, slot = aligned(i, wt), lax.rem(i, 2)

            @pl.when(i >= 2)
            def _():
                turn_copy(slot, j, cols_i).wait()

            stage[slot, 0:wt, 0:rows] = hid[rows_j, cols_i].T
            turn_copy(slot, j, cols_i).start()
            return 0

        n_turn = width // wt
        lax.fori_loop(0, n_turn, turn, 0)
        for i in range(max(n_turn - 2, 0), n_turn):
            turn_copy(i % 2, j, pl.ds(0, wt)).wait()

    h_chain.by_distance(0, 2 * count - 3, project)
    g_o.land()
    h_chain.by_distance(2 * count - 3, 2 * count - 1, project)
    g_f2.land()
    if count > 2:
        c_chain.pump(1)

    qb = tile_of(length, QBLOCK)
    pairs = hcols // LANES

    def attend(pair, _):
        cols = aligned(pair, LANES)
        k_cols, v_cols = aligned(pairs + pair, LANES), aligned(2 * pairs + pair, LANES)
        lane = lax.broadcasted_iota(jnp.int32, (1, LANES), 1)
        for b in range(length // qb):
            here = slice(b * qb, (b + 1) * qb)
            before = b * qb
            q2 = qkv[here, cols]
            seg_q = segs[here, 0:1].astype(F32)
            ki = lax.broadcasted_iota(jnp.int32, (qb, qb), 1)
            qi = lax.broadcasted_iota(jnp.int32, (qb, qb), 0)
            seen_here = jnp.logical_or(jnp.logical_and(seg_q == key_row[:, here], ki <= qi), ki == qi)
            out = jnp.zeros((qb, LANES), F32)
            stat = jnp.zeros((qb, LANES), F32)
            for h in range(2):
                mine = (lane // HEAD_DIM) == h
                qh = jnp.where(mine, q2, BF16(0))
                s_here = jnp.where(seen_here, dot_nt(qh, qkv[here, k_cols]), NEGATIVE)
                top = jnp.max(s_here, axis=-1, keepdims=True)
                if before:
                    s_before = jnp.where(
                        seg_q == key_row[:, :before], dot_nt(qh, qkv[:before, k_cols]), NEGATIVE
                    )
                    top = jnp.maximum(top, jnp.max(s_before, axis=-1, keepdims=True))
                e_here = jnp.exp(s_here - top)
                total = jnp.sum(e_here, axis=-1, keepdims=True)
                if before:
                    e_before = jnp.exp(s_before - top)
                    total = total + jnp.sum(e_before, axis=-1, keepdims=True)
                share = 1.0 / total
                o = dot_nn((e_here * share).astype(BF16), jnp.where(mine, qkv[here, v_cols], BF16(0)))
                if before:
                    o = o + dot_nn(
                        (e_before * share).astype(BF16), jnp.where(mine, qkv[:before, v_cols], BF16(0))
                    )
                out = out + o
                stat = jnp.where(mine, top + jnp.log(total), stat)
            att[here, cols] = out.astype(BF16)
            att_t[cols, here] = out.T.astype(BF16)
            turned = stat.T
            lse[pl.ds(2 * pair, 1), here] = turned[0:1, :]
            lse[pl.ds(2 * pair + 1, 1), here] = turned[HEAD_DIM : HEAD_DIM + 1, :]
        return 0

    half_pairs = pairs // 2
    lax.fori_loop(0, half_pairs, attend, 0)
    for s in range(2, count - 1):
        c_chain.pump(s)
    lax.fori_loop(half_pairs, pairs - 1, attend, 0)
    g_f1.land_last()
    lax.fori_loop(pairs - 1, pairs, attend, 0)
    g_f1.arrive()

    mt, ft = tile_of(length), tile_of(units)
    per_row = units // ft
    n_tiles = (length // mt) * per_row

    def staged(slot, rows_i, cols_i):
        return pltpu.make_async_copy(stage.at[slot, pl.ds(0, ft), :], act_t.at[cols_i, rows_i], st_sem.at[slot])

    def unit(i, _):
        rows_i, cols_i = aligned(lax.div(i, per_row), mt), aligned(lax.rem(i, per_row), ft)
        slot = lax.rem(i, 2)

        @pl.when(i >= 2)
        def _():
            staged(slot, rows_i, cols_i).wait()

        y = dot_nn(hid[rows_i, :], vf1[:, cols_i]) + bf1[:, cols_i]
        square = y * y
        t = jnp.tanh(GELU_C * (y + GELU_A * (y * square)))
        half = 0.5 * (1.0 + t)
        low = (y * half).astype(BF16)
        act[rows_i, cols_i] = low
        stage[slot, 0:ft, :] = low.T
        dg[rows_i, cols_i] = (
            half + 0.5 * y * (1.0 - t * t) * (GELU_C * (1.0 + 3.0 * GELU_A * square))
        ).astype(BF16)
        staged(slot, rows_i, cols_i).start()
        return 0

    half_tiles = n_tiles // 2
    lax.fori_loop(0, half_tiles, unit, 0)
    for gw in (g_o, g_f2):
        gw.land_last()
    lax.fori_loop(half_tiles, n_tiles, unit, 0)
    for i in range(max(n_tiles - 2, 0), n_tiles):
        staged(i % 2, pl.ds(0, mt), pl.ds(0, ft)).wait()
    for gw in (g_o, g_f2):
        gw.arrive()

    h_chain.finish()

    def output(d):
        here = pl.ds(d * rows, rows)

        def body(i, _):
            cols_i = aligned(i, wt)
            part[here, cols_i] = (
                dot_nn(act[here, :], vf2[:, cols_i]) + dot_nn(att[here, :], vo[:, cols_i])
            ).astype(BF16)
            return 0

        lax.fori_loop(0, width // wt, body, 0)

    dests = list(dict.fromkeys(d for both in zip(range(last, -1, -1), range(count)) for d in both))
    for d in dests:
        output(d)
        if d > 0:
            fold_out.first(True, last - d, rows_of(part, d))
        if d < last:
            fold_out.first(False, d, rows_of(part, d))
    fetch_cot.wait()


    def unit_back(j):
        rows_j = aligned(j, rows)
        def body(i, _):
            cols_i = aligned(i, ft)
            low = (dot_nt(g[rows_j, :], vf2[cols_i, :]) * dg[rows_j, cols_i].astype(F32)).astype(BF16)
            dg[rows_j, cols_i] = low
            to = pl.ds(pl.multiple_of(at_f1 + i * ft, LANES), ft)
            vec[:, to] += jnp.sum(low.astype(F32), axis=0, keepdims=True)
            return 0

        lax.fori_loop(0, per_row, body, 0)
        att[rows_j, :] = dot_nt(g[rows_j, :], vo[...]).astype(BF16)
        vec[:, at_ob:at_gain] += jnp.sum(g[rows_j, :].astype(F32), axis=0, keepdims=True)

    c_chain.by_distance(0, 2 * count - 1, unit_back)
    g_o.finish()
    g_f2.finish()
    c_chain.finish()
    load_act = pltpu.make_async_copy(act_t, act_v, act_sem)
    load_act.start()
    hand_over(pair_free)
    own_part = lambda up, d: rows_of(part, d)
    load_act.wait()
    if count > 2:
        fold_out.pump(1, own_part, rows)
    sc_f2.run()
    sc_o.run()
    for k in range(2, count - 1):
        fold_out.pump(k, own_part, rows)


    def key_of(lo, hi):
        seg = segs[lo:hi, 0:1].astype(F32)
        return jnp.where(seg == 0.0, -1.0, seg)

    def turn_back(y, at):
        return y * tab_c[at, :] - swapped(y) * tab_s[at, :]

    def attend_back(pair, _):
        q_cols = aligned(pair, LANES)
        k_cols, v_cols = aligned(pairs + pair, LANES), aligned(2 * pairs + pair, LANES)
        lane = lax.broadcasted_iota(jnp.int32, (1, LANES), 1)
        dk_acc[...] = jnp.zeros_like(dk_acc)
        dv_acc[...] = jnp.zeros_like(dv_acc)
        k_t[...] = qkv[:, k_cols].T
        for b in range(length // qb):
            here, reach = slice(b * qb, (b + 1) * qb), (b + 1) * qb
            before = b * qb
            q2, g2 = qkv[here, q_cols], att[here, q_cols]
            ki = lax.broadcasted_iota(jnp.int32, (qb, qb), 0)
            qi = lax.broadcasted_iota(jnp.int32, (qb, qb), 1)
            seen_here = jnp.logical_or(
                jnp.logical_and(key_of(before, reach) == row_segs[:, here], ki <= qi), ki == qi
            )
            dq_t = []
            for h in range(2):
                mine = (lane // HEAD_DIM) == h
                qh, gh = jnp.where(mine, q2, BF16(0)), jnp.where(mine, g2, BF16(0))
                stat = lse[pl.ds(2 * pair + h, 1), here]
                spans = ([(0, before)] if before else []) + [(before, reach)]
                probs, grads = [], []
                delta = jnp.zeros((1, qb), F32)
                for lo, hi in spans:
                    seen = seen_here if lo == before else key_of(lo, hi) == row_segs[:, here]
                    p = jnp.exp(jnp.where(seen, dot_nt(qkv[lo:hi, k_cols], qh), NEGATIVE) - stat)
                    pg = dot_nt(qkv[lo:hi, v_cols], gh)
                    delta = delta + jnp.sum(p * pg, axis=0, keepdims=True)
                    probs.append(p)
                    grads.append(pg)
                acc = jnp.zeros((HEAD_DIM, qb), F32)
                for (lo, hi), p, pg in zip(spans, probs, grads):
                    sg = (p * (pg - delta)).astype(BF16)
                    dv_acc[lo:hi, :] += dot_nn(p.astype(BF16), gh)
                    dk_acc[lo:hi, :] += dot_nn(sg, qh)
                    acc = acc + dot_nn(k_t[h * HEAD_DIM : (h + 1) * HEAD_DIM, lo:hi], sg)
                dq_t.append(acc)
            dq = jnp.concatenate(dq_t, axis=0).T * HEAD_DIM**-0.5
            qkv[here, q_cols] = turn_back(dq, here).astype(BF16)
        for b in range(length // qb):
            here = slice(b * qb, (b + 1) * qb)
            qkv[here, k_cols] = turn_back(dk_acc[here, :], here).astype(BF16)
            qkv[here, v_cols] = dv_acc[here, :].astype(BF16)
        for cols in (q_cols, k_cols, v_cols):
            vec[:, cols] = jnp.sum(qkv[:, cols].astype(F32), axis=0, keepdims=True)
        return 0

    lax.fori_loop(0, pairs, attend_back, 0)

    def hidden_back(d):
        here = pl.ds(d * rows, rows)

        def body(i, _):
            cols_i = aligned(i, wt)
            g[here, cols_i] = (
                dot_nt(dg[here, :], vf1[cols_i, :]) + dot_nt(qkv[here, :], vqkv[cols_i, :])
            ).astype(BF16)
            return 0

        lax.fori_loop(0, width // wt, body, 0)

    def set_out(d):
        if d > 0:
            fold_hid.first(True, last - d, rows_of(g, d))
        if d < last:
            fold_hid.first(False, d, rows_of(g, d))

    for d in dests[:2]:
        hidden_back(d)

    fold_out.arrive()
    def finish_output(i, _):
        part = aligned(i, 32)
        at = pl.ds(pl.multiple_of(z * rows + i * 32, 32), 32)
        y = fold_out.total(hid[at, :].astype(F32), part)
        hid[at, :] = (x[part, :].astype(F32) + y + out_bias[...]).astype(BF16)
        return 0

    lax.fori_loop(0, rows // 32, finish_output, 0)
    save_out = pltpu.make_async_copy(hid.at[aligned(z, rows), :], block_out, out_sem)
    save_out.start()
    fold_out.finish()

    @pl.when(z > 0)
    def _():
        pl.semaphore_signal(free_up, inc=1, device_id=(dp, z - 1), device_id_type=MESH)

    @pl.when(z < last)
    def _():
        pl.semaphore_signal(free_dn, inc=1, device_id=(dp, z + 1), device_id_type=MESH)

    @pl.when(z < last)
    def _():
        pl.semaphore_wait(free_up, 1)

    @pl.when(z > 0)
    def _():
        pl.semaphore_wait(free_dn, 1)

    for d in dests[:2]:
        set_out(d)
    sc_f2.relay()
    sc_o.relay()
    for d in dests[2:]:
        hidden_back(d)
        set_out(d)
    own_grad = lambda up, d: rows_of(g, d)

    def pump_hidden(lo, hi):
        for k in range(lo, hi):
            fold_hid.pump(k, own_grad, rows)

    pump_hidden(1, min(2, count - 1))
    run_rows(sc_f1)
    save_out.wait()
    hand_over(hid_free)
    run_rows(sc_qkv, lambda: pump_hidden(2, count - 1))
    sc_f1.relay()
    sc_f2.sent()
    load_cot = pltpu.make_async_copy(cot, vf2.at[0:rows, 0:width], cot_sem)
    load_cot.start()
    sc_qkv.relay()
    fold_hid.arrive()
    load_cot.wait()

    step_rows = 16

    def ig_copy(i, slot):
        return pltpu.make_async_copy(ig_stage.at[slot], input_grad.at[aligned(i, step_rows), :], ig_sem.at[slot])

    def norm_back(i, _):
        part = aligned(i, step_rows)
        slot = lax.rem(i, 2)
        inputs = x[part, :].astype(F32)
        center = inputs - jnp.mean(inputs, axis=-1, keepdims=True)
        inverse = lax.rsqrt(jnp.mean(center * center, axis=-1, keepdims=True) + EPSILON)
        normed = center * inverse
        own = g[pl.ds(pl.multiple_of(z * rows + i * step_rows, step_rows), step_rows), :].astype(F32)
        y = fold_hid.total(own, part)
        vec[:, at_gain : at_gain + width] += jnp.sum(y * normed, axis=0, keepdims=True)
        vec[:, at_beta : at_beta + width] += jnp.sum(y, axis=0, keepdims=True)
        scaled = y * gain[...]
        result = vf2[part, :].astype(F32) + inverse * (
            scaled
            - jnp.mean(scaled, axis=-1, keepdims=True)
            - normed * jnp.mean(scaled * normed, axis=-1, keepdims=True)
        )

        @pl.when(i >= 2)
        def _():
            ig_copy(i, slot).wait()

        ig_stage[slot] = result
        ig_copy(i, slot).start()
        return 0

    steps = rows // step_rows
    lax.fori_loop(0, steps, norm_back, 0)

    to_pair = pltpu.make_async_remote_copy(
        src_ref=vec, dst_ref=vec_pair, send_sem=v_ps, recv_sem=v_pr,
        device_id=(chip * 2 + 1 - core, z), device_id_type=MESH,
    )
    to_pair.start()
    for i in range(max(steps - 2, 0), steps):
        ig_copy(i, i % 2).wait()
    to_pair.wait()
    vec_chip[chip] = vec[...] + vec_pair[...]

    def chip_copy(r, slot):
        return pltpu.make_async_remote_copy(
            src_ref=vec_chip.at[chip], dst_ref=vec_chip.at[slot], send_sem=v_cs.at[r - 1], recv_sem=v_cr.at[r - 1],
            device_id=(flip(chip, r) * 2 + core, z), device_id_type=MESH,
        )

    for r in range(1, chips):
        chip_copy(r, chip).start()
    for r in range(1, chips):
        chip_copy(r, flip(chip, r)).wait_recv()
    total = vec_chip[0]
    for c in range(1, chips):
        total = total + vec_chip[c]
    vec_out[:, 0:at_gain] = total[:, 0:at_gain]
    vec_z[z] = total[:, at_gain:]

    def z_copy(shift, slot):
        return pltpu.make_async_remote_copy(
            src_ref=vec_z.at[z], dst_ref=vec_z.at[slot], send_sem=v_zs.at[shift - 1], recv_sem=v_zr.at[shift - 1],
            device_id=(dp, lax.rem(z + shift, count)), device_id_type=MESH,
        )

    for shift in range(1, count):
        z_copy(shift, z).start()
    for shift in range(1, count):
        z_copy(shift, lax.rem(z + count - shift, count)).wait_recv()
    total = vec_z[0]
    for n in range(1, count):
        total = total + vec_z[n]
    vec_out[:, at_gain:] = total
    for r in range(1, chips):
        chip_copy(r, chip).wait_send()
    for shift in range(1, count):
        z_copy(shift, z).wait_send()
    fold_hid.finish()
    for s in (sc_f1, sc_o, sc_qkv):
        s.sent()
    for s in (sc_f2, sc_f1, sc_o, sc_qkv):
        s.finish()
    for gw in (*g_qkv, g_f1):
        gw.finish()


def run_block(ndp, count, x, gain, beta, bqkv, bf1, out_bias, seg_row, frequency, wq, wk, wv, wf1, wo, wf2, cot):
    chips = ndp // 2
    rows, width = x.shape
    length = rows * count
    hcols, units = wo.shape[0], wf2.shape[0]
    part_w = width // ndp
    total = 3 * hcols + units + 3 * width
    lands = 2 if chips == 4 else chips - 1
    heads = hcols // HEAD_DIM
    mt, ft, wt = tile_of(length), tile_of(units), tile_of(width)
    anywhere = pl.BlockSpec(memory_space=pl.ANY)
    vmem = pl.BlockSpec(memory_space=pltpu.VMEM)
    low = lambda *shape: jax.ShapeDtypeStruct(shape, BF16)
    wide = lambda *shape: jax.ShapeDtypeStruct(shape, F32)
    outs = [
        low(rows, width), wide(rows, width), wide(1, total),
        wide(part_w, 3 * hcols), wide(part_w, units), wide(hcols, part_w), wide(units, part_w),
        low(lands, part_w, 3 * hcols), low(lands, part_w, units), low(lands, hcols, part_w), low(lands, units, part_w),
        low(width, length), low(units, length),
        low(2, part_w // 2, 3 * hcols), low(2, part_w // 2, units), low(2, hcols // 2, part_w), low(2, units // 2, part_w),
    ]
    v = lambda *shape: pltpu.VMEM(shape, BF16)
    w = lambda *shape: pltpu.VMEM(shape, F32)
    steps = max(count - 1, 1)
    dma = lambda *shape: pltpu.SemaphoreType.DMA(shape)
    one, plain = pltpu.SemaphoreType.DMA, pltpu.SemaphoreType.REGULAR
    row_tile = max(piece_of(units), piece_of(3 * hcols))
    col_tile = max(piece_of(units), piece_of(hcols))
    scratch = [
        v(length, width), v(width, 3 * hcols), v(width, units), v(units, width), v(hcols, width),
        v(length, 3 * hcols), v(length, hcols), v(hcols, length), w(heads, length), v(length, units), v(length, units),
        v(length, width), v(2, max(ft, wt, part_w), max(mt, part_w)), w(length, LANES), w(length, LANES), v(length, LANES),
        w(length, LANES), w(length, LANES), v(LANES, length), v(steps, rows, width), v(steps, rows, width),
        w(part_w, row_tile), w(col_tile, part_w),
        w(2, 16, width), w(1, total), w(1, total), w(chips, 1, total), w(count, 1, 2 * width),
        dma(6, chips - 1), dma(6, chips - 1), dma(6, 2), dma(6, 2), dma(6, chips), dma(6, chips), dma(6),
        *[dma(steps) for _ in range(8)], one, dma(2),
        one, dma(2), one, dma(2), dma(2), dma(2),
        dma(4, chips), dma(4, max(chips - 1, 4)), dma(4, max(chips - 1, 4)), one, one, dma(4, 2), dma(4, 2), dma(2),
        *[dma(steps, 2) for _ in range(8)], plain, plain, plain, plain,
        one, one, dma(chips - 1), dma(chips - 1), dma(steps), dma(steps),
    ]
    return pl.pallas_call(
        functools.partial(block_kernel, chips, count),
        out_shape=outs,
        in_specs=[vmem] * 8 + [anywhere] * 7,
        out_specs=[anywhere, anywhere, vmem] + [anywhere] * 14,
        scratch_shapes=scratch,
        compiler_params=pltpu.CompilerParams(
            collective_id=0, has_side_effects=True, vmem_limit_bytes=VMEM_LIMIT
        ),
        name="block_step",
    )(x, gain, beta, bqkv, bf1, out_bias, seg_row, frequency, wq, wk, wv, wf1, wo, wf2, cot)[:11]


def on_device(
    ndp, count,
    block_input, segment_ids, out_cotangent, norm_gain, norm_bias, query_weight, key_weight, value_weight,
    query_bias, key_bias, value_bias, out_weight, fc1_weight, fc1_bias, fc2_weight, output_bias,
):
    x = block_input[0]
    cot = out_cotangent[0]
    width = x.shape[1]
    half_rot = ROT // 2
    frequency = 10000.0 ** (-2.0 * (jnp.arange(LANES, dtype=jnp.int32) % half_rot).astype(F32) / ROT)
    bqkv = jnp.concatenate([query_bias, key_bias, value_bias])[None, :]
    gain, seg_row = norm_gain[None, :], segment_ids
    (block_output, input_grad, vec, own_qkv, own_f1, own_o, own_f2, land_qkv, land_f1, land_o, land_f2) = run_block(
        ndp, count, x, gain, norm_bias[None, :], bqkv, fc1_bias[None, :], output_bias[None, :], seg_row,
        frequency[None, :], query_weight, key_weight, value_weight, fc1_weight, out_weight, fc2_weight, cot,
    )
    hcols, units = out_weight.shape[0], fc2_weight.shape[0]

    def summed(own, landed):
        for n in range(landed.shape[0]):
            own = own + landed[n].astype(F32)
        return own

    def third(i):
        cols = slice(i * hcols, (i + 1) * hcols)
        return summed(own_qkv[:, cols], land_qkv[:, :, cols])

    sizes = (hcols, hcols, hcols, units, width, width, width)
    pieces, at = [], 0
    for size in sizes:
        pieces.append(vec[0, at : at + size])
        at += size
    qb, kb, vb, f1b, ob, gain_grad, beta_grad = pieces
    return (
        block_output[None], input_grad[None], gain_grad, beta_grad,
        third(0), third(1), third(2), qb, kb, vb,
        summed(own_o, land_o), summed(own_f1, land_f1), f1b, summed(own_f2, land_f2), ob,
    )


def solution(mesh):
    tokens, vector, split = P("dp", "branch", None), P(), P("branch")
    rows_first, cols_first = P("dp", "branch"), P("branch", "dp")
    in_specs = (
        tokens, P("dp", None), tokens, vector, vector, rows_first, rows_first, rows_first,
        split, split, split, cols_first, rows_first, split, cols_first, vector,
    )
    out_specs = (
        tokens, tokens, vector, vector, rows_first, rows_first, rows_first, split, split, split,
        cols_first, rows_first, split, cols_first, vector,
    )
    return jax.shard_map(
        functools.partial(on_device, mesh.shape["dp"], mesh.shape["branch"]),
        mesh=mesh, in_specs=in_specs, out_specs=out_specs, check_vma=False,
    )
```
